128 devices in a mesh: gx: 16 (over x, z), gy: 8 (over y, core).
Axes of the slice: x: 4, y: 4, z: 4, core: 2. Of those that a mesh axis runs over, the one named last changes fastest.
Arguments:
- state: float32 [9, 56, 32768], P(None, None, ('gx', 'gy')), may hold values from -6 to 6
- star: float32 [3, 9, 9, 32768], P(None, None, None, ('gx', 'gy')), may hold values from -1.5 to 1.5
- deriv: float32 [3, 56, 56], replicated, may hold values from -0.75 to 0.75
- trace_ops: float32 [4, 56, 21], replicated, may hold values from -0.75 to 0.75
- lift: float32 [4, 21, 56], replicated, may hold values from -1.25 to 1.25
- face_flux: float32 [4, 9, 9, 32768], P(None, None, None, ('gx', 'gy')), may hold values from -0.3 to 0.3
- orient: int32 [4, 32768], P(None, ('gx', 'gy')), may hold values from 0 to 2
- neighbours: int32 [4, 32768], P(None, ('gx', 'gy')), may hold values from 0 to 1536, as said below
- send_faces: int32 [16, 8, 4, 128], P('gx', 'gy'), may hold values from 0 to 1023, as said below
- sea_faces: int32 [16384], P(('gx', 'gy')), may hold values from 0 to 1023
- sea_owner: int32 [16384, 1], P(('gx', 'gy')), may hold values from 0 to 127; in each aligned block of 128 rows (0 to 127, 128 to 255, ...) at most 2 rows name the same one
- sea_blocks: int32 [16384], P(('gx', 'gy')), may hold values from 0 to 255
- sea_weights: float32 [21, 16384, 256], P(None, ('gx', 'gy')), may hold values from -0.6 to 0.6
- depth: float32 [4096, 2048], P('gx', 'gy'), may hold values from 1 to 3
- wet: int32 [4096, 2048], P('gx', 'gy'), may hold values 0 or 1
- sea_state: float32 [3, 4096, 2048], P(None, 'gx', 'gy'), may hold values from -0.6 to 0.6
Outputs:
- elastic: float32 [9, 56, 32768], P(None, None, ('gx', 'gy'))
- ocean: float32 [3, 4096, 2048], P(None, 'gx', 'gy')
The draws below stay inside these ranges and needn't reach their ends.
Inputs may be any that keep to these rules, and one draw needn't show every extreme that they name: `neighbours`: A code below 1024 names a face of the same device, paired both ways; 1024 + k * 128 + s names the face in slot s of the back-pointing list of the grid neighbour in direction k, which lists this face in its slot s; 1536 marks a face at the edge of the device grid. `send_faces`: local face codes; each face of a device stands in at most one of its lists, once. `sea_faces`: local face codes. `sea_owner`: the flat index of a device, gx index times the gy axis's length plus gy index; among the 128 rows of one device at most 2 name the same owner, and some owner is named 2 times.
All inputs are finite; a program needn't handle non-finite values. No bound on the sum of `wet` on one device may be relied on, other than what follows from the above.
Results may differ from the reference program's by a relative error of at most 0.0001.
Values sent between devices are 32-bit elements; how exact they have to be, the bound alone decides.
A program may use at most 128 MiB of HBM per device.

```python
import math
import jax
import jax.numpy as jnp
import numpy as np
from jax import lax

VARS = 9
ORDER = 6
BASIS = 56
FACE_NODES = 21
EL_DEV = 256
SLOTS = 128
STEPS = 2
SEA_DEV = 128
CAP = 2
BS = 16
TX = 256
TY = 256
TAPS = 65
HALF = 32
CELLS = 256
BLOCKS = 256
ELEMENTS = 32768
SEA_ALL = 16384
RX = 4096
RY = 2048
N_GX = 16
N_GY = 8
DEVICES = 128


def link_table(key):
    base = jax.random.fold_in(key, 11)
    keys = jax.random.split(base, N_GX * N_GY)
    return jax.vmap(lambda single: jax.random.permutation(single, 4 * EL_DEV))(keys).astype(jnp.int32)


def draw_send_faces(key, part):
    perms = link_table(key)
    return perms[:, :4 * SLOTS].reshape(N_GX, N_GY, 4, SLOTS).astype(jnp.int32)


def draw_neighbours(key, part):
    perms = link_table(key)
    devs = N_GX * N_GY
    places = jnp.arange(4 * EL_DEV, dtype=jnp.int32)
    device_ids = jnp.arange(devs, dtype=jnp.int32)
    row_x = device_ids // N_GY
    row_y = device_ids % N_GY
    exists = jnp.stack([row_x > 0, row_x < N_GX - 1, row_y > 0, row_y < N_GY - 1], axis=1)
    direction = jnp.minimum(places // SLOTS, 3)
    present = exists[:, direction]
    cross_code = jnp.where(present, 4 * EL_DEV + places[None, :], 4 * EL_DEV + 4 * SLOTS)
    rest = jnp.maximum(places - 4 * SLOTS, 0)
    mate = jnp.minimum(4 * SLOTS + jnp.bitwise_xor(rest, 1), 4 * EL_DEV - 1)
    local_code = perms[:, mate]
    values = jnp.where((places < 4 * SLOTS)[None, :], cross_code, local_code).astype(jnp.int32)
    table = jnp.zeros((devs, 4 * EL_DEV), jnp.int32)
    table = table.at[device_ids[:, None], perms].set(values)
    return table.reshape(devs, 4, EL_DEV).transpose(1, 0, 2).reshape(4, devs * EL_DEV)


def touch_ends(values, key, least, largest):
    index_at = [jax.random.randint(jax.random.fold_in(key, axis), (), 0, length) for axis, length in enumerate(values.shape)]
    main_axis = values.shape.index(max(values.shape))
    next_to = index_at[:main_axis] + [(index_at[main_axis] + 1) % values.shape[main_axis]] + index_at[main_axis + 1:]
    return values.at[tuple(index_at)].set(least).at[tuple(next_to)].set(largest)


def block_scale(rng, extent, shards, least, top_value):
    def one(dim, shards_of):
        heights = jax.random.uniform(jax.random.fold_in(jax.random.fold_in(rng, 6), dim), (shards_of,), jnp.float32, least / len(shards), top_value / len(shards))
        return jnp.repeat(jnp.exp(heights), extent[dim] // shards_of).reshape((-1,) + (1,) * (len(extent) - dim - 1))

    gain = one(*shards[0])
    for cut in shards[1:]:
        gain = gain * one(*cut)
    return gain


def assign_block(own_key, own, number, rows, count, top, most, slope):
    sequence = jax.random.permutation(own_key, count)
    packed, usual = portions_of(count, rows * top, most, slope, True), portions_of(count, rows * top, most, slope, False)
    places = jnp.arange(count)

    def named(sizes, turn):
        used = int((sizes > 0).sum())
        fixed = max(1, used // 4)
        passed = fixed + (places - fixed + turn * (used - fixed)) % max(1, count - fixed)
        return jnp.zeros((count,), jnp.int32).at[sequence[jnp.where(places < fixed, places, passed)]].set(jnp.asarray(sizes, jnp.int32))

    sizes = jnp.where(number % 4 == 0, named(packed, number // 4), named(usual, number - number // 4 - 1))
    mixed = jax.random.permutation(jax.random.fold_in(own, 3), count)
    source_of, sink = mixed[0:count // 2 * 2:2], mixed[1:count // 2 * 2:2]
    margin = jnp.minimum(sizes[source_of] - 1, most - sizes[sink]) // 2
    margin = jnp.where((source_of == sequence[0]) | (sink == sequence[0]) | (sizes[sink] == 0), 0, jnp.maximum(margin, 0))
    passed = jax.random.randint(jax.random.fold_in(own, 4), (count // 2,), 0, 1 << 20) % (margin + 1)
    sizes = sizes.at[source_of].add(-passed).at[sink].add(passed)
    members = jnp.searchsorted(jnp.cumsum(sizes), jnp.arange(rows * top), side="right").astype(jnp.int32)
    table = members.reshape(top, rows).T
    table = table[jax.random.permutation(jax.random.fold_in(own, 1), rows)]
    turn = jax.random.randint(jax.random.fold_in(own, 2), (rows, 1), 0, top)
    return jnp.take_along_axis(table, (jnp.arange(top)[None, :] + turn) % top, axis=1)


def portions_of(count, total, most, lean, full):
    portions = [(1 << 20) // math.isqrt(rank ** lean) + 1 for rank in range(1, count + 1)]
    largest = most if full else min(most, max(-(-total // count), total * portions[0] // sum(portions)))
    least = 1 if total - largest >= count - 1 else 0
    counts, spare = [largest] + [least] * (count - 1), total - largest - least * (count - 1)
    while spare > 0:
        free = [i for i in range(1, count) if counts[i] < largest] or [i for i in range(1, count) if counts[i] < most]
        whole, left = sum([portions[i] for i in free]), spare
        for i in free:
            addition = min(most - counts[i], max(1, left * portions[i] // whole), spare)
            counts[i] = counts[i] + addition
            spare = spare - addition
    return np.array(counts)


def centred(rng, extent, scale, most, cuts=(), kind=jnp.bfloat16):
    values = jax.random.normal(rng, extent, jnp.float32) * scale
    if len(cuts) > 0:
        values = block_scale(rng, extent, cuts, -0.22, 0.18) * values
    return jnp.clip(values, min=-most, max=most).astype(kind)


def setup_inputs(seed: int = 0) -> dict:
    seeds = jax.random.split(jax.random.key(seed), 17)
    state = centred(seeds[0], (VARS, BASIS, ELEMENTS), 1.0, 6.0, ((2, 128),), jnp.float32)
    star = centred(seeds[1], (3, VARS, VARS, ELEMENTS), 0.25, 1.5, ((3, 128),), jnp.float32)
    deriv = centred(seeds[2], (3, BASIS, BASIS), BASIS ** -0.5, 0.75, (), jnp.float32)
    trace_ops = centred(seeds[3], (4, BASIS, FACE_NODES), BASIS ** -0.5, 0.75, (), jnp.float32)
    lift = centred(seeds[4], (4, FACE_NODES, BASIS), FACE_NODES ** -0.5, 1.25, (), jnp.float32)
    face_flux = centred(seeds[5], (4, VARS, VARS, ELEMENTS), 0.05, 0.3, ((3, 128),), jnp.float32)
    orient = touch_ends(jax.random.randint(seeds[6], (4, ELEMENTS), 0, 3), jax.random.fold_in(seeds[6], 1), 0, 2).astype(jnp.int32)
    neighbours = draw_neighbours(jax.random.fold_in(seeds[16], 71), 0)
    send_faces = draw_send_faces(jax.random.fold_in(seeds[16], 71), 0)
    sea_faces = touch_ends(jax.random.randint(seeds[9], (SEA_ALL,), 0, 4 * EL_DEV), jax.random.fold_in(seeds[9], 1), 0, (4 * EL_DEV) - 1).astype(jnp.int32)
    sea_owner_keys = jax.random.split(jax.random.fold_in(seeds[10], 1), SEA_ALL // SEA_DEV)
    sea_owner_turns = jax.random.permutation(jax.random.fold_in(seeds[10], 3), SEA_ALL // SEA_DEV)
    sea_owner = jax.vmap(lambda own, number: assign_block(jax.random.fold_in(seeds[10], 2), own, number, SEA_DEV, DEVICES, 1, CAP, 2))(sea_owner_keys, sea_owner_turns).reshape((SEA_ALL, 1))
    sea_blocks = touch_ends(jax.random.randint(seeds[11], (SEA_ALL,), 0, BLOCKS), jax.random.fold_in(seeds[11], 1), 0, BLOCKS - 1).astype(jnp.int32)
    sea_weights = centred(seeds[12], (FACE_NODES, SEA_ALL, CELLS), 0.1, 0.6, ((1, 128),), jnp.float32)
    depth = jnp.clip(1.0 + 2.0 * jax.random.uniform(seeds[13], (RX, RY), jnp.float32) ** block_scale(seeds[13], (RX, RY), ((0, 16), (1, 8)), -0.2, 0.2), 1.0, 3.0)
    wet = touch_ends((jax.random.randint(seeds[14], (RX, RY), 0, 4) < 3).astype(jnp.int32), jax.random.fold_in(seeds[14], 1), 0, 1)
    sea_state = centred(seeds[15], (3, RX, RY), 0.1, 0.6, ((1, 16), (2, 8)), jnp.float32)
    return dict(state=state, star=star, deriv=deriv, trace_ops=trace_ops, lift=lift, face_flux=face_flux, orient=orient, neighbours=neighbours, send_faces=send_faces, sea_faces=sea_faces, sea_owner=sea_owner, sea_blocks=sea_blocks, sea_weights=sea_weights, depth=depth, wet=wet, sea_state=sea_state)


spread_cells = 8.0
gravity = 1.0
courant = 0.25
best = lax.Precision.HIGHEST


def node_turns():
    upper = ORDER - 1
    nodes = [(i, j) for i in range(upper + 1) for j in range(upper + 1 - i)]
    once = [nodes.index((pair[1], upper - pair[0] - pair[1])) for pair in nodes]
    twice = [once[once[number]] for number in range(len(nodes))]
    return np.array(once), np.array(twice)


def filter_taps():
    offsets = jnp.arange(-HALF, HALF + 1).astype(jnp.float32)
    scaled = math.pi * offsets / (2.0 * spread_cells)
    raw = 2.0 / (jnp.exp(scaled) + jnp.exp(-scaled))
    return raw / jnp.sum(raw)


def derive(field, star, deriv):
    total = jnp.zeros(field.shape, jnp.float32)
    for direction in range(3):
        moved = jnp.einsum("vbe,bc->vce", field, deriv[direction], precision=best)
        total = total + jnp.einsum("uve,vce->uce", star[direction], moved, precision=best)
    return total


def predict(field, star, deriv):
    term = field
    integ = field
    for order_k in range(1, ORDER):
        term = -derive(term, star, deriv)
        integ = integ + term / float(math.factorial(order_k + 1))
    return integ


def turn_nodes(partner, orient):
    once, twice = node_turns()
    turned = jnp.where(orient == 1, partner[:, once], partner)
    return jnp.where(orient == 2, partner[:, twice], turned)


def settle(field, integ, own_faces, partner, orient, face_flux, lift, star, deriv):
    jump = own_faces - turn_nodes(partner, orient)
    flux = jnp.einsum("fuve,vnfe->unfe", face_flux, jump, precision=best)
    surface = jnp.einsum("unfe,fnb->ube", flux, lift, precision=best)
    return field - derive(integ, star, deriv) - surface


def advance(fields, wide, wet_field):
    plus_x = wide[:, 2:, 1:-1]
    minus_x = wide[:, :-2, 1:-1]
    plus_y = wide[:, 1:-1, 2:]
    minus_y = wide[:, 1:-1, :-2]
    mean = 0.25 * (plus_x + minus_x + plus_y + minus_y)
    east_speed = fields[1]
    north_speed = fields[2]
    factor = 0.5 * courant
    eta_new = mean[0] - factor * ((plus_x[3] - minus_x[3]) + (plus_y[4] - minus_y[4]))
    east_new = mean[1] - factor * (east_speed * (plus_x[1] - minus_x[1]) + north_speed * (plus_y[1] - minus_y[1]) + gravity * (plus_x[0] - minus_x[0]))
    north_new = mean[2] - factor * (east_speed * (plus_x[2] - minus_x[2]) + north_speed * (plus_y[2] - minus_y[2]) + gravity * (plus_y[0] - minus_y[0]))
    return eta_new * wet_field, east_new * wet_field, north_new * wet_field


def reference(state, star, deriv, trace_ops, lift, face_flux, orient, neighbours, send_faces, sea_faces, sea_owner, sea_blocks, sea_weights, depth, wet, sea_state):
    devs = N_GX * N_GY
    width = VARS * FACE_NODES
    limit = 4 * EL_DEV + 4 * SLOTS
    lists = send_faces.reshape(devs, 4 * SLOTS)
    codes = neighbours.reshape(4, devs, EL_DEV).transpose(1, 0, 2).reshape(devs, 4 * EL_DEV)
    sea_lists = sea_faces.reshape(devs, SEA_DEV)
    field = state
    vertical = []
    for turn in range(STEPS):
        integ = predict(field, star, deriv)
        own_faces = jnp.einsum("vbe,fbn->vnfe", integ, trace_ops, precision=best)
        local = own_faces.reshape(VARS, FACE_NODES, 4, devs, EL_DEV).transpose(3, 0, 1, 2, 4).reshape(devs, width, 4 * EL_DEV)
        sent = jax.vmap(lambda table, picks: table[:, picks])(local, lists).reshape(N_GX, N_GY, width, 4, SLOTS)
        blank_x = jnp.zeros((1, N_GY, width, SLOTS), jnp.float32)
        blank_y = jnp.zeros((N_GX, 1, width, SLOTS), jnp.float32)
        from_low_x = jnp.concatenate([blank_x, sent[:-1, :, :, 1]], 0)
        from_high_x = jnp.concatenate([sent[1:, :, :, 0], blank_x], 0)
        from_low_y = jnp.concatenate([blank_y, sent[:, :-1, :, 3]], 1)
        from_high_y = jnp.concatenate([sent[:, 1:, :, 2], blank_y], 1)
        arrived = jnp.stack([from_low_x, from_high_x, from_low_y, from_high_y], 3).reshape(devs, width, 4 * SLOTS)
        pool = jnp.concatenate([local, arrived], 2)
        picked = jax.vmap(lambda table, picks: table[:, jnp.minimum(picks, limit - 1)])(pool, codes)
        picked = jnp.where(codes[:, None, :] < limit, picked, 0.0)
        partner = picked.reshape(devs, VARS, FACE_NODES, 4, EL_DEV).transpose(1, 2, 3, 0, 4).reshape(VARS, FACE_NODES, 4, ELEMENTS)
        upward = local[:, 2 * FACE_NODES:3 * FACE_NODES, :]
        vertical.append(jax.vmap(lambda table, picks: table[:, picks])(upward, sea_lists))
        field = settle(field, integ, own_faces, partner, orient, face_flux, lift, star, deriv)
    frames = []
    running = jnp.zeros(vertical[0].shape, jnp.float32)
    for piece in vertical:
        running = running + piece
        frames.append(running)
    disp = jnp.stack(frames)
    weights = sea_weights.reshape(FACE_NODES, devs, SEA_DEV, CELLS)
    rows = jnp.einsum("sdnr,ndrc->drsc", disp, weights, precision=best).reshape(SEA_ALL, STEPS * CELLS)
    segment = sea_owner[:, 0] * BLOCKS + sea_blocks
    summed = jax.ops.segment_sum(rows, segment, num_segments=devs * BLOCKS)
    uplift = summed.reshape(N_GX, N_GY, TX // BS, TY // BS, STEPS, BS, BS).transpose(4, 0, 2, 5, 1, 3, 6).reshape(STEPS, RX, RY)
    taps = filter_taps()
    padded = jnp.pad(uplift, ((0, 0), (HALF, HALF), (0, 0)))
    along_x = jnp.zeros(uplift.shape, jnp.float32)
    for offset in range(TAPS):
        along_x = along_x + taps[offset] * padded[:, offset:offset + RX, :]
    padded = jnp.pad(along_x, ((0, 0), (0, 0), (HALF, HALF)))
    filtered = jnp.zeros(uplift.shape, jnp.float32)
    for offset in range(TAPS):
        filtered = filtered + taps[offset] * padded[:, :, offset:offset + RY]
    wet_field = wet.astype(jnp.float32)
    eta, east_speed, north_speed = sea_state[0], sea_state[1], sea_state[2]
    for turn in range(STEPS):
        force = filtered[0] if turn == 0 else filtered[turn] - filtered[turn - 1]
        eta = eta + wet_field * force
        column = depth + eta
        fields = jnp.stack([eta, east_speed, north_speed, column * east_speed, column * north_speed])
        wide = jnp.pad(fields, ((0, 0), (1, 1), (1, 1)))
        eta, east_speed, north_speed = advance(fields, wide, wet_field)
    return field, jnp.stack([eta, east_speed, north_speed])
```

```python
import functools
import math

import jax
import jax.numpy as jnp
import numpy as np
from jax import lax
from jax.experimental import pallas as pl
from jax.experimental.pallas import tpu as pltpu
from jax.sharding import PartitionSpec as P

VARS = 9
ORDER = 6
BASIS = 56
NODES = 21
NX, NY = 16, 8
HALF = 32
NPAD = 24
EXT_X, EXT_Y = 264, 384
bf16, f32, i32 = jnp.bfloat16, jnp.float32, jnp.int32
MESH = pl.DeviceIdType.MESH


def turned_nodes():
    upper = ORDER - 1
    nodes = [(i, j) for i in range(upper + 1) for j in range(upper + 1 - i)]
    once = [nodes.index((p[1], upper - p[0] - p[1])) for p in nodes]
    twice = [once[once[n]] for n in range(len(nodes))]
    rest = list(range(NODES, NPAD))
    return np.array(once + rest), np.array(twice + rest)


def filter_matrices():
    k = np.arange(-HALF, HALF + 1)
    raw = 1.0 / np.cosh(math.pi * k / 16.0)
    taps = raw / raw.sum()

    def tap(offset):
        inside = np.abs(offset) <= HALF
        return np.where(inside, taps[np.clip(offset + HALF, 0, 2 * HALF)], 0.0)

    far = 10**6
    cell_x = np.array([r if r < 258 else (r - EXT_X if r >= 262 else far) for r in range(EXT_X)])
    cell_y = np.array([c if c < 258 else (c - EXT_Y if c >= 382 else far) for c in range(EXT_Y)])
    rows_up = np.concatenate([np.arange(0, 32), np.arange(256, 264)])
    rows_down = np.arange(224, 264)
    xs = np.concatenate([cell_x, cell_x[rows_up] + 256, cell_x[rows_down] - 256, np.full(8, far)])
    lane = np.arange(128)
    up = np.where(lane < 64, lane, 256 + lane)
    down = np.where(lane < 64, 256 + lane, 128 + lane)
    ys = np.concatenate([cell_y, cell_y[up] + 256, cell_y[down] - 256])
    column = np.arange(256)
    x_of = (column % 16) * 16 + column // 16
    wx = tap(xs[:, None] - x_of[None, :]).astype(np.float32)
    wy = tap(ys[None, :] - np.arange(256)[:, None]).astype(np.float32)

    def parts(w):
        high = w.astype(jnp.bfloat16)
        low = (w - high.astype(np.float32)).astype(jnp.bfloat16)
        return high, low

    xh, xl = parts(wx)
    yh, yl = parts(wy)
    return np.concatenate([xh, xl], 0), np.concatenate([yh, yl], 1)


def split(x):
    high = x.astype(bf16)
    low = (x - high.astype(f32)).astype(bf16)
    return high, low


def dot(a, b):
    return jnp.dot(a, b, preferred_element_type=f32)


def iota(shape, dim):
    return lax.broadcasted_iota(i32, shape, dim)


def kernel(
    state, star, deriv, trace, lift, flux9, orient, codes, sends, seaf, owner, blocks, weights,
    depth, wet, sea, wx, wy, turns,
    out_el, out_oc,
    star8, flux8, a_op, t_op, l_op, stack, moved, term, integ, base, own, xs, g_out, p_loc, p_arr,
    part, sbuf, arr, xa, fstack, zed, place, disp_t, rows, pay0, pay1, bx0, bx1, my0, my1, by0, by1,
    sel, upl, cont, halo_x, halo_y, halo_c, force, sw, gh_x, gh_y, gh_c, ext,
    orient8, sem_f, sem_x, sem_y, sem_h, sem_g,
):
    gx, gy = lax.axis_index("gx"), lax.axis_index("gy")

    def at(dx, dy):
        return (lax.rem(gx + dx + NX, NX), lax.rem(gy + dy + NY, NY))

    peers = [at(k, 0) for k in range(1, NX)] + [at(0, k) for k in range(1, NY)]
    peers += [at(dx, dy) for dx in (-1, 1) for dy in (-1, 1)]
    barrier = pltpu.get_barrier_semaphore()
    for peer in peers:
        pl.semaphore_signal(barrier, inc=1, device_id=peer, device_id_type=MESH)

    def remote(src, dst, sems, number, peer):
        return pltpu.make_async_remote_copy(
            src_ref=src, dst_ref=dst, send_sem=sems.at[0, number], recv_sem=sems.at[1, number],
            device_id=peer, device_id_type=MESH,
        )

    sw[0:3] = sea[...]
    sw[3] = depth[...]
    sw[4] = wet[...].astype(f32)
    pl.semaphore_wait(barrier, len(peers))
    ghosts = []
    edges_x = {1: pl.ds(248, 8), -1: pl.ds(0, 8)}
    edges_y = {1: pl.ds(128, 128), -1: pl.ds(0, 128)}
    for n, d in enumerate((1, -1)):
        ghosts.append(remote(sw.at[:, edges_x[d], :], gh_x.at[n], sem_g, n, at(d, 0)))
        ghosts.append(remote(sw.at[:, :, edges_y[d]], gh_y.at[n], sem_g, 2 + n, at(0, d)))
        for m, e in enumerate((1, -1)):
            ghosts.append(remote(sw.at[:, edges_x[d], edges_y[e]], gh_c.at[2 * n + m], sem_g, 4 + 2 * n + m, at(d, e)))
    for copy in ghosts:
        copy.start()

    def spread(source, target, sign):
        def body(i, carry):
            block = source[i]
            for v in range(VARS):
                target[i, v] = jnp.broadcast_to(sign * block[v : v + 1, :], (8, 256))
            return carry
        return body

    lax.fori_loop(0, 27, spread(star, star8, -1.0), 0)
    lax.fori_loop(0, 36, spread(flux9, flux8, 1.0), 0)

    for f in range(4):
        orient8[f] = jnp.broadcast_to(orient[f : f + 1, :], (8, 256))

    low_lanes = iota((192, 128), 1) < 64

    def packed(x, mask):
        high, low = split(x)
        high, low = high.astype(f32), low.astype(f32)
        both = jnp.where(mask, high, pltpu.roll(low, 64, 1))
        return jnp.concatenate([both, both], 1).astype(bf16)

    pieces = []
    for d in range(3):
        zed[...] = jnp.zeros((128, 128), f32)
        zed[0:BASIS, 0:BASIS] = deriv[d]
        pieces.append(zed[...].T[0:64])
    a_op[...] = packed(jnp.concatenate(pieces, 0), low_lanes)
    pieces = []
    for f in range(4):
        zed[...] = jnp.zeros((128, 128), f32)
        zed[0:BASIS, 0:NODES] = trace[f]
        pieces.append(zed[...].T[0:NPAD])
    t_op[...] = packed(jnp.concatenate(pieces, 0), low_lanes[0:96])
    zed[...] = jnp.zeros((128, 128), f32)
    for f in range(4):
        zed[32 * f : 32 * f + NODES, 0:BASIS] = lift[f]
    high, low = split(zed[...].T[0:64])
    l_op[0:64] = jnp.concatenate([high, high], 1)
    l_op[64:128] = jnp.concatenate([low, low], 1)

    def hot(target, count, first, lanes, row):
        def body(i, carry):
            here = iota((64, row.shape[1]), 0) + (64 * i + first)
            target[pl.ds(pl.multiple_of(64 * i, 64), 64), lanes] = jnp.where(here == row, 1.0, 0.0).astype(bf16)
            return carry
        lax.fori_loop(0, count // 64, body, 0)

    for k in range(4):
        hot(g_out, 1024, 0, pl.ds(128 * k, 128), sends[k : k + 1, :])
    hot(g_out, 1024, 0, pl.ds(512, 128), seaf[...])
    for f in range(4):
        hot(p_loc, 1024, 0, pl.ds(256 * f, 256), codes[f : f + 1, :])
        hot(p_arr, 512, 1024, pl.ds(256 * f, 256), codes[f : f + 1, :])

    who = owner[...]
    who_t = jnp.broadcast_to(who, (128, 128)).T
    earlier = iota((128, 128), 0) < iota((128, 128), 1)
    rank = jnp.sum(jnp.where((who_t == who) & earlier, 1.0, 0.0), axis=0, keepdims=True).astype(i32)
    spot = (who // 8) * 16 + jnp.where(rank > 0, 8, 0) + lax.rem(who, 8)
    place[...] = jnp.where(iota((256, 128), 0) == spot, 1.0, 0.0).astype(bf16)
    rows[:, 256:384] = jnp.broadcast_to((blocks[...] + 1).astype(f32), (128, 128)).T
    zed[...] = jnp.zeros((128, 128), f32)

    for v in range(VARS):
        term[v, 56:64] = jnp.zeros((8, 256), f32)
        integ[v, 56:64] = jnp.zeros((8, 256), f32)
        base[v, 56:64] = jnp.zeros((8, 256), f32)
    own[216:224] = jnp.zeros((8, 1024), f32)

    def stacked(source):
        def body(v, carry):
            high, low = split(source[v])
            stack[v, 0:64] = high
            stack[v, 64:128] = high
            stack[v, 128:192] = low
            stack[v, 192:256] = low
            return carry
        lax.fori_loop(0, VARS, body, 0)

    def derive(c_integ, c_base, last):
        for v in range(VARS):
            moved[v] = dot(a_op[...], stack[v])

        def body(g, carry):
            at_rows = pl.ds(pl.multiple_of(8 * g, 8), 8)
            for side in range(2):
                lanes = pl.ds(128 * side, 128)
                m = [
                    [moved[v, pl.ds(pl.multiple_of(64 * d + 8 * g, 8), 8), lanes] for d in range(3)]
                    for v in range(VARS)
                ]
                for u in range(VARS):
                    sums = []
                    for d in range(3):
                        acc = m[0][d] * star8[d * 9 + u, 0, :, lanes]
                        for v in range(1, VARS):
                            acc = acc + m[v][d] * star8[d * 9 + u, v, :, lanes]
                        sums.append(acc)
                    acc = sums[0] + sums[1] + sums[2]
                    base[u, at_rows, lanes] = base[u, at_rows, lanes] + c_base * acc
                    if not last:
                        integ[u, at_rows, lanes] = integ[u, at_rows, lanes] + c_integ * acc
                        term[u, at_rows, lanes] = acc
            return carry

        lax.fori_loop(0, 7, body, 0)

    def predict():
        def body(k, carry):
            c_base = jnp.where(k == 1, 1.0, jnp.where(k == 2, 1 / 2, jnp.where(k == 3, 1 / 6, jnp.where(k == 4, 1 / 24, 1 / 120)))).astype(f32)
            c_integ = jnp.where(k == 1, 1 / 2, jnp.where(k == 2, 1 / 6, jnp.where(k == 3, 1 / 24, jnp.where(k == 4, 1 / 120, 1 / 720)))).astype(f32)
            stacked(term)
            derive(c_integ, c_base, False)
            return carry
        lax.fori_loop(1, ORDER, body, 0)
        stacked(integ)
        for v in range(VARS):
            faces = dot(t_op[...], stack[v])
            for f in range(4):
                own[NPAD * v : NPAD * v + NPAD, 256 * f : 256 * f + 256] = faces[NPAD * f : NPAD * f + NPAD]
        high, low = split(own[...])
        xs[0:224] = high
        xs[224:448] = low

    def pick(step):
        got = dot(xs[...], g_out[...])
        got = got[0:224] + got[224:448]
        for k in range(4):
            sbuf[step, k] = got[:, 128 * k : 128 * k + 128]
        zed[0:NPAD] = got[2 * NPAD : 3 * NPAD, 512:640]
        disp_t[...] = zed[...].T

    def project(target):
        def body(i, carry):
            at_rows = pl.ds(pl.multiple_of(32 * i, 32), 32)
            values = disp_t[at_rows]
            acc = values[:, 0:1] * weights[0, at_rows, :]
            for n in range(1, NODES):
                acc = acc + values[:, n : n + 1] * weights[n, at_rows, :]
            rows[at_rows, 0:256] = acc
            return carry
        lax.fori_loop(0, 4, body, 0)
        count = target.shape[0]
        high, low = split(rows[:, 0 : 128 * count])
        placed = dot(place[...], high) + dot(place[...], low)
        for q in range(count):
            target[q] = placed[:, 128 * q : 128 * q + 128]

    directions = ((-1, 0), (1, 0), (0, -1), (0, 1))

    def face_copies(step):
        return [
            remote(sbuf.at[step, k], arr.at[step, k ^ 1], sem_f, 4 * step + k, at(*directions[k]))
            for k in range(4)
        ]

    def x_copies(step, payload, landing):
        slots = pl.ds(pl.multiple_of(16 * gx, 16), 16)
        copies = []
        for k in range(1, NX):
            to = lax.rem(gx + k, NX)
            block = payload.at[:, pl.ds(pl.multiple_of(16 * to, 16), 16), :]
            copies.append(remote(block, landing.at[:, slots, :], sem_x, 15 * step + k - 1, (to, gy)))
        return copies

    def y_copies(step, message, landing):
        copies = []
        for k in range(1, NY):
            to = lax.rem(gy + k, NY)
            copies.append(remote(message.at[to], landing.at[gy], sem_y, 7 * step + k - 1, (gx, to)))
        return copies

    def keep_x(payload, landing):
        slots = pl.ds(pl.multiple_of(16 * gx, 16), 16)
        for q in range(payload.shape[0]):
            landing[q, slots] = payload[q, slots]

    def regroup(landing, message, final):
        for j in range(NY):
            for q in range(landing.shape[0]):
                message[j, q] = landing[q, pl.ds(j, 32, stride=8)]
        final[gy] = message[gy]

    def local_partner():
        got = dot(xs[...], p_loc[...])
        part[...] = got[0:224] + got[224:448]

    def settle(step, target):
        for k in range(4):
            high, low = split(arr[step, k])
            xa[0:224, 128 * k : 128 * k + 128] = high
            xa[224:448, 128 * k : 128 * k + 128] = low
        got = dot(xa[...], p_arr[...])
        part[...] = part[...] + got[0:224] + got[224:448]

        def body(f, carry):
            for side in range(2):
                lanes = pl.ds(128 * side, 128)
                wide = pl.ds(pl.multiple_of(256 * f + 128 * side, 128), 128)
                turn = orient8[f, :, lanes]
                picks = [
                    jnp.where(turn == 0, turns[0, 8 * g : 8 * g + 8], jnp.where(turn == 1, turns[1, 8 * g : 8 * g + 8], turns[2, 8 * g : 8 * g + 8]))
                    for g in range(3)
                ]
                inner = [lax.rem(p, 8) for p in picks]
                jump = []
                for v in range(VARS):
                    source = [part[NPAD * v + 8 * g : NPAD * v + 8 * g + 8, wide] for g in range(3)]
                    jump.append([])
                    for g in range(3):
                        t = [jnp.take_along_axis(s, inner[g], axis=0, mode="promise_in_bounds") for s in source]
                        turned = jnp.where(picks[g] < 8, t[0], jnp.where(picks[g] < 16, t[1], t[2]))
                        jump[v].append(own[NPAD * v + 8 * g : NPAD * v + 8 * g + 8, wide] - turned)
                for u in range(VARS):
                    acc = None
                    for v in range(VARS):
                        w = flux8[f * 9 + u, v, :, lanes]
                        new = [w * jump[v][g] for g in range(3)]
                        acc = new if acc is None else [a + b for a, b in zip(acc, new)]
                    high, low = split(jnp.concatenate(acc + [jnp.zeros((8, 128), f32)], 0))
                    fstack[u, pl.ds(pl.multiple_of(32 * f, 32), 32), lanes] = high
                    fstack[u, pl.ds(pl.multiple_of(128 + 32 * f, 32), 32), lanes] = low
            return carry

        lax.fori_loop(0, 4, body, 0)
        for u in range(VARS):
            s = dot(l_op[...], fstack[u])
            target[u, 0:BASIS] = base[u, 0:BASIS] - (s[0:64] + s[64:128])[0:BASIS]

    def choose(landing):
        labels = landing[:, 2].reshape(256, 128).T[0:1]
        r = iota((256, 256), 0)
        block = lax.rem(r, 16) * 16 + r // 16
        sel[...] = jnp.where(block.astype(f32) + 1.0 == labels, 1.0, 0.0).astype(bf16)

    lane_group = iota((16, 128), 1) // 16

    def contribute(step, landing):
        got = jnp.concatenate([landing[:, q].reshape(256, 128) for q in range(2)], 1)
        high, low = split(got)
        summed = dot(sel[...], high) + dot(sel[...], low)
        for h in range(2):
            half = summed[:, 128 * h : 128 * h + 128]
            turned = [half if s == 0 else pltpu.roll(half, 16 * s, 1) for s in range(8)]
            for j in range(8):
                cx = 8 * h + j
                for hb in range(2):
                    acc = None
                    for b in range(8):
                        block = 8 * hb + b
                        piece = turned[(b - j) % 8][16 * block : 16 * block + 16]
                        acc = piece if acc is None else jnp.where(lane_group == b, piece, acc)
                    upl[16 * cx : 16 * cx + 16, 128 * hb : 128 * hb + 128] = acc
        high, low = split(upl[...])
        first = dot(wx[...], high)
        first = first[0:352] + first[352:704] + dot(wx[0:352], low)
        high, low = split(first)
        cont[step] = dot(high, wy[:, 0:640]) + dot(low, wy[:, 0:640]) + dot(high, wy[:, 640:1280])

    def halo_copies(step):
        copies = []
        x_part = {1: pl.ds(264, 40), -1: pl.ds(304, 40)}
        y_part = {1: pl.ds(384, 128), -1: pl.ds(512, 128)}
        for n, d in enumerate((1, -1)):
            copies.append(remote(cont.at[step, x_part[d], pl.ds(0, 384)], halo_x.at[step, n], sem_h, 8 * step + n, at(d, 0)))
            copies.append(remote(cont.at[step, pl.ds(0, 264), y_part[d]], halo_y.at[step, n], sem_h, 8 * step + 2 + n, at(0, d)))
            for m, e in enumerate((1, -1)):
                copies.append(remote(cont.at[step, x_part[d], y_part[e]], halo_c.at[step, 2 * n + m], sem_h, 8 * step + 4 + 2 * n + m, at(d, e)))
        return copies

    from_x = (gx > 0, gx < NX - 1)
    from_y = (gy > 0, gy < NY - 1)

    def gather_force(step):
        force[...] = cont[step, 0:EXT_X, 0:EXT_Y]

        def add_lanes(row_slice, value, m):
            low = iota(value.shape, 1) < 64
            first, second = jnp.where(low, value, 0.0), jnp.where(low, 0.0, value)
            if m == 0:
                force[row_slice, 0:128] = force[row_slice, 0:128] + first
                force[row_slice, 256:384] = force[row_slice, 256:384] + second
            else:
                force[row_slice, 256:384] = force[row_slice, 256:384] + first
                force[row_slice, 128:256] = force[row_slice, 128:256] + second

        def row_parts(n):
            return ((slice(0, 32), slice(0, 32)), (slice(256, 264), slice(32, 40))) if n == 0 else ((slice(224, 264), slice(0, 40)),)

        for n in range(2):
            value = jnp.where(from_x[n], halo_x[step, n], 0.0)
            for to, of in row_parts(n):
                force[to] = force[to] + value[of]
            add_lanes(slice(0, EXT_X), jnp.where(from_y[n], halo_y[step, n], 0.0), n)
            for m in range(2):
                value = jnp.where(from_x[n] & from_y[m], halo_c[step, 2 * n + m], 0.0)
                for to, of in row_parts(n):
                    add_lanes(to, value[of], m)

    def extend():
        wide = iota((256, 128), 1) < 64
        thin = iota((8, 128), 1) < 64
        upper = iota((8, 256), 0) < 4
        upper_c = iota((8, 128), 0) < 4
        for q in range(5):
            ext[q, 0:256, 0:256] = sw[q]
            minus = jnp.where(from_y[0], gh_y[0, q], 0.0)
            plus = jnp.where(from_y[1], gh_y[1, q], 0.0)
            ext[q, 0:256, 256:384] = jnp.where(wide, plus, minus)
            minus = jnp.where(from_x[0], gh_x[0, q], 0.0)
            plus = jnp.where(from_x[1], gh_x[1, q], 0.0)
            ext[q, 256:264, 0:256] = jnp.where(upper, plus, minus)
            c = [[jnp.where(from_x[n] & from_y[m], gh_c[2 * n + m, q], 0.0) for m in range(2)] for n in range(2)]
            ext[q, 256:264, 256:384] = jnp.where(
                upper_c, jnp.where(thin, c[1][1], c[1][0]), jnp.where(thin, c[0][1], c[0][0])
            )

    def water(eta, us, vs, hold):
        deep, wetf = ext[3], ext[4]
        eta = eta + wetf * force[...]
        column = deep + eta

        def px(a):
            return pltpu.roll(a, EXT_X - 1, 0)

        def mx(a):
            return pltpu.roll(a, 1, 0)

        def py(a):
            return pltpu.roll(a, EXT_Y - 1, 1)

        def my(a):
            return pltpu.roll(a, 1, 1)

        ep, em, en, es = px(eta), mx(eta), py(eta), my(eta)
        up, um, un, us_ = px(us), mx(us), py(us), my(us)
        vp, vm, vn, vs_ = px(vs), mx(vs), py(vs), my(vs)
        qx, qy = column * us, column * vs
        e2 = 0.25 * (ep + em + en + es) - 0.125 * ((px(qx) - mx(qx)) + (py(qy) - my(qy)))
        u2 = 0.25 * (up + um + un + us_) - 0.125 * (us * (up - um) + vs * (un - us_) + (ep - em))
        v2 = 0.25 * (vp + vm + vn + vs_) - 0.125 * (us * (vp - vm) + vs * (vn - vs_) + (en - es))
        hold(0, e2 * wetf)
        hold(1, u2 * wetf)
        hold(2, v2 * wetf)

    def start(copies):
        for copy in copies:
            copy.start()

    def arrive(copies):
        for copy in copies:
            copy.wait()

    def load_field(source):
        for v in range(VARS):
            value = source[v, 0:BASIS]
            term[v, 0:BASIS] = value
            integ[v, 0:BASIS] = value
            base[v, 0:BASIS] = value

    load_field(state)
    predict()
    pick(0)
    faces = face_copies(0)
    start(faces)
    project(pay0)
    xc = x_copies(0, pay0, bx0)
    start(xc)
    keep_x(pay0, bx0)
    stacked(term)
    derive(0.0, 1 / 720, True)
    local_partner()
    arrive(xc)
    regroup(bx0, my0, by0)
    yc0 = y_copies(0, my0, by0)
    start(yc0)
    arrive(faces)
    settle(0, out_el)

    load_field(out_el)
    predict()
    pick(1)
    project(pay1)
    xc = x_copies(1, pay1, bx1)
    start(xc)
    keep_x(pay1, bx1)
    faces = face_copies(1)
    start(faces)
    arrive(yc0)
    choose(by0)
    contribute(0, by0)
    hc0 = halo_copies(0)
    start(hc0)
    arrive(xc)
    regroup(bx1, my1, by1)
    yc1 = y_copies(1, my1, by1)
    start(yc1)
    stacked(term)
    derive(0.0, 1 / 720, True)
    local_partner()
    arrive(ghosts)
    extend()
    arrive(hc0)
    gather_force(0)

    def keep(n, value):
        ext[n] = value

    water(ext[0], ext[1], ext[2], keep)
    arrive(yc1)
    contribute(1, by1)
    hc1 = halo_copies(1)
    start(hc1)
    arrive(faces)
    settle(1, out_el)
    arrive(hc1)
    gather_force(1)

    def emit(n, value):
        out_oc[n] = value[0:256, 0:256]

    water(ext[0], ext[1], ext[2], emit)


def on_device(
    state, star, deriv, trace_ops, lift, face_flux, orient, neighbours, send_faces, sea_faces,
    sea_owner, sea_blocks, sea_weights, depth, wet, sea_state,
):
    wx, wy = filter_matrices()
    once, twice = turned_nodes()
    turns = np.stack([np.arange(NPAD), once, twice]).astype(np.int32)
    turns = np.broadcast_to(turns[:, :, None], (3, NPAD, 128)).copy()
    V = lambda shape, kind=f32: pltpu.VMEM(shape, kind)
    scratch = [
        V((27, 9, 8, 256)), V((36, 9, 8, 256)), V((192, 256), bf16), V((96, 256), bf16), V((128, 256), bf16),
        V((9, 256, 256), bf16), V((9, 192, 256)), V((9, 64, 256)), V((9, 64, 256)), V((9, 64, 256)),
        V((224, 1024)), V((448, 1024), bf16), V((1024, 640), bf16), V((1024, 1024), bf16), V((512, 1024), bf16),
        V((224, 1024)), V((2, 4, 224, 128)), V((2, 4, 224, 128)), V((448, 512), bf16), V((9, 256, 256), bf16),
        V((128, 128)), V((256, 128), bf16), V((128, 128)), V((128, 384)),
        V((3, 256, 128)), V((2, 256, 128)), V((3, 256, 128)), V((2, 256, 128)),
        V((8, 3, 32, 128)), V((8, 2, 32, 128)), V((8, 3, 32, 128)), V((8, 2, 32, 128)),
        V((256, 256), bf16), V((256, 256)), V((2, 352, 640)),
        V((2, 2, 40, 384)), V((2, 2, 264, 128)), V((2, 4, 40, 128)), V((EXT_X, EXT_Y)),
        V((5, 256, 256)), V((2, 5, 8, 256)), V((2, 5, 256, 128)), V((4, 5, 8, 128)), V((5, EXT_X, EXT_Y)),
        V((4, 8, 256), i32),
        pltpu.SemaphoreType.DMA((2, 8)), pltpu.SemaphoreType.DMA((2, 30)), pltpu.SemaphoreType.DMA((2, 14)),
        pltpu.SemaphoreType.DMA((2, 16)), pltpu.SemaphoreType.DMA((2, 8)),
    ]
    ins = [pl.BlockSpec(memory_space=pltpu.VMEM)] * 19
    return pl.pallas_call(
        kernel,
        out_shape=(jax.ShapeDtypeStruct((9, 56, 256), f32), jax.ShapeDtypeStruct((3, 256, 256), f32)),
        in_specs=ins,
        out_specs=(pl.BlockSpec(memory_space=pltpu.VMEM),) * 2,
        scratch_shapes=scratch,
        compiler_params=pltpu.CompilerParams(
            collective_id=0, has_side_effects=True, vmem_limit_bytes=60 * 2**20
        ),
    )(
        state, star.reshape(27, 9, 256), deriv, trace_ops, lift, face_flux.reshape(36, 9, 256), orient,
        neighbours, send_faces.reshape(4, 128), sea_faces.reshape(1, 128), sea_owner.reshape(1, 128),
        sea_blocks.reshape(1, 128), sea_weights, depth, wet, sea_state,
        jnp.asarray(wx), jnp.asarray(wy), jnp.asarray(turns),
    )


def solution(mesh):
    flat = ("gx", "gy")
    placed = (
        P(None, None, flat), P(None, None, None, flat), P(), P(), P(), P(None, None, None, flat), P(None, flat),
        P(None, flat), P("gx", "gy", None, None), P(flat), P(flat, None), P(flat), P(None, flat, None),
        P("gx", "gy"), P("gx", "gy"), P(None, "gx", "gy"),
    )
    return jax.shard_map(
        on_device, mesh=mesh, in_specs=placed,
        out_specs=(P(None, None, flat), P(None, "gx", "gy")), check_vma=False,
    )
```

```python
import functools
import math

import jax
import jax.numpy as jnp
import numpy as np
from jax import lax
from jax.experimental import pallas as pl
from jax.experimental.pallas import tpu as pltpu
from jax.sharding import PartitionSpec as P

VARS = 9
ORDER = 6
BASIS = 56
NODES = 21
NX, NY = 16, 8
HALF = 32
NPAD = 24
EXT_X, EXT_Y = 264, 384
bf16, f32, i32 = jnp.bfloat16, jnp.float32, jnp.int32
MESH = pl.DeviceIdType.MESH


def turned_nodes():
    upper = ORDER - 1
    nodes = [(i, j) for i in range(upper + 1) for j in range(upper + 1 - i)]
    once = [nodes.index((p[1], upper - p[0] - p[1])) for p in nodes]
    twice = [once[once[n]] for n in range(len(nodes))]
    rest = list(range(NODES, NPAD))
    return np.array(once + rest), np.array(twice + rest)


def filter_matrices():
    k = np.arange(-HALF, HALF + 1)
    raw = 1.0 / np.cosh(math.pi * k / 16.0)
    taps = raw / raw.sum()

    def tap(offset):
        inside = np.abs(offset) <= HALF
        return np.where(inside, taps[np.clip(offset + HALF, 0, 2 * HALF)], 0.0)

    far = 10**6
    cell_x = np.array([r if r < 258 else (r - EXT_X if r >= 262 else far) for r in range(EXT_X)])
    cell_y = np.array([c if c < 258 else (c - EXT_Y if c >= 382 else far) for c in range(EXT_Y)])
    rows_up = np.concatenate([np.arange(0, 32), np.arange(256, 264)])
    rows_down = np.arange(224, 264)
    xs = np.concatenate([cell_x, cell_x[rows_up] + 256, cell_x[rows_down] - 256, np.full(8, far)])
    lane = np.arange(128)
    up = np.where(lane < 64, lane, 256 + lane)
    down = np.where(lane < 64, 256 + lane, 128 + lane)
    ys = np.concatenate([cell_y, cell_y[up] + 256, cell_y[down] - 256])
    column = np.arange(256)
    x_of = (column % 16) * 16 + column // 16
    wx = tap(xs[:, None] - x_of[None, :]).astype(np.float32)
    wy = tap(ys[None, :] - np.arange(256)[:, None]).astype(np.float32)

    def parts(w):
        high = w.astype(jnp.bfloat16)
        low = (w - high.astype(np.float32)).astype(jnp.bfloat16)
        return high, low

    xh, xl = parts(wx)
    yh, yl = parts(wy)
    return np.concatenate([xh, xl], 0), np.concatenate([yh, yl], 1)


def split(x):
    high = x.astype(bf16)
    low = (x - high.astype(f32)).astype(bf16)
    return high, low


def dot(a, b):
    return jnp.dot(a, b, preferred_element_type=f32)


def iota(shape, dim):
    return lax.broadcasted_iota(i32, shape, dim)


def kernel(
    state_h, star_h, deriv_h, trace_h, lift_h, flux_h, orient_h, codes_h, sends_h, seaf_h, owner_h, blocks_h, weights_h,
    depth_h, wet_h, sea_h, wx_h, wy_h, turns_h,
    out_el, out_oc,
    state, star, deriv, trace, lift, flux9, orient, codes, sends, seaf, owner, blocks, weights,
    wet, wx, wy, turns, field, water_out, sem_in, sem_out,
    star8, flux8, a_op, t_op, l_op, stack, istack, moved, integ, base, own, xs, g_out, p_loc, p_arr,
    part, sbuf, arr, xa, fstack, zed, place, disp_t, rows, pay0, pay1, bx0, bx1, my0, my1, by0, by1,
    sel, upl, cont, halo_x, halo_y, halo_c, force, sw, gh_x, gh_y, gh_c, ext,
    orient8, edge_y, sem_f, sem_x, sem_y, sem_h, sem_g,
):
    gx, gy = lax.axis_index("gx"), lax.axis_index("gy")

    def at(dx, dy):
        return (lax.rem(gx + dx + NX, NX), lax.rem(gy + dy + NY, NY))

    peers = [at(k, 0) for k in range(1, NX)] + [at(0, k) for k in range(1, NY)]
    peers += [at(dx, dy) for dx in (-1, 1) for dy in (-1, 1)]
    incoming = {}
    order = (
        ("star", star_h, star), ("deriv", deriv_h, deriv), ("state", state_h, state), ("trace", trace_h, trace),
        ("sends", sends_h, sends), ("seaf", seaf_h, seaf), ("owner", owner_h, owner), ("blocks", blocks_h, blocks),
        ("weights", weights_h, weights), ("codes", codes_h, codes), ("lift", lift_h, lift), ("flux", flux_h, flux9),
        ("orient", orient_h, orient), ("turns", turns_h, turns), ("sea", sea_h, sw.at[0:3]),
        ("depth", depth_h, sw.at[3]), ("wet", wet_h, wet), ("wx", wx_h, wx), ("wy", wy_h, wy),
    )
    for number, (name, source, target) in enumerate(order):
        incoming[name] = pltpu.make_async_copy(source, target, sem_in.at[number])
        incoming[name].start()

    def need(*names):
        for name in names:
            incoming[name].wait()

    barrier = pltpu.get_barrier_semaphore()
    for peer in peers:
        pl.semaphore_signal(barrier, inc=1, device_id=peer, device_id_type=MESH)

    def remote(src, dst, sems, number, peer):
        return pltpu.make_async_remote_copy(
            src_ref=src, dst_ref=dst, send_sem=sems.at[0, number], recv_sem=sems.at[1, number],
            device_id=peer, device_id_type=MESH,
        )

    def spread(source, target, count, sign):
        def body(u, carry):
            block = source[u]
            for v in range(VARS):
                for k in range(count):
                    target[u, v * count + k] = jnp.broadcast_to(sign * block[v, k : k + 1, :], (8, 256))
            return carry
        lax.fori_loop(0, VARS, body, 0)

    def packed(x):
        high, low = split(x)
        high, low = high.astype(f32), low.astype(f32)
        both = jnp.where(iota(x.shape, 1) < 64, high, pltpu.roll(low, 64, 1))
        return jnp.concatenate([both, both], 1).astype(bf16)

    need("star", "deriv")
    spread(star, star8, 3, -1.0)
    pieces = []
    zed[...] = jnp.zeros((128, 128), f32)
    for d in range(3):
        zed[0:BASIS, 0:BASIS] = deriv[d]
        pieces.append(zed[...].T[0:64])
    a_op[...] = packed(jnp.concatenate(pieces, 0))
    need("trace")
    zed[...] = jnp.zeros((128, 128), f32)
    for n in range(NODES):
        for f in range(4):
            zed[NPAD * f + n : NPAD * f + n + 1, 0:BASIS] = trace[n, f : f + 1, :]
    t_op[...] = packed(zed[0:96])
    need("lift")
    zed[...] = jnp.zeros((128, 128), f32)
    for n in range(NODES):
        for f in range(4):
            zed[32 * f + n : 32 * f + n + 1, 0:BASIS] = lift[n, f : f + 1, :]
    high, low = split(zed[...].T[0:64])
    l_op[0:64] = jnp.concatenate([high, high], 1)
    l_op[64:128] = jnp.concatenate([low, low], 1)
    need("flux", "orient", "sends", "seaf", "owner", "blocks", "codes", "turns")
    spread(flux9, flux8, 4, 1.0)
    for f in range(4):
        orient8[f] = jnp.broadcast_to(orient[f : f + 1, :], (8, 256))

    def hot(target, count, first, lanes, row):
        def body(i, carry):
            here = iota((64, row.shape[1]), 0) + (64 * i + first)
            target[pl.ds(pl.multiple_of(64 * i, 64), 64), lanes] = jnp.where(here == row, 1.0, 0.0).astype(bf16)
            return carry
        lax.fori_loop(0, count // 64, body, 0)

    for k in range(4):
        hot(g_out, 1024, 0, pl.ds(128 * k, 128), sends[k : k + 1, :])
    hot(g_out, 1024, 0, pl.ds(512, 128), seaf[...])
    for f in range(4):
        hot(p_loc, 1024, 0, pl.ds(256 * f, 256), codes[f : f + 1, :])
        hot(p_arr, 512, 1024, pl.ds(256 * f, 256), codes[f : f + 1, :])

    who = owner[...]
    who_t = jnp.broadcast_to(who, (128, 128)).T
    earlier = iota((128, 128), 0) < iota((128, 128), 1)
    rank = jnp.sum(jnp.where((who_t == who) & earlier, 1.0, 0.0), axis=0, keepdims=True).astype(i32)
    spot = (who // 8) * 16 + jnp.where(rank > 0, 8, 0) + lax.rem(who, 8)
    place[...] = jnp.where(iota((256, 128), 0) == spot, 1.0, 0.0).astype(bf16)
    rows[:, 256:384] = jnp.broadcast_to((blocks[...] + 1).astype(f32), (128, 128)).T
    zed[...] = jnp.zeros((128, 128), f32)

    own[216:224] = jnp.zeros((8, 1024), f32)

    blank = jnp.zeros((8, 256), f32)

    def load_field(source):
        def body(v, carry):
            value = source[v]
            integ[v] = value
            base[v] = value
            hold_split(stack, v, pl.ds(0, 256), jnp.concatenate([value, blank], 0))
            return carry
        lax.fori_loop(0, VARS, body, 0)

    def hold_split(target, v, lanes, value):
        high, low = split(value)
        target[v, 0:64, lanes] = high
        target[v, 64:128, lanes] = high
        target[v, 128:192, lanes] = low
        target[v, 192:256, lanes] = low

    def derive(c_integ, c_base, last):
        for v in range(VARS):
            moved[v] = dot(a_op[...], stack[v])

        def body(block, carry):
            for side in range(2):
                lanes = pl.ds(128 * side, 128)
                acc = None
                for v in range(VARS):
                    for d in range(3):
                        m = [moved[v, 64 * d + 8 * g : 64 * d + 8 * g + 8, lanes] for g in range(7)]
                        new = []
                        for k in range(3):
                            w = star8[3 * block + k, v * 3 + d, :, lanes]
                            new += [w * x for x in m]
                        acc = new if acc is None else [p + q for p, q in zip(acc, new)]
                for k in range(3):
                    u = 3 * block + k
                    value = jnp.concatenate(acc[7 * k : 7 * k + 7], 0)
                    base[u, :, lanes] = base[u, :, lanes] + c_base * value
                    if not last:
                        integ[u, :, lanes] = integ[u, :, lanes] + c_integ * value
                        hold_split(stack, u, lanes, jnp.concatenate([value, jnp.zeros((8, 128), f32)], 0))
            return carry

        lax.fori_loop(0, 3, body, 0)

    def predict():
        def body(k, carry):
            c_base = jnp.where(k == 1, 1.0, jnp.where(k == 2, 1 / 2, jnp.where(k == 3, 1 / 6, jnp.where(k == 4, 1 / 24, 1 / 120)))).astype(f32)
            c_integ = jnp.where(k == 1, 1 / 2, jnp.where(k == 2, 1 / 6, jnp.where(k == 3, 1 / 24, jnp.where(k == 4, 1 / 120, 1 / 720)))).astype(f32)
            derive(c_integ, c_base, False)
            return carry
        lax.fori_loop(1, ORDER, body, 0)
        for v in range(VARS):
            hold_split(istack, v, pl.ds(0, 256), jnp.concatenate([integ[v], blank], 0))
            faces = dot(t_op[...], istack[v])
            for f in range(4):
                own[NPAD * v : NPAD * v + NPAD, 256 * f : 256 * f + 256] = faces[NPAD * f : NPAD * f + NPAD]
        high, low = split(own[...])
        xs[0:224] = high
        xs[224:448] = low

    def pick(step):
        got = dot(xs[...], g_out[...])
        got = got[0:224] + got[224:448]
        for k in range(4):
            sbuf[step, k] = got[:, 128 * k : 128 * k + 128]
        zed[0:NPAD] = got[2 * NPAD : 3 * NPAD, 512:640]
        disp_t[...] = zed[...].T

    def project(target):
        def body(i, carry):
            at_rows = pl.ds(pl.multiple_of(32 * i, 32), 32)
            values = disp_t[at_rows]
            acc = values[:, 0:1] * weights[0, at_rows, :]
            for n in range(1, NODES):
                acc = acc + values[:, n : n + 1] * weights[n, at_rows, :]
            rows[at_rows, 0:256] = acc
            return carry
        lax.fori_loop(0, 4, body, 0)
        count = target.shape[0]
        high, low = split(rows[:, 0 : 128 * count])
        placed = dot(place[...], high) + dot(place[...], low)
        for q in range(count):
            target[q] = placed[:, 128 * q : 128 * q + 128]

    directions = ((-1, 0), (1, 0), (0, -1), (0, 1))

    def face_copies(step):
        return [
            remote(sbuf.at[step, k], arr.at[step, k ^ 1], sem_f, 4 * step + k, at(*directions[k]))
            for k in range(4)
        ]

    def x_copies(step, payload, landing):
        slots = pl.ds(pl.multiple_of(16 * gx, 16), 16)
        copies = []
        for k in range(1, NX):
            to = lax.rem(gx + k, NX)
            block = payload.at[:, pl.ds(pl.multiple_of(16 * to, 16), 16), :]
            copies.append(remote(block, landing.at[:, slots, :], sem_x, 15 * step + k - 1, (to, gy)))
        return copies

    def y_copies(step, message, landing):
        copies = []
        for k in range(1, NY):
            to = lax.rem(gy + k, NY)
            copies.append(remote(message.at[to], landing.at[gy], sem_y, 7 * step + k - 1, (gx, to)))
        return copies

    def keep_x(payload, landing):
        slots = pl.ds(pl.multiple_of(16 * gx, 16), 16)
        for q in range(payload.shape[0]):
            landing[q, slots] = payload[q, slots]

    def regroup(landing, message, final):
        for j in range(NY):
            for q in range(landing.shape[0]):
                message[j, q] = landing[q, pl.ds(j, 32, stride=8)]
        final[gy] = message[gy]

    def local_partner():
        got = dot(xs[...], p_loc[...])
        part[...] = got[0:224] + got[224:448]

    def settle(step, target):
        for k in range(4):
            high, low = split(arr[step, k])
            xa[0:224, 128 * k : 128 * k + 128] = high
            xa[224:448, 128 * k : 128 * k + 128] = low
        got = dot(xa[...], p_arr[...])
        part[...] = part[...] + got[0:224] + got[224:448]

        def body(f, carry):
            for side in range(2):
                lanes = pl.ds(128 * side, 128)
                wide = pl.ds(pl.multiple_of(256 * f + 128 * side, 128), 128)
                turn = orient8[f, :, lanes]
                picks = [
                    jnp.where(turn == 0, turns[0, 8 * g : 8 * g + 8], jnp.where(turn == 1, turns[1, 8 * g : 8 * g + 8], turns[2, 8 * g : 8 * g + 8]))
                    for g in range(3)
                ]
                inner = [lax.rem(p, 8) for p in picks]
                jump = []
                for v in range(VARS):
                    source = [part[NPAD * v + 8 * g : NPAD * v + 8 * g + 8, wide] for g in range(3)]
                    jump.append([])
                    for g in range(3):
                        t = [jnp.take_along_axis(s, inner[g], axis=0, mode="promise_in_bounds") for s in source]
                        turned = jnp.where(picks[g] < 8, t[0], jnp.where(picks[g] < 16, t[1], t[2]))
                        jump[v].append(own[NPAD * v + 8 * g : NPAD * v + 8 * g + 8, wide] - turned)
                for u in range(VARS):
                    acc = None
                    for v in range(VARS):
                        w = flux8[u, v * 4 + f, :, lanes]
                        new = [w * jump[v][g] for g in range(3)]
                        acc = new if acc is None else [a + b for a, b in zip(acc, new)]
                    high, low = split(jnp.concatenate(acc + [jnp.zeros((8, 128), f32)], 0))
                    fstack[u, pl.ds(pl.multiple_of(32 * f, 32), 32), lanes] = high
                    fstack[u, pl.ds(pl.multiple_of(128 + 32 * f, 32), 32), lanes] = low
            return carry

        lax.fori_loop(0, 4, body, 0)
        for u in range(VARS):
            s = dot(l_op[...], fstack[u])
            target[u] = base[u] - (s[0:64] + s[64:128])[0:BASIS]

    def choose(landing):
        labels = landing[:, 2].reshape(256, 128).T[0:1]
        r = iota((256, 256), 0)
        block = lax.rem(r, 16) * 16 + r // 16
        sel[...] = jnp.where(block.astype(f32) + 1.0 == labels, 1.0, 0.0).astype(bf16)

    lane_group = iota((16, 128), 1) // 16

    def contribute(step, landing):
        got = jnp.concatenate([landing[:, q].reshape(256, 128) for q in range(2)], 1)
        high, low = split(got)
        summed = dot(sel[...], high) + dot(sel[...], low)
        for h in range(2):
            half = summed[:, 128 * h : 128 * h + 128]
            turned = [half if s == 0 else pltpu.roll(half, 16 * s, 1) for s in range(8)]
            for j in range(8):
                cx = 8 * h + j
                for hb in range(2):
                    acc = None
                    for b in range(8):
                        block = 8 * hb + b
                        piece = turned[(b - j) % 8][16 * block : 16 * block + 16]
                        acc = piece if acc is None else jnp.where(lane_group == b, piece, acc)
                    upl[16 * cx : 16 * cx + 16, 128 * hb : 128 * hb + 128] = acc
        high, low = split(upl[...])
        first = dot(wx[...], high)
        first = first[0:352] + first[352:704] + dot(wx[0:352], low)
        high, low = split(first)
        cont[step] = dot(high, wy[:, 0:640]) + dot(low, wy[:, 0:640]) + dot(high, wy[:, 640:1280])

    def halo_copies(step):
        copies = []
        x_part = {1: pl.ds(264, 40), -1: pl.ds(304, 40)}
        y_part = {1: pl.ds(384, 128), -1: pl.ds(512, 128)}
        for n, d in enumerate((1, -1)):
            copies.append(remote(cont.at[step, x_part[d], pl.ds(0, 384)], halo_x.at[step, n], sem_h, 8 * step + n, at(d, 0)))
            copies.append(remote(cont.at[step, pl.ds(0, 264), y_part[d]], halo_y.at[step, n], sem_h, 8 * step + 2 + n, at(0, d)))
            for m, e in enumerate((1, -1)):
                copies.append(remote(cont.at[step, x_part[d], y_part[e]], halo_c.at[step, 2 * n + m], sem_h, 8 * step + 4 + 2 * n + m, at(d, e)))
        return copies

    from_x = (gx > 0, gx < NX - 1)
    from_y = (gy > 0, gy < NY - 1)

    def gather_force(step):
        force[...] = cont[step, 0:EXT_X, 0:EXT_Y]

        def add_lanes(row_slice, value, m):
            low = iota(value.shape, 1) < 64
            first, second = jnp.where(low, value, 0.0), jnp.where(low, 0.0, value)
            if m == 0:
                force[row_slice, 0:128] = force[row_slice, 0:128] + first
                force[row_slice, 256:384] = force[row_slice, 256:384] + second
            else:
                force[row_slice, 256:384] = force[row_slice, 256:384] + first
                force[row_slice, 128:256] = force[row_slice, 128:256] + second

        def row_parts(n):
            return ((slice(0, 32), slice(0, 32)), (slice(256, 264), slice(32, 40))) if n == 0 else ((slice(224, 264), slice(0, 40)),)

        for n in range(2):
            value = jnp.where(from_x[n], halo_x[step, n], 0.0)
            for to, of in row_parts(n):
                force[to] = force[to] + value[of]
            add_lanes(slice(0, EXT_X), jnp.where(from_y[n], halo_y[step, n], 0.0), n)
            for m in range(2):
                value = jnp.where(from_x[n] & from_y[m], halo_c[step, 2 * n + m], 0.0)
                for to, of in row_parts(n):
                    add_lanes(to, value[of], m)

    def ghost_copies():
        copies = []
        edges_x = {1: pl.ds(248, 8), -1: pl.ds(0, 8)}
        edges_y = {1: pl.ds(128, 128), -1: pl.ds(0, 128)}
        for n, d in enumerate((1, -1)):
            copies.append(remote(sw.at[:, edges_x[d], :], gh_x.at[n], sem_g, n, at(d, 0)))
            copies.append(remote(edge_y.at[n], gh_y.at[n], sem_g, 2 + n, at(0, d)))
            for m, e in enumerate((1, -1)):
                copies.append(remote(sw.at[:, edges_x[d], edges_y[e]], gh_c.at[2 * n + m], sem_g, 4 + 2 * n + m, at(d, e)))
        return copies

    def edges():
        sw[4] = wet[...].astype(f32)
        for q in range(5):
            edge_y[0, q] = sw[q, :, 128:256].T[120:128]
            edge_y[1, q] = sw[q, :, 0:128].T[0:8]

    def extend():
        thin = iota((8, 128), 1) < 64
        upper = iota((8, 256), 0) < 4
        upper_c = iota((8, 128), 0) < 4
        for q in range(5):
            ext[q, 0:256, 0:256] = sw[q]
            minus = jnp.where(from_y[0], gh_y[0, q], 0.0)
            plus = jnp.where(from_y[1], gh_y[1, q], 0.0)
            middle = jnp.zeros((112, 256), f32)
            ext[q, 0:256, 256:384] = jnp.concatenate([plus, middle, minus], 0).T
            minus = jnp.where(from_x[0], gh_x[0, q], 0.0)
            plus = jnp.where(from_x[1], gh_x[1, q], 0.0)
            ext[q, 256:264, 0:256] = jnp.where(upper, plus, minus)
            c = [[jnp.where(from_x[n] & from_y[m], gh_c[2 * n + m, q], 0.0) for m in range(2)] for n in range(2)]
            ext[q, 256:264, 256:384] = jnp.where(
                upper_c, jnp.where(thin, c[1][1], c[1][0]), jnp.where(thin, c[0][1], c[0][0])
            )

    def water(eta, us, vs, hold):
        deep, wetf = ext[3], ext[4]
        eta = eta + wetf * force[...]
        column = deep + eta

        def px(a):
            return pltpu.roll(a, EXT_X - 1, 0)

        def mx(a):
            return pltpu.roll(a, 1, 0)

        def py(a):
            return pltpu.roll(a, EXT_Y - 1, 1)

        def my(a):
            return pltpu.roll(a, 1, 1)

        ep, em, en, es = px(eta), mx(eta), py(eta), my(eta)
        up, um, un, us_ = px(us), mx(us), py(us), my(us)
        vp, vm, vn, vs_ = px(vs), mx(vs), py(vs), my(vs)
        qx, qy = column * us, column * vs
        e2 = 0.25 * (ep + em + en + es) - 0.125 * ((px(qx) - mx(qx)) + (py(qy) - my(qy)))
        u2 = 0.25 * (up + um + un + us_) - 0.125 * (us * (up - um) + vs * (un - us_) + (ep - em))
        v2 = 0.25 * (vp + vm + vn + vs_) - 0.125 * (us * (vp - vm) + vs * (vn - vs_) + (en - es))
        hold(0, e2 * wetf)
        hold(1, u2 * wetf)
        hold(2, v2 * wetf)

    def start(copies):
        for copy in copies:
            copy.start()

    def arrive(copies):
        for copy in copies:
            copy.wait()

    pl.semaphore_wait(barrier, len(peers))
    need("state")
    load_field(state)
    predict()
    pick(0)
    faces = face_copies(0)
    start(faces)
    need("weights")
    project(pay0)
    xc = x_copies(0, pay0, bx0)
    start(xc)
    keep_x(pay0, bx0)
    derive(0.0, 1 / 720, True)
    local_partner()
    arrive(xc)
    regroup(bx0, my0, by0)
    yc0 = y_copies(0, my0, by0)
    start(yc0)
    need("sea", "depth", "wet")
    edges()
    ghosts = ghost_copies()
    start(ghosts)
    arrive(faces)
    settle(0, field)

    load_field(field)
    predict()
    pick(1)
    project(pay1)
    xc = x_copies(1, pay1, bx1)
    start(xc)
    keep_x(pay1, bx1)
    faces = face_copies(1)
    start(faces)
    need("wx", "wy")
    arrive(yc0)
    choose(by0)
    contribute(0, by0)
    hc0 = halo_copies(0)
    start(hc0)
    arrive(xc)
    regroup(bx1, my1, by1)
    yc1 = y_copies(1, my1, by1)
    start(yc1)
    derive(0.0, 1 / 720, True)
    local_partner()
    arrive(ghosts)
    extend()
    arrive(hc0)
    gather_force(0)

    def keep(n, value):
        ext[n] = value

    water(ext[0], ext[1], ext[2], keep)
    arrive(yc1)
    contribute(1, by1)
    hc1 = halo_copies(1)
    start(hc1)
    arrive(faces)
    settle(1, field)
    elastic_out = pltpu.make_async_copy(field, out_el, sem_out.at[0])
    elastic_out.start()
    arrive(hc1)
    gather_force(1)

    def emit(n, value):
        water_out[n] = value[0:256, 0:256]

    water(ext[0], ext[1], ext[2], emit)
    ocean_out = pltpu.make_async_copy(water_out, out_oc, sem_out.at[1])
    ocean_out.start()
    elastic_out.wait()
    ocean_out.wait()


def hand_over(a, b, out_a, out_b, sems):
    copies = [pltpu.make_async_copy(a, out_a, sems.at[0]), pltpu.make_async_copy(b, out_b, sems.at[1])]
    for copy in copies:
        copy.start()
    for copy in copies:
        copy.wait()


def on_device(
    state, star, deriv, trace_ops, lift, face_flux, orient, neighbours, send_faces, sea_faces,
    sea_owner, sea_blocks, sea_weights, depth, wet, sea_state,
):
    wx, wy = filter_matrices()
    once, twice = turned_nodes()
    turns = np.stack([np.arange(NPAD), once, twice]).astype(np.int32)
    turns = np.broadcast_to(turns[:, :, None], (3, NPAD, 128)).copy()
    V = lambda shape, kind=f32: pltpu.VMEM(shape, kind)
    scratch = [
        V((9, 56, 256)), V((9, 9, 3, 256)), V((3, 56, 56)), V((21, 4, 56)), V((21, 4, 56)), V((9, 9, 4, 256)),
        V((4, 256), i32), V((4, 256), i32), V((4, 128), i32), V((1, 128), i32), V((1, 128), i32), V((1, 128), i32),
        V((21, 128, 256)), V((256, 256), i32), V((704, 256), bf16), V((256, 1280), bf16), V((3, NPAD, 128), i32),
        V((9, 56, 256)), V((3, 256, 256)), pltpu.SemaphoreType.DMA((19,)), pltpu.SemaphoreType.DMA((2,)),
        V((9, 27, 8, 256)), V((9, 36, 8, 256)), V((192, 256), bf16), V((96, 256), bf16), V((128, 256), bf16),
        V((9, 256, 256), bf16), V((9, 256, 256), bf16), V((9, 192, 256)), V((9, 56, 256)), V((9, 56, 256)),
        V((224, 1024)), V((448, 1024), bf16), V((1024, 640), bf16), V((1024, 1024), bf16), V((512, 1024), bf16),
        V((224, 1024)), V((2, 4, 224, 128)), V((2, 4, 224, 128)), V((448, 512), bf16), V((9, 256, 256), bf16),
        V((128, 128)), V((256, 128), bf16), V((128, 128)), V((128, 384)),
        V((3, 256, 128)), V((2, 256, 128)), V((3, 256, 128)), V((2, 256, 128)),
        V((8, 3, 32, 128)), V((8, 2, 32, 128)), V((8, 3, 32, 128)), V((8, 2, 32, 128)),
        V((256, 256), bf16), V((256, 256)), V((2, 352, 640)),
        V((2, 2, 40, 384)), V((2, 2, 264, 128)), V((2, 4, 40, 128)), V((EXT_X, EXT_Y)),
        V((5, 256, 256)), V((2, 5, 8, 256)), V((2, 5, 8, 256)), V((4, 5, 8, 128)), V((5, EXT_X, EXT_Y)),
        V((4, 8, 256), i32), V((2, 5, 8, 256)),
        pltpu.SemaphoreType.DMA((2, 8)), pltpu.SemaphoreType.DMA((2, 30)), pltpu.SemaphoreType.DMA((2, 14)),
        pltpu.SemaphoreType.DMA((2, 16)), pltpu.SemaphoreType.DMA((2, 8)),
    ]
    place_any = pl.BlockSpec(memory_space=pl.ANY)
    shapes = (jax.ShapeDtypeStruct((9, 56, 256), f32), jax.ShapeDtypeStruct((3, 256, 256), f32))
    results = pl.pallas_call(
        kernel,
        out_shape=shapes,
        in_specs=[place_any] * 19,
        out_specs=(place_any,) * 2,
        scratch_shapes=scratch,
        compiler_params=pltpu.CompilerParams(
            collective_id=0, has_side_effects=True, vmem_limit_bytes=60 * 2**20
        ),
    )(
        state, star.transpose(1, 2, 0, 3), deriv, trace_ops.transpose(2, 0, 1), lift.transpose(1, 0, 2),
        face_flux.transpose(1, 2, 0, 3), orient,
        neighbours, send_faces.reshape(4, 128), sea_faces.reshape(1, 128), sea_owner.reshape(1, 128),
        sea_blocks.reshape(1, 128), sea_weights, depth, wet, sea_state,
        jnp.asarray(wx), jnp.asarray(wy), jnp.asarray(turns),
    )
    return pl.pallas_call(
        hand_over, out_shape=shapes, in_specs=[place_any] * 2, out_specs=(place_any,) * 2,
        scratch_shapes=[pltpu.SemaphoreType.DMA((2,))],
    )(*results)


def solution(mesh):
    flat = ("gx", "gy")
    placed = (
        P(None, None, flat), P(None, None, None, flat), P(), P(), P(), P(None, None, None, flat), P(None, flat),
        P(None, flat), P("gx", "gy", None, None), P(flat), P(flat, None), P(flat), P(None, flat, None),
        P("gx", "gy"), P("gx", "gy"), P(None, "gx", "gy"),
    )
    return jax.shard_map(
        on_device, mesh=mesh, in_specs=placed,
        out_specs=(P(None, None, flat), P(None, "gx", "gy")), check_vma=False,
    )
```

```python
import functools
import math

import jax
import jax.numpy as jnp
import numpy as np
from jax import lax
from jax.experimental import pallas as pl
from jax.experimental.pallas import tpu as pltpu
from jax.sharding import PartitionSpec as P

VARS = 9
ORDER = 6
BASIS = 56
NODES = 21
NX, NY = 16, 8
HALF = 32
NPAD = 24
EXT_X, EXT_Y = 264, 384
bf16, f32, i32 = jnp.bfloat16, jnp.float32, jnp.int32
MESH = pl.DeviceIdType.MESH


def turned_nodes():
    upper = ORDER - 1
    nodes = [(i, j) for i in range(upper + 1) for j in range(upper + 1 - i)]
    once = [nodes.index((p[1], upper - p[0] - p[1])) for p in nodes]
    twice = [once[once[n]] for n in range(len(nodes))]
    rest = list(range(NODES, NPAD))
    return np.array(once + rest), np.array(twice + rest)


def filter_matrices():
    k = np.arange(-HALF, HALF + 1)
    raw = 1.0 / np.cosh(math.pi * k / 16.0)
    taps = raw / raw.sum()

    def tap(offset):
        inside = np.abs(offset) <= HALF
        return np.where(inside, taps[np.clip(offset + HALF, 0, 2 * HALF)], 0.0)

    far = 10**6
    cell_x = np.array([r if r < 258 else (r - EXT_X if r >= 262 else far) for r in range(EXT_X)])
    cell_y = np.array([c if c < 258 else (c - EXT_Y if c >= 382 else far) for c in range(EXT_Y)])
    rows_up = np.concatenate([np.arange(0, 32), np.arange(256, 264)])
    rows_down = np.arange(224, 264)
    xs = np.concatenate([cell_x, cell_x[rows_up] + 256, cell_x[rows_down] - 256, np.full(8, far)])
    lane = np.arange(128)
    up = np.where(lane < 64, lane, 256 + lane)
    down = np.where(lane < 64, 256 + lane, 128 + lane)
    ys = np.concatenate([cell_y, cell_y[up] + 256, cell_y[down] - 256])
    column = np.arange(256)
    x_of = (column % 16) * 16 + column // 16
    wx = tap(xs[:, None] - x_of[None, :]).astype(np.float32)
    wy = tap(ys[None, :] - np.arange(256)[:, None]).astype(np.float32)

    def parts(w):
        high = w.astype(jnp.bfloat16)
        low = (w - high.astype(np.float32)).astype(jnp.bfloat16)
        return high, low

    xh, xl = parts(wx)
    yh, yl = parts(wy)
    return np.concatenate([xh, xl], 0), np.concatenate([yh, yl], 1)


def split(x):
    high = x.astype(bf16)
    low = (x - high.astype(f32)).astype(bf16)
    return high, low


def dot(a, b):
    return jnp.dot(a, b, preferred_element_type=f32)


def iota(shape, dim):
    return lax.broadcasted_iota(i32, shape, dim)


def kernel(
    state_h, star_h, deriv_h, trace_h, lift_h, flux_h, orient_h, codes_h, sends_h, seaf_h, owner_h, blocks_h, weights_h,
    depth_h, wet_h, sea_h, wx_h, wy_h, turns_h,
    out_el, out_oc,
    state, star, deriv, trace, lift, flux9, orient, codes, sends, seaf, owner, blocks, weights,
    wet, wx, wy, turns, field, water_out, sem_in, sem_out,
    star8, flux8, a_op, t_op, l_op, stack_a, stack_b, istack, moved_a, moved_b, integ, base, own, xs, g_out, p_loc, p_arr,
    part, sbuf, arr, xa, fstack, zed, place, disp_t, rows, pay0, pay1, bx0, bx1, my0, my1, by0, by1,
    sel, upl, cont, halo_x, halo_y, halo_c, force, sw, gh_x, gh_y, gh_c, ext,
    orient8, edge_y, sem_f, sem_x, sem_y, sem_h, sem_g,
):
    gx, gy = lax.axis_index("gx"), lax.axis_index("gy")

    def at(dx, dy):
        return (lax.rem(gx + dx + NX, NX), lax.rem(gy + dy + NY, NY))

    peers = [at(k, 0) for k in range(1, NX)] + [at(0, k) for k in range(1, NY)]
    peers += [at(dx, dy) for dx in (-1, 1) for dy in (-1, 1)]
    incoming = {}
    order = (
        ("star", star_h, star), ("deriv", deriv_h, deriv), ("state", state_h, state), ("trace", trace_h, trace),
        ("sends", sends_h, sends), ("seaf", seaf_h, seaf), ("owner", owner_h, owner), ("blocks", blocks_h, blocks),
        ("weights", weights_h, weights), ("codes", codes_h, codes), ("lift", lift_h, lift), ("flux", flux_h, flux9),
        ("orient", orient_h, orient), ("turns", turns_h, turns), ("sea", sea_h, sw.at[0:3]),
        ("depth", depth_h, sw.at[3]), ("wet", wet_h, wet), ("wx", wx_h, wx), ("wy", wy_h, wy),
    )
    for number, (name, source, target) in enumerate(order):
        incoming[name] = pltpu.make_async_copy(source, target, sem_in.at[number])
        incoming[name].start()

    def need(*names):
        for name in names:
            incoming[name].wait()

    barrier = pltpu.get_barrier_semaphore()
    for peer in peers:
        pl.semaphore_signal(barrier, inc=1, device_id=peer, device_id_type=MESH)

    def remote(src, dst, sems, number, peer):
        return pltpu.make_async_remote_copy(
            src_ref=src, dst_ref=dst, send_sem=sems.at[0, number], recv_sem=sems.at[1, number],
            device_id=peer, device_id_type=MESH,
        )

    def spread(source, target, count, sign):
        def body(u, carry):
            block = source[u]
            for v in range(VARS):
                for k in range(count):
                    target[u, v * count + k] = jnp.broadcast_to(sign * block[v, k : k + 1, :], (8, 256))
            return carry
        lax.fori_loop(0, VARS, body, 0)

    def packed(x):
        high, low = split(x)
        high, low = high.astype(f32), low.astype(f32)
        both = jnp.where(iota(x.shape, 1) < 64, high, pltpu.roll(low, 64, 1))
        return jnp.concatenate([both, both], 1).astype(bf16)

    need("star", "deriv")
    spread(star, star8, 3, -1.0)
    pieces = []
    zed[...] = jnp.zeros((128, 128), f32)
    for d in range(3):
        zed[0:BASIS, 0:BASIS] = deriv[d]
        pieces.append(zed[...].T[0:64])
    a_op[...] = packed(jnp.concatenate(pieces, 0))
    need("trace")
    zed[...] = jnp.zeros((128, 128), f32)
    for n in range(NODES):
        for f in range(4):
            zed[NPAD * f + n : NPAD * f + n + 1, 0:BASIS] = trace[n, f : f + 1, :]
    t_op[...] = packed(zed[0:96])
    need("lift")
    zed[...] = jnp.zeros((128, 128), f32)
    for n in range(NODES):
        for f in range(4):
            zed[32 * f + n : 32 * f + n + 1, 0:BASIS] = lift[n, f : f + 1, :]
    high, low = split(zed[...].T[0:64])
    l_op[0:64] = jnp.concatenate([high, high], 1)
    l_op[64:128] = jnp.concatenate([low, low], 1)
    need("flux", "orient", "sends", "seaf", "owner", "blocks", "codes", "turns")
    spread(flux9, flux8, 4, 1.0)
    for f in range(4):
        orient8[f] = jnp.broadcast_to(orient[f : f + 1, :], (8, 256))

    def hot(target, count, first, lanes, row):
        def body(i, carry):
            here = iota((64, row.shape[1]), 0) + (64 * i + first)
            target[pl.ds(pl.multiple_of(64 * i, 64), 64), lanes] = jnp.where(here == row, 1.0, 0.0).astype(bf16)
            return carry
        lax.fori_loop(0, count // 64, body, 0)

    for k in range(4):
        hot(g_out, 1024, 0, pl.ds(128 * k, 128), sends[k : k + 1, :])
    hot(g_out, 1024, 0, pl.ds(512, 128), seaf[...])
    for f in range(4):
        hot(p_loc, 1024, 0, pl.ds(256 * f, 256), codes[f : f + 1, :])
        hot(p_arr, 512, 1024, pl.ds(256 * f, 256), codes[f : f + 1, :])

    who = owner[...]
    who_t = jnp.broadcast_to(who, (128, 128)).T
    earlier = iota((128, 128), 0) < iota((128, 128), 1)
    rank = jnp.sum(jnp.where((who_t == who) & earlier, 1.0, 0.0), axis=0, keepdims=True).astype(i32)
    spot = (who // 8) * 16 + jnp.where(rank > 0, 8, 0) + lax.rem(who, 8)
    place[...] = jnp.where(iota((256, 128), 0) == spot, 1.0, 0.0).astype(bf16)
    rows[:, 256:384] = jnp.broadcast_to((blocks[...] + 1).astype(f32), (128, 128)).T
    zed[...] = jnp.zeros((128, 128), f32)

    own[216:224] = jnp.zeros((8, 1024), f32)

    halves = ((stack_a, moved_a), (stack_b, moved_b))
    blank = jnp.zeros((8, 128), f32)

    def hold_split(target, lanes, value):
        high, low = split(jnp.concatenate([value, blank], 0))
        target[0:64, lanes] = high
        target[64:128, lanes] = high
        target[128:192, lanes] = low
        target[192:256, lanes] = low

    def load_field(source):
        for v in range(VARS):
            value = source[v]
            integ[v] = value
            base[v] = value
            for side in range(2):
                hold_split(halves[side][0], pl.ds(128 * v, 128), value[:, 128 * side : 128 * side + 128])
        moved_a[...] = dot(a_op[...], stack_a[...])

    def phase(side, c_integ, c_base, last, feed):
        held, moved = halves[side]
        other_held, other_moved = halves[1 - side]
        lanes = pl.ds(128 * side, 128)

        def body(block, carry):
            if feed:
                third = pl.ds(pl.multiple_of(384 * block, 128), 384)
                other_moved[:, third] = dot(a_op[...], other_held[:, third])
            acc = None
            for v in range(VARS):
                for d in range(3):
                    m = [moved[64 * d + 8 * g : 64 * d + 8 * g + 8, 128 * v : 128 * v + 128] for g in range(7)]
                    new = []
                    for k in range(3):
                        w = star8[3 * block + k, v * 3 + d, :, lanes]
                        new += [w * x for x in m]
                    acc = new if acc is None else [p + q for p, q in zip(acc, new)]
            for k in range(3):
                u = 3 * block + k
                value = jnp.concatenate(acc[7 * k : 7 * k + 7], 0)
                base[u, :, lanes] = base[u, :, lanes] + c_base * value
                if not last:
                    integ[u, :, lanes] = integ[u, :, lanes] + c_integ * value
                    hold_split(held, pl.ds(pl.multiple_of(128 * u, 128), 128), value)
            return carry

        lax.fori_loop(0, 3, body, 0)

    def derive(c_integ, c_base, last):
        phase(0, c_integ, c_base, last, True)
        phase(1, c_integ, c_base, last, not last)

    def predict(least, most):
        def body(k, carry):
            c_base = jnp.where(k == 1, 1.0, jnp.where(k == 2, 1 / 2, jnp.where(k == 3, 1 / 6, jnp.where(k == 4, 1 / 24, 1 / 120)))).astype(f32)
            c_integ = jnp.where(k == 1, 1 / 2, jnp.where(k == 2, 1 / 6, jnp.where(k == 3, 1 / 24, jnp.where(k == 4, 1 / 120, 1 / 720)))).astype(f32)
            derive(c_integ, c_base, False)
            return carry
        lax.fori_loop(least, most, body, 0)

    def traces():
        for v in range(VARS):
            for side in range(2):
                hold_split(istack, pl.ds(256 * v + 128 * side, 128), integ[v, :, 128 * side : 128 * side + 128])
            faces = dot(t_op[...], istack[:, 256 * v : 256 * v + 256])
            for f in range(4):
                own[NPAD * v : NPAD * v + NPAD, 256 * f : 256 * f + 256] = faces[NPAD * f : NPAD * f + NPAD]
        high, low = split(own[...])
        xs[0:224] = high
        xs[224:448] = low

    def pick(step):
        got = dot(xs[...], g_out[...])
        got = got[0:224] + got[224:448]
        for k in range(4):
            sbuf[step, k] = got[:, 128 * k : 128 * k + 128]
        zed[0:NPAD] = got[2 * NPAD : 3 * NPAD, 512:640]
        disp_t[...] = zed[...].T

    def project(target):
        def body(i, carry):
            at_rows = pl.ds(pl.multiple_of(32 * i, 32), 32)
            values = disp_t[at_rows]
            acc = values[:, 0:1] * weights[0, at_rows, :]
            for n in range(1, NODES):
                acc = acc + values[:, n : n + 1] * weights[n, at_rows, :]
            rows[at_rows, 0:256] = acc
            return carry
        lax.fori_loop(0, 4, body, 0)
        count = target.shape[0]
        high, low = split(rows[:, 0 : 128 * count])
        placed = dot(place[...], high) + dot(place[...], low)
        for q in range(count):
            target[q] = placed[:, 128 * q : 128 * q + 128]

    directions = ((-1, 0), (1, 0), (0, -1), (0, 1))

    def face_copies(step):
        return [
            remote(sbuf.at[step, k], arr.at[step, k ^ 1], sem_f, 4 * step + k, at(*directions[k]))
            for k in range(4)
        ]

    def x_copies(step, payload, landing):
        slots = pl.ds(pl.multiple_of(16 * gx, 16), 16)
        copies = []
        for k in range(1, NX):
            to = lax.rem(gx + k, NX)
            block = payload.at[:, pl.ds(pl.multiple_of(16 * to, 16), 16), :]
            copies.append(remote(block, landing.at[:, slots, :], sem_x, 15 * step + k - 1, (to, gy)))
        return copies

    def y_copies(step, message, landing):
        copies = []
        for k in range(1, NY):
            to = lax.rem(gy + k, NY)
            copies.append(remote(message.at[to], landing.at[gy], sem_y, 7 * step + k - 1, (gx, to)))
        return copies

    def keep_x(payload, landing):
        slots = pl.ds(pl.multiple_of(16 * gx, 16), 16)
        for q in range(payload.shape[0]):
            landing[q, slots] = payload[q, slots]

    def regroup(landing, message, final):
        for j in range(NY):
            for q in range(landing.shape[0]):
                message[j, q] = landing[q, pl.ds(j, 32, stride=8)]
        final[gy] = message[gy]

    def local_partner():
        got = dot(xs[...], p_loc[...])
        part[...] = got[0:224] + got[224:448]

    def settle(step, target):
        for k in range(4):
            high, low = split(arr[step, k])
            xa[0:224, 128 * k : 128 * k + 128] = high
            xa[224:448, 128 * k : 128 * k + 128] = low
        got = dot(xa[...], p_arr[...])
        part[...] = part[...] + got[0:224] + got[224:448]

        def body(f, carry):
            for side in range(2):
                lanes = pl.ds(128 * side, 128)
                wide = pl.ds(pl.multiple_of(256 * f + 128 * side, 128), 128)
                turn = orient8[f, :, lanes]
                picks = [
                    jnp.where(turn == 0, turns[0, 8 * g : 8 * g + 8], jnp.where(turn == 1, turns[1, 8 * g : 8 * g + 8], turns[2, 8 * g : 8 * g + 8]))
                    for g in range(3)
                ]
                inner = [lax.rem(p, 8) for p in picks]
                jump = []
                for v in range(VARS):
                    source = [part[NPAD * v + 8 * g : NPAD * v + 8 * g + 8, wide] for g in range(3)]
                    jump.append([])
                    for g in range(3):
                        t = [jnp.take_along_axis(s, inner[g], axis=0, mode="promise_in_bounds") for s in source]
                        turned = jnp.where(picks[g] < 8, t[0], jnp.where(picks[g] < 16, t[1], t[2]))
                        jump[v].append(own[NPAD * v + 8 * g : NPAD * v + 8 * g + 8, wide] - turned)
                for u in range(VARS):
                    acc = None
                    for v in range(VARS):
                        w = flux8[u, v * 4 + f, :, lanes]
                        new = [w * jump[v][g] for g in range(3)]
                        acc = new if acc is None else [a + b for a, b in zip(acc, new)]
                    high, low = split(jnp.concatenate(acc + [jnp.zeros((8, 128), f32)], 0))
                    fstack[u, pl.ds(pl.multiple_of(32 * f, 32), 32), lanes] = high
                    fstack[u, pl.ds(pl.multiple_of(128 + 32 * f, 32), 32), lanes] = low
            return carry

        lax.fori_loop(0, 4, body, 0)
        for u in range(VARS):
            s = dot(l_op[...], fstack[u])
            target[u] = base[u] - (s[0:64] + s[64:128])[0:BASIS]

    def choose(landing):
        labels = landing[:, 2].reshape(256, 128).T[0:1]
        r = iota((256, 256), 0)
        block = lax.rem(r, 16) * 16 + r // 16
        sel[...] = jnp.where(block.astype(f32) + 1.0 == labels, 1.0, 0.0).astype(bf16)

    lane_group = iota((16, 128), 1) // 16

    def contribute(step, landing):
        got = jnp.concatenate([landing[:, q].reshape(256, 128) for q in range(2)], 1)
        high, low = split(got)
        summed = dot(sel[...], high) + dot(sel[...], low)
        for h in range(2):
            half = summed[:, 128 * h : 128 * h + 128]
            turned = [half if s == 0 else pltpu.roll(half, 16 * s, 1) for s in range(8)]
            for j in range(8):
                cx = 8 * h + j
                for hb in range(2):
                    acc = None
                    for b in range(8):
                        block = 8 * hb + b
                        piece = turned[(b - j) % 8][16 * block : 16 * block + 16]
                        acc = piece if acc is None else jnp.where(lane_group == b, piece, acc)
                    upl[16 * cx : 16 * cx + 16, 128 * hb : 128 * hb + 128] = acc
        high, low = split(upl[...])
        first = dot(wx[...], high)
        first = first[0:352] + first[352:704] + dot(wx[0:352], low)
        high, low = split(first)
        cont[step] = dot(high, wy[:, 0:640]) + dot(low, wy[:, 0:640]) + dot(high, wy[:, 640:1280])

    def halo_copies(step):
        copies = []
        x_part = {1: pl.ds(264, 40), -1: pl.ds(304, 40)}
        y_part = {1: pl.ds(384, 128), -1: pl.ds(512, 128)}
        for n, d in enumerate((1, -1)):
            copies.append(remote(cont.at[step, x_part[d], pl.ds(0, 384)], halo_x.at[step, n], sem_h, 8 * step + n, at(d, 0)))
            copies.append(remote(cont.at[step, pl.ds(0, 264), y_part[d]], halo_y.at[step, n], sem_h, 8 * step + 2 + n, at(0, d)))
            for m, e in enumerate((1, -1)):
                copies.append(remote(cont.at[step, x_part[d], y_part[e]], halo_c.at[step, 2 * n + m], sem_h, 8 * step + 4 + 2 * n + m, at(d, e)))
        return copies

    from_x = (gx > 0, gx < NX - 1)
    from_y = (gy > 0, gy < NY - 1)

    def gather_force(step):
        force[...] = cont[step, 0:EXT_X, 0:EXT_Y]

        def add_lanes(row_slice, value, m):
            low = iota(value.shape, 1) < 64
            first, second = jnp.where(low, value, 0.0), jnp.where(low, 0.0, value)
            if m == 0:
                force[row_slice, 0:128] = force[row_slice, 0:128] + first
                force[row_slice, 256:384] = force[row_slice, 256:384] + second
            else:
                force[row_slice, 256:384] = force[row_slice, 256:384] + first
                force[row_slice, 128:256] = force[row_slice, 128:256] + second

        def row_parts(n):
            return ((slice(0, 32), slice(0, 32)), (slice(256, 264), slice(32, 40))) if n == 0 else ((slice(224, 264), slice(0, 40)),)

        for n in range(2):
            value = jnp.where(from_x[n], halo_x[step, n], 0.0)
            for to, of in row_parts(n):
                force[to] = force[to] + value[of]
            add_lanes(slice(0, EXT_X), jnp.where(from_y[n], halo_y[step, n], 0.0), n)
            for m in range(2):
                value = jnp.where(from_x[n] & from_y[m], halo_c[step, 2 * n + m], 0.0)
                for to, of in row_parts(n):
                    add_lanes(to, value[of], m)

    def ghost_copies():
        copies = []
        edges_x = {1: pl.ds(248, 8), -1: pl.ds(0, 8)}
        edges_y = {1: pl.ds(128, 128), -1: pl.ds(0, 128)}
        for n, d in enumerate((1, -1)):
            copies.append(remote(sw.at[:, edges_x[d], :], gh_x.at[n], sem_g, n, at(d, 0)))
            copies.append(remote(edge_y.at[n], gh_y.at[n], sem_g, 2 + n, at(0, d)))
            for m, e in enumerate((1, -1)):
                copies.append(remote(sw.at[:, edges_x[d], edges_y[e]], gh_c.at[2 * n + m], sem_g, 4 + 2 * n + m, at(d, e)))
        return copies

    def edges():
        sw[4] = wet[...].astype(f32)
        for q in range(5):
            edge_y[0, q] = sw[q, :, 128:256].T[120:128]
            edge_y[1, q] = sw[q, :, 0:128].T[0:8]

    def extend():
        thin = iota((8, 128), 1) < 64
        upper = iota((8, 256), 0) < 4
        upper_c = iota((8, 128), 0) < 4
        for q in range(5):
            ext[q, 0:256, 0:256] = sw[q]
            minus = jnp.where(from_y[0], gh_y[0, q], 0.0)
            plus = jnp.where(from_y[1], gh_y[1, q], 0.0)
            middle = jnp.zeros((112, 256), f32)
            ext[q, 0:256, 256:384] = jnp.concatenate([plus, middle, minus], 0).T
            minus = jnp.where(from_x[0], gh_x[0, q], 0.0)
            plus = jnp.where(from_x[1], gh_x[1, q], 0.0)
            ext[q, 256:264, 0:256] = jnp.where(upper, plus, minus)
            c = [[jnp.where(from_x[n] & from_y[m], gh_c[2 * n + m, q], 0.0) for m in range(2)] for n in range(2)]
            ext[q, 256:264, 256:384] = jnp.where(
                upper_c, jnp.where(thin, c[1][1], c[1][0]), jnp.where(thin, c[0][1], c[0][0])
            )

    def water(eta, us, vs, hold):
        deep, wetf = ext[3], ext[4]
        eta = eta + wetf * force[...]
        column = deep + eta

        def px(a):
            return pltpu.roll(a, EXT_X - 1, 0)

        def mx(a):
            return pltpu.roll(a, 1, 0)

        def py(a):
            return pltpu.roll(a, EXT_Y - 1, 1)

        def my(a):
            return pltpu.roll(a, 1, 1)

        ep, em, en, es = px(eta), mx(eta), py(eta), my(eta)
        up, um, un, us_ = px(us), mx(us), py(us), my(us)
        vp, vm, vn, vs_ = px(vs), mx(vs), py(vs), my(vs)
        qx, qy = column * us, column * vs
        e2 = 0.25 * (ep + em + en + es) - 0.125 * ((px(qx) - mx(qx)) + (py(qy) - my(qy)))
        u2 = 0.25 * (up + um + un + us_) - 0.125 * (us * (up - um) + vs * (un - us_) + (ep - em))
        v2 = 0.25 * (vp + vm + vn + vs_) - 0.125 * (us * (vp - vm) + vs * (vn - vs_) + (en - es))
        hold(0, e2 * wetf)
        hold(1, u2 * wetf)
        hold(2, v2 * wetf)

    def start(copies):
        for copy in copies:
            copy.start()

    def arrive(copies):
        for copy in copies:
            copy.wait()

    pl.semaphore_wait(barrier, len(peers))
    need("state")
    load_field(state)
    predict(1, ORDER)
    traces()
    pick(0)
    faces = face_copies(0)
    start(faces)
    derive(0.0, 1 / 720, True)
    local_partner()
    need("weights")
    project(pay0)
    keep_x(pay0, bx0)
    arrive(faces)
    xc = x_copies(0, pay0, bx0)
    start(xc)
    settle(0, field)

    load_field(field)
    need("sea", "depth", "wet")
    edges()
    ghosts = ghost_copies()
    start(ghosts)
    predict(1, 4)
    arrive(xc)
    regroup(bx0, my0, by0)
    yc0 = y_copies(0, my0, by0)
    start(yc0)
    predict(4, ORDER)
    traces()
    pick(1)
    project(pay1)
    arrive(yc0)
    xc = x_copies(1, pay1, bx1)
    start(xc)
    keep_x(pay1, bx1)
    need("wx", "wy")
    choose(by0)
    contribute(0, by0)
    hc0 = halo_copies(0)
    start(hc0)
    derive(0.0, 1 / 720, True)
    local_partner()
    arrive(xc)
    regroup(bx1, my1, by1)
    yc1 = y_copies(1, my1, by1)
    start(yc1)
    faces = face_copies(1)
    start(faces)
    arrive(ghosts)
    extend()
    arrive(hc0)
    gather_force(0)

    def keep(n, value):
        ext[n] = value

    water(ext[0], ext[1], ext[2], keep)
    arrive(yc1)
    contribute(1, by1)
    hc1 = halo_copies(1)
    start(hc1)
    arrive(faces)
    settle(1, field)
    elastic_out = pltpu.make_async_copy(field, out_el, sem_out.at[0])
    elastic_out.start()
    arrive(hc1)
    gather_force(1)

    def emit(n, value):
        water_out[n] = value[0:256, 0:256]

    water(ext[0], ext[1], ext[2], emit)
    ocean_out = pltpu.make_async_copy(water_out, out_oc, sem_out.at[1])
    ocean_out.start()
    elastic_out.wait()
    ocean_out.wait()


def hand_over(a, b, out_a, out_b, hold_a, hold_b, sems):
    moves = ((a, hold_a), (b, hold_b), (hold_a, out_a), (hold_b, out_b))
    copies = [pltpu.make_async_copy(source, target, sems.at[n]) for n, (source, target) in enumerate(moves)]
    copies[0].start()
    copies[1].start()
    for n in range(2):
        copies[n].wait()
        copies[n + 2].start()
    copies[2].wait()
    copies[3].wait()


def on_device(
    state, star, deriv, trace_ops, lift, face_flux, orient, neighbours, send_faces, sea_faces,
    sea_owner, sea_blocks, sea_weights, depth, wet, sea_state,
):
    wx, wy = filter_matrices()
    once, twice = turned_nodes()
    turns = np.stack([np.arange(NPAD), once, twice]).astype(np.int32)
    turns = np.broadcast_to(turns[:, :, None], (3, NPAD, 128)).copy()
    V = lambda shape, kind=f32: pltpu.VMEM(shape, kind)
    scratch = [
        V((9, 56, 256)), V((9, 9, 3, 256)), V((3, 56, 56)), V((21, 4, 56)), V((21, 4, 56)), V((9, 9, 4, 256)),
        V((4, 256), i32), V((4, 256), i32), V((4, 128), i32), V((1, 128), i32), V((1, 128), i32), V((1, 128), i32),
        V((21, 128, 256)), V((256, 256), i32), V((704, 256), bf16), V((256, 1280), bf16), V((3, NPAD, 128), i32),
        V((9, 56, 256)), V((3, 256, 256)), pltpu.SemaphoreType.DMA((19,)), pltpu.SemaphoreType.DMA((2,)),
        V((9, 27, 8, 256)), V((9, 36, 8, 256)), V((192, 256), bf16), V((96, 256), bf16), V((128, 256), bf16),
        V((256, 1152), bf16), V((256, 1152), bf16), V((256, 2304), bf16), V((192, 1152)), V((192, 1152)), V((9, 56, 256)), V((9, 56, 256)),
        V((224, 1024)), V((448, 1024), bf16), V((1024, 640), bf16), V((1024, 1024), bf16), V((512, 1024), bf16),
        V((224, 1024)), V((2, 4, 224, 128)), V((2, 4, 224, 128)), V((448, 512), bf16), V((9, 256, 256), bf16),
        V((128, 128)), V((256, 128), bf16), V((128, 128)), V((128, 384)),
        V((3, 256, 128)), V((2, 256, 128)), V((3, 256, 128)), V((2, 256, 128)),
        V((8, 3, 32, 128)), V((8, 2, 32, 128)), V((8, 3, 32, 128)), V((8, 2, 32, 128)),
        V((256, 256), bf16), V((256, 256)), V((2, 352, 640)),
        V((2, 2, 40, 384)), V((2, 2, 264, 128)), V((2, 4, 40, 128)), V((EXT_X, EXT_Y)),
        V((5, 256, 256)), V((2, 5, 8, 256)), V((2, 5, 8, 256)), V((4, 5, 8, 128)), V((5, EXT_X, EXT_Y)),
        V((4, 8, 256), i32), V((2, 5, 8, 256)),
        pltpu.SemaphoreType.DMA((2, 8)), pltpu.SemaphoreType.DMA((2, 30)), pltpu.SemaphoreType.DMA((2, 14)),
        pltpu.SemaphoreType.DMA((2, 16)), pltpu.SemaphoreType.DMA((2, 8)),
    ]
    place_any = pl.BlockSpec(memory_space=pl.ANY)
    shapes = (jax.ShapeDtypeStruct((9, 56, 256), f32), jax.ShapeDtypeStruct((3, 256, 256), f32))
    results = pl.pallas_call(
        kernel,
        out_shape=shapes,
        in_specs=[place_any] * 19,
        out_specs=(place_any,) * 2,
        scratch_shapes=scratch,
        compiler_params=pltpu.CompilerParams(
            collective_id=0, has_side_effects=True, vmem_limit_bytes=60 * 2**20
        ),
    )(
        state, star.transpose(1, 2, 0, 3), deriv, trace_ops.transpose(2, 0, 1), lift.transpose(1, 0, 2),
        face_flux.transpose(1, 2, 0, 3), orient,
        neighbours, send_faces.reshape(4, 128), sea_faces.reshape(1, 128), sea_owner.reshape(1, 128),
        sea_blocks.reshape(1, 128), sea_weights, depth, wet, sea_state,
        jnp.asarray(wx), jnp.asarray(wy), jnp.asarray(turns),
    )
    return pl.pallas_call(
        hand_over, out_shape=shapes, in_specs=[place_any] * 2, out_specs=(place_any,) * 2,
        scratch_shapes=[V((9, 56, 256)), V((3, 256, 256)), pltpu.SemaphoreType.DMA((4,))],
    )(*results)


def solution(mesh):
    flat = ("gx", "gy")
    placed = (
        P(None, None, flat), P(None, None, None, flat), P(), P(), P(), P(None, None, None, flat), P(None, flat),
        P(None, flat), P("gx", "gy", None, None), P(flat), P(flat, None), P(flat), P(None, flat, None),
        P("gx", "gy"), P("gx", "gy"), P(None, "gx", "gy"),
    )
    return jax.shard_map(
        on_device, mesh=mesh, in_specs=placed,
        out_specs=(P(None, None, flat), P(None, "gx", "gy")), check_vma=False,
    )
```

```python
import functools
import math

import jax
import jax.numpy as jnp
import numpy as np
from jax import lax
from jax.experimental import pallas as pl
from jax.experimental.pallas import tpu as pltpu
from jax.sharding import PartitionSpec as P

VARS = 9
ORDER = 6
BASIS = 56
NODES = 21
NX, NY = 16, 8
HALF = 32
NPAD = 24
EXT_X, EXT_Y = 264, 384
bf16, f32, i32 = jnp.bfloat16, jnp.float32, jnp.int32
MESH = pl.DeviceIdType.MESH


def turned_nodes():
    upper = ORDER - 1
    nodes = [(i, j) for i in range(upper + 1) for j in range(upper + 1 - i)]
    once = [nodes.index((p[1], upper - p[0] - p[1])) for p in nodes]
    twice = [once[once[n]] for n in range(len(nodes))]
    rest = list(range(NODES, NPAD))
    return np.array(once + rest), np.array(twice + rest)


def filter_matrices():
    k = np.arange(-HALF, HALF + 1)
    raw = 1.0 / np.cosh(math.pi * k / 16.0)
    taps = raw / raw.sum()

    def tap(offset):
        inside = np.abs(offset) <= HALF
        return np.where(inside, taps[np.clip(offset + HALF, 0, 2 * HALF)], 0.0)

    far = 10**6
    cell_x = np.array([r if r < 258 else (r - EXT_X if r >= 262 else far) for r in range(EXT_X)])
    cell_y = np.array([c if c < 258 else (c - EXT_Y if c >= 382 else far) for c in range(EXT_Y)])
    rows_up = np.concatenate([np.arange(0, 32), np.arange(256, 264)])
    rows_down = np.arange(224, 264)
    xs = np.concatenate([cell_x, cell_x[rows_up] + 256, cell_x[rows_down] - 256, np.full(8, far)])
    lane = np.arange(128)
    up = np.where(lane < 64, lane, 256 + lane)
    down = np.where(lane < 64, 256 + lane, 128 + lane)
    ys = np.concatenate([cell_y, cell_y[up] + 256, cell_y[down] - 256])
    column = np.arange(256)
    x_of = (column % 16) * 16 + column // 16
    wx = tap(xs[:, None] - x_of[None, :]).astype(np.float32)
    wy = tap(ys[None, :] - np.arange(256)[:, None]).astype(np.float32)

    def parts(w):
        high = w.astype(jnp.bfloat16)
        low = (w - high.astype(np.float32)).astype(jnp.bfloat16)
        return high, low

    xh, xl = parts(wx)
    yh, yl = parts(wy)
    return np.concatenate([xh, xl], 0), np.concatenate([yh, yl], 1)


def split(x):
    high = x.astype(bf16)
    low = (x - high.astype(f32)).astype(bf16)
    return high, low


def dot(a, b):
    return jnp.dot(a, b, preferred_element_type=f32)


def iota(shape, dim):
    return lax.broadcasted_iota(i32, shape, dim)


def kernel(
    state_h, star_h, deriv_h, trace_h, lift_h, flux_h, orient_h, codes_h, sends_h, seaf_h, owner_h, blocks_h, weights_h,
    depth_h, wet_h, sea_h, wx_h, wy_h, turns_h,
    out_el, out_oc,
    state, star, deriv, trace, lift, flux9, orient, codes, sends, seaf, owner, blocks, weights,
    wet, wx, wy, turns, field, water_out, sem_in, sem_out,
    star8, flux8, a_op, t_op, l_op, stack_a, stack_b, istack, moved_a, moved_b, integ, base, own, xs, g_out, p_loc, p_arr,
    part, sbuf, arr, xa, fstack, zed, place, disp_t, rows, pay0, pay1, bx0, bx1, my0, my1, by0, by1, mx0, mx1, fx0, fx1,
    sel, upl, cont, halo_x, halo_y, halo_c, force, sw, gh_x, gh_y, gh_c, ext,
    orient8, edge_y, zed_l, sem_f, sem_x, sem_y, sem_h, sem_g,
):
    gx, gy = lax.axis_index("gx"), lax.axis_index("gy")

    def at(dx, dy):
        return (lax.rem(gx + dx + NX, NX), lax.rem(gy + dy + NY, NY))

    peers = [at(k, 0) for k in range(1, NX)] + [at(0, k) for k in range(1, NY)]
    peers += [at(dx, dy) for dx in (-1, 1) for dy in (-1, 1)]
    incoming = {}
    order = (
        ("star", star_h, star), ("deriv", deriv_h, deriv), ("state", state_h, state), ("trace", trace_h, trace),
        ("sends", sends_h, sends), ("seaf", seaf_h, seaf), ("owner", owner_h, owner), ("blocks", blocks_h, blocks),
        ("weights", weights_h, weights), ("codes", codes_h, codes), ("lift", lift_h, lift), ("flux", flux_h, flux9),
        ("orient", orient_h, orient), ("turns", turns_h, turns), ("sea", sea_h, sw.at[0:3]),
        ("depth", depth_h, sw.at[3]), ("wet", wet_h, wet), ("wx", wx_h, wx), ("wy", wy_h, wy),
    )
    for number, (name, source, target) in enumerate(order):
        incoming[name] = pltpu.make_async_copy(source, target, sem_in.at[number])
        incoming[name].start()

    def need(*names):
        for name in names:
            incoming[name].wait()

    barrier = pltpu.get_barrier_semaphore()
    for peer in peers:
        pl.semaphore_signal(barrier, inc=1, device_id=peer, device_id_type=MESH)

    def remote(src, dst, sems, number, peer):
        return pltpu.make_async_remote_copy(
            src_ref=src, dst_ref=dst, send_sem=sems.at[0, number], recv_sem=sems.at[1, number],
            device_id=peer, device_id_type=MESH,
        )

    def spread(source, target, count, sign):
        def body(u, carry):
            block = source[u]
            for v in range(VARS):
                for k in range(count):
                    target[u, v * count + k] = jnp.broadcast_to(sign * block[v, k : k + 1, :], (8, 256))
            return carry
        lax.fori_loop(0, VARS, body, 0)

    def packed(x):
        high, low = split(x)
        high, low = high.astype(f32), low.astype(f32)
        both = jnp.where(iota(x.shape, 1) < 64, high, pltpu.roll(low, 64, 1))
        return jnp.concatenate([both, both], 1).astype(bf16)

    need("star", "deriv")
    spread(star, star8, 3, -1.0)
    pieces = []
    zed[...] = jnp.zeros((128, 128), f32)
    for d in range(3):
        zed[0:BASIS, 0:BASIS] = deriv[d]
        pieces.append(zed[...].T[0:64])
    a_op[...] = packed(jnp.concatenate(pieces, 0))
    need("trace")
    zed[...] = jnp.zeros((128, 128), f32)
    for n in range(NODES):
        for f in range(4):
            zed[NPAD * f + n : NPAD * f + n + 1, 0:BASIS] = trace[n, f : f + 1, :]
    t_op[...] = packed(zed[0:96])
    def hot(target, count, first, lanes, row):
        def body(i, carry):
            here = iota((64, row.shape[1]), 0) + (64 * i + first)
            target[pl.ds(pl.multiple_of(64 * i, 64), 64), lanes] = jnp.where(here == row, 1.0, 0.0).astype(bf16)
            return carry
        lax.fori_loop(0, count // 64, body, 0)

    need("sends", "seaf")
    for k in range(4):
        hot(g_out, 1024, 0, pl.ds(128 * k, 128), sends[k : k + 1, :])
    hot(g_out, 1024, 0, pl.ds(512, 128), seaf[...])
    zed[...] = jnp.zeros((128, 128), f32)
    own[216:224] = jnp.zeros((8, 1024), f32)

    def prepare_surface():
        need("lift")
        zed_l[...] = jnp.zeros((128, 128), f32)
        for n in range(NODES):
            for f in range(4):
                zed_l[32 * f + n : 32 * f + n + 1, 0:BASIS] = lift[n, f : f + 1, :]
        high, low = split(zed_l[...].T[0:64])
        l_op[0:64] = jnp.concatenate([high, high], 1)
        l_op[64:128] = jnp.concatenate([low, low], 1)
        need("flux", "orient", "owner", "blocks", "codes", "turns")
        spread(flux9, flux8, 4, 1.0)
        for f in range(4):
            orient8[f] = jnp.broadcast_to(orient[f : f + 1, :], (8, 256))

        for f in range(4):
            hot(p_loc, 1024, 0, pl.ds(256 * f, 256), codes[f : f + 1, :])
            hot(p_arr, 512, 1024, pl.ds(256 * f, 256), codes[f : f + 1, :])

        who = owner[...]
        who_t = jnp.broadcast_to(who, (128, 128)).T
        earlier = iota((128, 128), 0) < iota((128, 128), 1)
        rank = jnp.sum(jnp.where((who_t == who) & earlier, 1.0, 0.0), axis=0, keepdims=True).astype(i32)
        spot = jnp.where(rank > 0, 128 + lax.rem(who, 8) * 16 + who // 8, who)
        place[...] = jnp.where(iota((256, 128), 0) == spot, 1.0, 0.0).astype(bf16)
        rows[:, 256:384] = jnp.broadcast_to((blocks[...] + 1).astype(f32), (128, 128)).T


    halves = ((stack_a, moved_a), (stack_b, moved_b))
    blank = jnp.zeros((8, 128), f32)

    def hold_split(target, lanes, value):
        high, low = split(jnp.concatenate([value, blank], 0))
        target[0:64, lanes] = high
        target[64:128, lanes] = high
        target[128:192, lanes] = low
        target[192:256, lanes] = low

    def load_field(source):
        for v in range(VARS):
            value = source[v]
            integ[v] = value
            base[v] = value
            for side in range(2):
                hold_split(halves[side][0], pl.ds(128 * v, 128), value[:, 128 * side : 128 * side + 128])
        moved_a[...] = dot(a_op[...], stack_a[...])

    def phase(side, c_integ, c_base, last, feed):
        held, moved = halves[side]
        other_held, other_moved = halves[1 - side]
        lanes = pl.ds(128 * side, 128)

        def body(block, carry):
            if feed:
                third = pl.ds(pl.multiple_of(384 * block, 128), 384)
                other_moved[:, third] = dot(a_op[...], other_held[:, third])
            acc = None
            for v in range(VARS):
                for d in range(3):
                    m = [moved[64 * d + 8 * g : 64 * d + 8 * g + 8, 128 * v : 128 * v + 128] for g in range(7)]
                    new = []
                    for k in range(3):
                        w = star8[3 * block + k, v * 3 + d, :, lanes]
                        new += [w * x for x in m]
                    acc = new if acc is None else [p + q for p, q in zip(acc, new)]
            for k in range(3):
                u = 3 * block + k
                value = jnp.concatenate(acc[7 * k : 7 * k + 7], 0)
                base[u, :, lanes] = base[u, :, lanes] + c_base * value
                if not last:
                    integ[u, :, lanes] = integ[u, :, lanes] + c_integ * value
                    hold_split(held, pl.ds(pl.multiple_of(128 * u, 128), 128), value)
            return carry

        lax.fori_loop(0, 3, body, 0)

    def derive(c_integ, c_base, last):
        phase(0, c_integ, c_base, last, True)
        phase(1, c_integ, c_base, last, not last)

    def predict(least, most):
        def body(k, carry):
            c_base = jnp.where(k == 1, 1.0, jnp.where(k == 2, 1 / 2, jnp.where(k == 3, 1 / 6, jnp.where(k == 4, 1 / 24, 1 / 120)))).astype(f32)
            c_integ = jnp.where(k == 1, 1 / 2, jnp.where(k == 2, 1 / 6, jnp.where(k == 3, 1 / 24, jnp.where(k == 4, 1 / 120, 1 / 720)))).astype(f32)
            derive(c_integ, c_base, False)
            return carry
        lax.fori_loop(least, most, body, 0)

    def traces(variables):
        for v in variables:
            for side in range(2):
                hold_split(istack, pl.ds(256 * v + 128 * side, 128), integ[v, :, 128 * side : 128 * side + 128])
            faces = dot(t_op[...], istack[:, 256 * v : 256 * v + 256])
            for f in range(4):
                own[NPAD * v : NPAD * v + NPAD, 256 * f : 256 * f + 256] = faces[NPAD * f : NPAD * f + NPAD]

    def hold_traces():
        high, low = split(own[...])
        xs[0:224] = high
        xs[224:448] = low

    others = tuple(v for v in range(VARS) if v != 2)

    def pick(step):
        got = dot(xs[...], g_out[:, 0:512])
        got = got[0:224] + got[224:448]
        for k in range(4):
            sbuf[step, k] = got[:, 128 * k : 128 * k + 128]

    def project(target):
        upward = jnp.concatenate([own[2 * NPAD : 3 * NPAD], jnp.zeros((8, 1024), f32)], 0)
        high, low = split(upward)
        got = dot(jnp.concatenate([high, low], 0), g_out[:, 512:640])
        zed[0:NPAD] = got[0:NPAD] + got[32 : 32 + NPAD]
        disp_t[...] = zed[...].T

        for i in range(4):
            at_rows = pl.ds(32 * i, 32)
            values = disp_t[at_rows]
            acc = values[:, 0:1] * weights[0, at_rows, :]
            for n in range(1, NODES):
                acc = acc + values[:, n : n + 1] * weights[n, at_rows, :]
            rows[at_rows, 0:256] = acc
        count = target.shape[0]
        high, low = split(rows[:, 0 : 128 * count])
        placed = dot(place[...], high) + dot(place[...], low)
        for q in range(count):
            target[q] = placed[:, 128 * q : 128 * q + 128]

    directions = ((-1, 0), (1, 0), (0, -1), (0, 1))

    def face_copies(step):
        return [
            remote(sbuf.at[step, k], arr.at[step, k ^ 1], sem_f, 4 * step + k, at(*directions[k]))
            for k in range(4)
        ]

    def part_x(k):
        return pl.ds(pl.multiple_of(8 * k, 8), 8)

    def part_y(k):
        return pl.ds(pl.multiple_of(128 + 16 * k, 16), 16)

    def first_copies(step, payload, landing):
        copies = []
        for k in range(1, NX):
            to = lax.rem(gx + k, NX)
            copies.append(remote(payload.at[:, part_x(to), :], landing.at[:, part_x(gx), :], sem_x, 30 * step + k - 1, (to, gy)))
        for k in range(1, NY):
            to = lax.rem(gy + k, NY)
            copies.append(remote(payload.at[:, part_y(to), :], landing.at[:, part_y(gy), :], sem_y, 14 * step + k - 1, (gx, to)))
        return copies

    def second_copies(step, along_y, along_x, final_y, final_x):
        copies = []
        for k in range(1, NX):
            to = lax.rem(gx + k, NX)
            copies.append(remote(along_x.at[to], final_x.at[gx], sem_x, 30 * step + 15 + k - 1, (to, gy)))
        for k in range(1, NY):
            to = lax.rem(gy + k, NY)
            copies.append(remote(along_y.at[to], final_y.at[gy], sem_y, 14 * step + 7 + k - 1, (gx, to)))
        return copies

    def keep_own(payload, landing):
        for q in range(payload.shape[0]):
            landing[q, part_x(gx)] = payload[q, part_x(gx)]
            landing[q, part_y(gy)] = payload[q, part_y(gy)]

    def regroup(landing, along_y, along_x, final_y, final_x):
        for q in range(landing.shape[0]):
            for j in range(NY):
                along_y[j, q] = landing[q, pl.ds(j, 16, stride=8)]
            for i in range(NX):
                along_x[i, q] = landing[q, pl.ds(128 + i, 8, stride=16)]
        final_y[gy] = along_y[gy]
        final_x[gx] = along_x[gx]

    def local_partner():
        got = dot(xs[...], p_loc[...])
        part[...] = got[0:224] + got[224:448]

    def settle(step, target):
        for k in range(4):
            high, low = split(arr[step, k])
            xa[0:224, 128 * k : 128 * k + 128] = high
            xa[224:448, 128 * k : 128 * k + 128] = low
        got = dot(xa[...], p_arr[...])
        part[...] = part[...] + got[0:224] + got[224:448]

        def body(f, carry):
            for side in range(2):
                lanes = pl.ds(128 * side, 128)
                wide = pl.ds(pl.multiple_of(256 * f + 128 * side, 128), 128)
                turn = orient8[f, :, lanes]
                picks = [
                    jnp.where(turn == 0, turns[0, 8 * g : 8 * g + 8], jnp.where(turn == 1, turns[1, 8 * g : 8 * g + 8], turns[2, 8 * g : 8 * g + 8]))
                    for g in range(3)
                ]
                inner = [lax.rem(p, 8) for p in picks]
                jump = []
                for v in range(VARS):
                    source = [part[NPAD * v + 8 * g : NPAD * v + 8 * g + 8, wide] for g in range(3)]
                    jump.append([])
                    for g in range(3):
                        t = [jnp.take_along_axis(s, inner[g], axis=0, mode="promise_in_bounds") for s in source]
                        turned = jnp.where(picks[g] < 8, t[0], jnp.where(picks[g] < 16, t[1], t[2]))
                        jump[v].append(own[NPAD * v + 8 * g : NPAD * v + 8 * g + 8, wide] - turned)
                for u in range(VARS):
                    acc = None
                    for v in range(VARS):
                        w = flux8[u, v * 4 + f, :, lanes]
                        new = [w * jump[v][g] for g in range(3)]
                        acc = new if acc is None else [a + b for a, b in zip(acc, new)]
                    high, low = split(jnp.concatenate(acc + [jnp.zeros((8, 128), f32)], 0))
                    fstack[u, pl.ds(pl.multiple_of(32 * f, 32), 32), lanes] = high
                    fstack[u, pl.ds(pl.multiple_of(128 + 32 * f, 32), 32), lanes] = low
            return carry

        lax.fori_loop(0, 4, body, 0)
        for u in range(VARS):
            s = dot(l_op[...], fstack[u])
            target[u] = base[u] - (s[0:64] + s[64:128])[0:BASIS]

    def landed(final_y, final_x, q):
        return jnp.concatenate([final_y[:, q].reshape(128, 128), final_x[:, q].reshape(128, 128)], 0)

    def choose(final_y, final_x):
        labels = landed(final_y, final_x, 2).T[0:1]
        r = iota((256, 256), 0)
        block = lax.rem(r, 16) * 16 + r // 16
        sel[...] = jnp.where(block.astype(f32) + 1.0 == labels, 1.0, 0.0).astype(bf16)

    lane_group = iota((16, 128), 1) // 16

    def contribute(step, final_y, final_x):
        got = jnp.concatenate([landed(final_y, final_x, q) for q in range(2)], 1)
        high, low = split(got)
        summed = dot(sel[...], high) + dot(sel[...], low)
        for h in range(2):
            half = summed[:, 128 * h : 128 * h + 128]
            turned = [half if s == 0 else pltpu.roll(half, 16 * s, 1) for s in range(8)]
            for j in range(8):
                cx = 8 * h + j
                for hb in range(2):
                    acc = None
                    for b in range(8):
                        block = 8 * hb + b
                        piece = turned[(b - j) % 8][16 * block : 16 * block + 16]
                        acc = piece if acc is None else jnp.where(lane_group == b, piece, acc)
                    upl[16 * cx : 16 * cx + 16, 128 * hb : 128 * hb + 128] = acc
        high, low = split(upl[...])
        first = dot(wx[...], high)
        first = first[0:352] + first[352:704] + dot(wx[0:352], low)
        high, low = split(first)
        cont[step] = dot(high, wy[:, 0:640]) + dot(low, wy[:, 0:640]) + dot(high, wy[:, 640:1280])

    def halo_copies(step):
        copies = []
        x_part = {1: pl.ds(264, 40), -1: pl.ds(304, 40)}
        y_part = {1: pl.ds(384, 128), -1: pl.ds(512, 128)}
        for n, d in enumerate((1, -1)):
            copies.append(remote(cont.at[step, x_part[d], pl.ds(0, 384)], halo_x.at[step, n], sem_h, 8 * step + n, at(d, 0)))
            copies.append(remote(cont.at[step, pl.ds(0, 264), y_part[d]], halo_y.at[step, n], sem_h, 8 * step + 2 + n, at(0, d)))
            for m, e in enumerate((1, -1)):
                copies.append(remote(cont.at[step, x_part[d], y_part[e]], halo_c.at[step, 2 * n + m], sem_h, 8 * step + 4 + 2 * n + m, at(d, e)))
        return copies

    from_x = (gx > 0, gx < NX - 1)
    from_y = (gy > 0, gy < NY - 1)

    def gather_force(step):
        force[...] = cont[step, 0:EXT_X, 0:EXT_Y]

        def add_lanes(row_slice, value, m):
            low = iota(value.shape, 1) < 64
            first, second = jnp.where(low, value, 0.0), jnp.where(low, 0.0, value)
            if m == 0:
                force[row_slice, 0:128] = force[row_slice, 0:128] + first
                force[row_slice, 256:384] = force[row_slice, 256:384] + second
            else:
                force[row_slice, 256:384] = force[row_slice, 256:384] + first
                force[row_slice, 128:256] = force[row_slice, 128:256] + second

        def row_parts(n):
            return ((slice(0, 32), slice(0, 32)), (slice(256, 264), slice(32, 40))) if n == 0 else ((slice(224, 264), slice(0, 40)),)

        for n in range(2):
            value = jnp.where(from_x[n], halo_x[step, n], 0.0)
            for to, of in row_parts(n):
                force[to] = force[to] + value[of]
            add_lanes(slice(0, EXT_X), jnp.where(from_y[n], halo_y[step, n], 0.0), n)
            for m in range(2):
                value = jnp.where(from_x[n] & from_y[m], halo_c[step, 2 * n + m], 0.0)
                for to, of in row_parts(n):
                    add_lanes(to, value[of], m)

    def ghost_copies():
        copies = []
        edges_x = {1: pl.ds(248, 8), -1: pl.ds(0, 8)}
        edges_y = {1: pl.ds(128, 128), -1: pl.ds(0, 128)}
        for n, d in enumerate((1, -1)):
            copies.append(remote(sw.at[:, edges_x[d], :], gh_x.at[n], sem_g, n, at(d, 0)))
            copies.append(remote(edge_y.at[n], gh_y.at[n], sem_g, 2 + n, at(0, d)))
            for m, e in enumerate((1, -1)):
                copies.append(remote(sw.at[:, edges_x[d], edges_y[e]], gh_c.at[2 * n + m], sem_g, 4 + 2 * n + m, at(d, e)))
        return copies

    def edges():
        sw[4] = wet[...].astype(f32)
        for q in range(5):
            edge_y[0, q] = sw[q, :, 128:256].T[120:128]
            edge_y[1, q] = sw[q, :, 0:128].T[0:8]

    def extend():
        thin = iota((8, 128), 1) < 64
        upper = iota((8, 256), 0) < 4
        upper_c = iota((8, 128), 0) < 4
        for q in range(5):
            ext[q, 0:256, 0:256] = sw[q]
            minus = jnp.where(from_y[0], gh_y[0, q], 0.0)
            plus = jnp.where(from_y[1], gh_y[1, q], 0.0)
            middle = jnp.zeros((112, 256), f32)
            ext[q, 0:256, 256:384] = jnp.concatenate([plus, middle, minus], 0).T
            minus = jnp.where(from_x[0], gh_x[0, q], 0.0)
            plus = jnp.where(from_x[1], gh_x[1, q], 0.0)
            ext[q, 256:264, 0:256] = jnp.where(upper, plus, minus)
            c = [[jnp.where(from_x[n] & from_y[m], gh_c[2 * n + m, q], 0.0) for m in range(2)] for n in range(2)]
            ext[q, 256:264, 256:384] = jnp.where(
                upper_c, jnp.where(thin, c[1][1], c[1][0]), jnp.where(thin, c[0][1], c[0][0])
            )

    def water(eta, us, vs, hold):
        deep, wetf = ext[3], ext[4]
        eta = eta + wetf * force[...]
        column = deep + eta

        def px(a):
            return pltpu.roll(a, EXT_X - 1, 0)

        def mx(a):
            return pltpu.roll(a, 1, 0)

        def py(a):
            return pltpu.roll(a, EXT_Y - 1, 1)

        def my(a):
            return pltpu.roll(a, 1, 1)

        ep, em, en, es = px(eta), mx(eta), py(eta), my(eta)
        up, um, un, us_ = px(us), mx(us), py(us), my(us)
        vp, vm, vn, vs_ = px(vs), mx(vs), py(vs), my(vs)
        qx, qy = column * us, column * vs
        e2 = 0.25 * (ep + em + en + es) - 0.125 * ((px(qx) - mx(qx)) + (py(qy) - my(qy)))
        u2 = 0.25 * (up + um + un + us_) - 0.125 * (us * (up - um) + vs * (un - us_) + (ep - em))
        v2 = 0.25 * (vp + vm + vn + vs_) - 0.125 * (us * (vp - vm) + vs * (vn - vs_) + (en - es))
        hold(0, e2 * wetf)
        hold(1, u2 * wetf)
        hold(2, v2 * wetf)

    def start(copies):
        for copy in copies:
            copy.start()

    def arrive(copies):
        for copy in copies:
            copy.wait()

    need("state")
    load_field(state)
    predict(1, ORDER)
    traces(range(VARS))
    hold_traces()
    pick(0)
    pl.semaphore_wait(barrier, len(peers))
    faces = face_copies(0)
    start(faces)
    prepare_surface()
    derive(0.0, 1 / 720, True)
    local_partner()
    need("weights")
    project(pay0)
    keep_own(pay0, bx0)
    need("sea", "depth", "wet")
    edges()
    arrive(faces)
    xc = first_copies(0, pay0, bx0)
    start(xc)
    settle(0, field)

    load_field(field)
    ghosts = ghost_copies()
    start(ghosts)
    predict(1, 4)
    arrive(xc)
    regroup(bx0, my0, mx0, by0, fx0)
    yc0 = second_copies(0, my0, mx0, by0, fx0)
    start(yc0)
    predict(4, ORDER)
    traces((2,))
    project(pay1)
    arrive(yc0)
    xc = first_copies(1, pay1, bx1)
    start(xc)
    keep_own(pay1, bx1)
    traces(others)
    hold_traces()
    pick(1)
    need("wx", "wy")
    choose(by0, fx0)
    contribute(0, by0, fx0)
    hc0 = halo_copies(0)
    start(hc0)
    derive(0.0, 1 / 720, True)
    local_partner()
    arrive(xc)
    regroup(bx1, my1, mx1, by1, fx1)
    yc1 = second_copies(1, my1, mx1, by1, fx1)
    start(yc1)
    faces = face_copies(1)
    start(faces)
    arrive(ghosts)
    extend()
    arrive(hc0)
    gather_force(0)

    def keep(n, value):
        ext[n] = value

    water(ext[0], ext[1], ext[2], keep)
    arrive(yc1)
    contribute(1, by1, fx1)
    hc1 = halo_copies(1)
    start(hc1)
    arrive(faces)
    settle(1, field)
    elastic_out = pltpu.make_async_copy(field, out_el, sem_out.at[0])
    elastic_out.start()
    arrive(hc1)
    gather_force(1)

    def emit(n, value):
        water_out[n] = value[0:256, 0:256]

    water(ext[0], ext[1], ext[2], emit)
    ocean_out = pltpu.make_async_copy(water_out, out_oc, sem_out.at[1])
    ocean_out.start()
    elastic_out.wait()
    ocean_out.wait()


def hand_over(a, b, out_a, out_b, hold_a, hold_b, sems):
    loads, stores = [], []
    for source, hold, target, count in ((a, hold_a, out_a, 3), (b, hold_b, out_b, 3)):
        size = source.shape[0] // count
        for n in range(count):
            some, number = pl.ds(size * n, size), len(loads)
            loads.append(pltpu.make_async_copy(source.at[some], hold.at[some], sems.at[0, number]))
            stores.append(pltpu.make_async_copy(hold.at[some], target.at[some], sems.at[1, number]))
    for copy in loads:
        copy.start()
    for load, store in zip(loads, stores):
        load.wait()
        store.start()
    for copy in stores:
        copy.wait()


def on_device(
    state, star, deriv, trace_ops, lift, face_flux, orient, neighbours, send_faces, sea_faces,
    sea_owner, sea_blocks, sea_weights, depth, wet, sea_state,
):
    wx, wy = filter_matrices()
    once, twice = turned_nodes()
    turns = np.stack([np.arange(NPAD), once, twice]).astype(np.int32)
    turns = np.broadcast_to(turns[:, :, None], (3, NPAD, 128)).copy()
    V = lambda shape, kind=f32: pltpu.VMEM(shape, kind)
    scratch = [
        V((9, 56, 256)), V((9, 9, 3, 256)), V((3, 56, 56)), V((21, 4, 56)), V((21, 4, 56)), V((9, 9, 4, 256)),
        V((4, 256), i32), V((4, 256), i32), V((4, 128), i32), V((1, 128), i32), V((1, 128), i32), V((1, 128), i32),
        V((21, 128, 256)), V((256, 256), i32), V((704, 256), bf16), V((256, 1280), bf16), V((3, NPAD, 128), i32),
        V((9, 56, 256)), V((3, 256, 256)), pltpu.SemaphoreType.DMA((19,)), pltpu.SemaphoreType.DMA((2,)),
        V((9, 27, 8, 256)), V((9, 36, 8, 256)), V((192, 256), bf16), V((96, 256), bf16), V((128, 256), bf16),
        V((256, 1152), bf16), V((256, 1152), bf16), V((256, 2304), bf16), V((192, 1152)), V((192, 1152)), V((9, 56, 256)), V((9, 56, 256)),
        V((224, 1024)), V((448, 1024), bf16), V((1024, 640), bf16), V((1024, 1024), bf16), V((512, 1024), bf16),
        V((224, 1024)), V((2, 4, 224, 128)), V((2, 4, 224, 128)), V((448, 512), bf16), V((9, 256, 256), bf16),
        V((128, 128)), V((256, 128), bf16), V((128, 128)), V((128, 384)),
        V((3, 256, 128)), V((2, 256, 128)), V((3, 256, 128)), V((2, 256, 128)),
        V((8, 3, 16, 128)), V((8, 2, 16, 128)), V((8, 3, 16, 128)), V((8, 2, 16, 128)),
        V((16, 3, 8, 128)), V((16, 2, 8, 128)), V((16, 3, 8, 128)), V((16, 2, 8, 128)),
        V((256, 256), bf16), V((256, 256)), V((2, 352, 640)),
        V((2, 2, 40, 384)), V((2, 2, 264, 128)), V((2, 4, 40, 128)), V((EXT_X, EXT_Y)),
        V((5, 256, 256)), V((2, 5, 8, 256)), V((2, 5, 8, 256)), V((4, 5, 8, 128)), V((5, EXT_X, EXT_Y)),
        V((4, 8, 256), i32), V((2, 5, 8, 256)), V((128, 128)),
        pltpu.SemaphoreType.DMA((2, 8)), pltpu.SemaphoreType.DMA((2, 60)), pltpu.SemaphoreType.DMA((2, 28)),
        pltpu.SemaphoreType.DMA((2, 16)), pltpu.SemaphoreType.DMA((2, 8)),
    ]
    place_any = pl.BlockSpec(memory_space=pl.ANY)
    shapes = (jax.ShapeDtypeStruct((9, 56, 256), f32), jax.ShapeDtypeStruct((3, 256, 256), f32))
    results = pl.pallas_call(
        kernel,
        out_shape=shapes,
        in_specs=[place_any] * 19,
        out_specs=(place_any,) * 2,
        scratch_shapes=scratch,
        compiler_params=pltpu.CompilerParams(
            collective_id=0, has_side_effects=True, vmem_limit_bytes=60 * 2**20
        ),
    )(
        state, star.transpose(1, 2, 0, 3), deriv, trace_ops.transpose(2, 0, 1), lift.transpose(1, 0, 2),
        face_flux.transpose(1, 2, 0, 3), orient,
        neighbours, send_faces.reshape(4, 128), sea_faces.reshape(1, 128), sea_owner.reshape(1, 128),
        sea_blocks.reshape(1, 128), sea_weights, depth, wet, sea_state,
        jnp.asarray(wx), jnp.asarray(wy), jnp.asarray(turns),
    )
    return pl.pallas_call(
        hand_over, out_shape=shapes, in_specs=[place_any] * 2, out_specs=(place_any,) * 2,
        scratch_shapes=[V((9, 56, 256)), V((3, 256, 256)), pltpu.SemaphoreType.DMA((2, 6))],
    )(*results)


def solution(mesh):
    flat = ("gx", "gy")
    placed = (
        P(None, None, flat), P(None, None, None, flat), P(), P(), P(), P(None, None, None, flat), P(None, flat),
        P(None, flat), P("gx", "gy", None, None), P(flat), P(flat, None), P(flat), P(None, flat, None),
        P("gx", "gy"), P("gx", "gy"), P(None, "gx", "gy"),
    )
    return jax.shard_map(
        on_device, mesh=mesh, in_specs=placed,
        out_specs=(P(None, None, flat), P(None, "gx", "gy")), check_vma=False,
    )
```

```python
import functools
import math

import jax
import jax.numpy as jnp
import numpy as np
from jax import lax
from jax.experimental import pallas as pl
from jax.experimental.pallas import tpu as pltpu
from jax.sharding import PartitionSpec as P

VARS = 9
ORDER = 6
BASIS = 56
NODES = 21
NX, NY = 16, 8
HALF = 32
NPAD = 24
EXT_X, EXT_Y = 264, 384
bf16, f32, i32 = jnp.bfloat16, jnp.float32, jnp.int32
MESH = pl.DeviceIdType.MESH


def turned_nodes():
    upper = ORDER - 1
    nodes = [(i, j) for i in range(upper + 1) for j in range(upper + 1 - i)]
    once = [nodes.index((p[1], upper - p[0] - p[1])) for p in nodes]
    twice = [once[once[n]] for n in range(len(nodes))]
    rest = list(range(NODES, NPAD))
    return np.array(once + rest), np.array(twice + rest)


def filter_matrices():
    k = np.arange(-HALF, HALF + 1)
    raw = 1.0 / np.cosh(math.pi * k / 16.0)
    taps = raw / raw.sum()

    def tap(offset):
        inside = np.abs(offset) <= HALF
        return np.where(inside, taps[np.clip(offset + HALF, 0, 2 * HALF)], 0.0)

    far = 10**6
    cell_x = np.array([r if r < 258 else (r - EXT_X if r >= 262 else far) for r in range(EXT_X)])
    cell_y = np.array([c if c < 258 else (c - EXT_Y if c >= 382 else far) for c in range(EXT_Y)])
    rows_up = np.concatenate([np.arange(0, 32), np.arange(256, 264)])
    rows_down = np.arange(224, 264)
    xs = np.concatenate([cell_x, cell_x[rows_up] + 256, cell_x[rows_down] - 256, np.full(8, far)])
    lane = np.arange(128)
    up = np.where(lane < 64, lane, 256 + lane)
    down = np.where(lane < 64, 256 + lane, 128 + lane)
    ys = np.concatenate([cell_y, cell_y[up] + 256, cell_y[down] - 256])
    column = np.arange(256)
    x_of = (column % 16) * 16 + column // 16
    wx = tap(xs[:, None] - x_of[None, :]).astype(np.float32)
    wy = tap(ys[None, :] - np.arange(256)[:, None]).astype(np.float32)

    def parts(w):
        high = w.astype(jnp.bfloat16)
        low = (w - high.astype(np.float32)).astype(jnp.bfloat16)
        return high, low

    xh, xl = parts(wx)
    yh, yl = parts(wy)
    return np.concatenate([xh, xl], 0), np.concatenate([yh, yl], 1)


def split(x):
    high = x.astype(bf16)
    low = (x - high.astype(f32)).astype(bf16)
    return high, low


def dot(a, b):
    return jnp.dot(a, b, preferred_element_type=f32)


def iota(shape, dim):
    return lax.broadcasted_iota(i32, shape, dim)


def kernel(
    state_h, star_h, deriv_h, trace_h, lift_h, flux_h, orient_h, codes_h, sends_h, seaf_h, owner_h, blocks_h, weights_h,
    depth_h, wet_h, sea_h, wx_h, wy_h, turns_h,
    out_el, out_oc,
    state, star, deriv, trace, lift, flux9, orient, codes, sends, seaf, owner, blocks, weights,
    wet, wx, wy, turns, field, water_out, sem_in, sem_out,
    star8, flux8, a_op, t_op, l_op, stack_a, stack_b, istack, moved_a, moved_b, integ, base, own, xs, g_out, p_loc, p_arr,
    part, sbuf, arr, xa, fstack, zed, place, disp_t, rows, pay0, pay1, bx0, bx1, my0, my1, by0, by1, mx0, mx1, fx0, fx1,
    sel, upl, cont, halo_x, halo_y, halo_c, force, sw, gh_x, gh_y, gh_c, ext,
    orient8, edge_y, zed_l, sem_f, sem_x, sem_y, sem_h, sem_g,
):
    gx, gy = lax.axis_index("gx"), lax.axis_index("gy")

    def at(dx, dy):
        return (lax.rem(gx + dx + NX, NX), lax.rem(gy + dy + NY, NY))

    peers = [at(k, 0) for k in range(1, NX)] + [at(0, k) for k in range(1, NY)]
    peers += [at(dx, dy) for dx in (-1, 1) for dy in (-1, 1)]
    incoming = {}
    order = (
        ("star", star_h, star), ("deriv", deriv_h, deriv), ("state", state_h, state), ("trace", trace_h, trace),
        ("sends", sends_h, sends), ("seaf", seaf_h, seaf), ("owner", owner_h, owner), ("blocks", blocks_h, blocks),
        ("weights", weights_h, weights), ("codes", codes_h, codes), ("lift", lift_h, lift), ("flux", flux_h, flux9),
        ("orient", orient_h, orient), ("turns", turns_h, turns), ("sea", sea_h, sw.at[0:3]),
        ("depth", depth_h, sw.at[3]), ("wet", wet_h, wet), ("wx", wx_h, wx), ("wy", wy_h, wy),
    )
    for number, (name, source, target) in enumerate(order):
        incoming[name] = pltpu.make_async_copy(source, target, sem_in.at[number])
        incoming[name].start()

    def need(*names):
        for name in names:
            incoming[name].wait()

    barrier = pltpu.get_barrier_semaphore()
    for peer in peers:
        pl.semaphore_signal(barrier, inc=1, device_id=peer, device_id_type=MESH)

    def remote(src, dst, sems, number, peer):
        return pltpu.make_async_remote_copy(
            src_ref=src, dst_ref=dst, send_sem=sems.at[0, number], recv_sem=sems.at[1, number],
            device_id=peer, device_id_type=MESH,
        )

    def spread(source, target, count, sign):
        def body(u, carry):
            block = source[u]
            for v in range(VARS):
                for k in range(count):
                    target[u, v * count + k] = jnp.broadcast_to(sign * block[v, k : k + 1, :], (8, 256))
            return carry
        lax.fori_loop(0, VARS, body, 0)

    def packed(x):
        high, low = split(x)
        high, low = high.astype(f32), low.astype(f32)
        both = jnp.where(iota(x.shape, 1) < 64, high, pltpu.roll(low, 64, 1))
        return jnp.concatenate([both, both], 1).astype(bf16)

    need("star", "deriv")
    spread(star, star8, 3, -1.0)
    pieces = []
    zed[...] = jnp.zeros((128, 128), f32)
    for d in range(3):
        zed[0:BASIS, 0:BASIS] = deriv[d]
        pieces.append(zed[...].T[0:64])
    a_op[...] = packed(jnp.concatenate(pieces, 0))
    need("trace")
    zed[...] = jnp.zeros((128, 128), f32)
    for n in range(NODES):
        for f in range(4):
            zed[NPAD * f + n : NPAD * f + n + 1, 0:BASIS] = trace[n, f : f + 1, :]
    t_op[...] = packed(zed[0:96])
    def hot(target, count, first, lanes, row):
        def body(i, carry):
            here = iota((64, row.shape[1]), 0) + (64 * i + first)
            target[pl.ds(pl.multiple_of(64 * i, 64), 64), lanes] = jnp.where(here == row, 1.0, 0.0).astype(bf16)
            return carry
        lax.fori_loop(0, count // 64, body, 0)

    need("sends", "seaf")
    for k in range(4):
        hot(g_out, 1024, 0, pl.ds(128 * k, 128), sends[k : k + 1, :])
    hot(g_out, 1024, 0, pl.ds(512, 128), seaf[...])
    zed[...] = jnp.zeros((128, 128), f32)
    own[216:224] = jnp.zeros((8, 1024), f32)

    def prepare_surface():
        need("lift")
        zed_l[...] = jnp.zeros((128, 128), f32)
        for n in range(NODES):
            for f in range(4):
                zed_l[32 * f + n : 32 * f + n + 1, 0:BASIS] = lift[n, f : f + 1, :]
        high, low = split(zed_l[...].T[0:64])
        l_op[0:64] = jnp.concatenate([high, high], 1)
        l_op[64:128] = jnp.concatenate([low, low], 1)
        need("flux", "orient", "owner", "blocks", "codes", "turns")
        spread(flux9, flux8, 4, 1.0)
        for f in range(4):
            orient8[f] = jnp.broadcast_to(orient[f : f + 1, :], (8, 256))

        for f in range(4):
            hot(p_loc, 1024, 0, pl.ds(256 * f, 256), codes[f : f + 1, :])
            hot(p_arr, 512, 1024, pl.ds(256 * f, 256), codes[f : f + 1, :])

        who = owner[...]
        who_t = jnp.broadcast_to(who, (128, 128)).T
        earlier = iota((128, 128), 0) < iota((128, 128), 1)
        rank = jnp.sum(jnp.where((who_t == who) & earlier, 1.0, 0.0), axis=0, keepdims=True).astype(i32)
        spot = jnp.where(rank > 0, 128 + lax.rem(who, 8) * 16 + who // 8, who)
        place[...] = jnp.where(iota((256, 128), 0) == spot, 1.0, 0.0).astype(bf16)
        rows[:, 256:384] = jnp.broadcast_to((blocks[...] + 1).astype(f32), (128, 128)).T


    halves = ((stack_a, moved_a), (stack_b, moved_b))
    blank = jnp.zeros((8, 128), f32)

    def hold_split(target, lanes, value):
        high, low = split(jnp.concatenate([value, blank], 0))
        target[0:64, lanes] = high
        target[64:128, lanes] = high
        target[128:192, lanes] = low
        target[192:256, lanes] = low

    def load_field(source):
        for v in range(VARS):
            value = source[v]
            integ[v] = value
            base[v] = value
            for side in range(2):
                hold_split(halves[side][0], pl.ds(128 * v, 128), value[:, 128 * side : 128 * side + 128])
        moved_a[...] = dot(a_op[...], stack_a[...])

    def phase(side, c_integ, c_base, last, feed):
        held, moved = halves[side]
        other_held, other_moved = halves[1 - side]
        lanes = pl.ds(128 * side, 128)

        def body(block, carry):
            if feed:
                third = pl.ds(pl.multiple_of(384 * block, 128), 384)
                other_moved[:, third] = dot(a_op[...], other_held[:, third])
            acc = None
            for v in range(VARS):
                for d in range(3):
                    m = [moved[64 * d + 8 * g : 64 * d + 8 * g + 8, 128 * v : 128 * v + 128] for g in range(7)]
                    new = []
                    for k in range(3):
                        w = star8[3 * block + k, v * 3 + d, :, lanes]
                        new += [w * x for x in m]
                    acc = new if acc is None else [p + q for p, q in zip(acc, new)]
            for k in range(3):
                u = 3 * block + k
                value = jnp.concatenate(acc[7 * k : 7 * k + 7], 0)
                base[u, :, lanes] = base[u, :, lanes] + c_base * value
                if not last:
                    integ[u, :, lanes] = integ[u, :, lanes] + c_integ * value
                    hold_split(held, pl.ds(pl.multiple_of(128 * u, 128), 128), value)
            return carry

        lax.fori_loop(0, 3, body, 0)

    def derive(c_integ, c_base, last):
        phase(0, c_integ, c_base, last, True)
        phase(1, c_integ, c_base, last, not last)

    def predict(least, most):
        def body(k, carry):
            c_base = jnp.where(k == 1, 1.0, jnp.where(k == 2, 1 / 2, jnp.where(k == 3, 1 / 6, jnp.where(k == 4, 1 / 24, 1 / 120)))).astype(f32)
            c_integ = jnp.where(k == 1, 1 / 2, jnp.where(k == 2, 1 / 6, jnp.where(k == 3, 1 / 24, jnp.where(k == 4, 1 / 120, 1 / 720)))).astype(f32)
            derive(c_integ, c_base, False)
            return carry
        lax.fori_loop(least, most, body, 0)

    def traces(variables):
        for v in variables:
            for side in range(2):
                hold_split(istack, pl.ds(256 * v + 128 * side, 128), integ[v, :, 128 * side : 128 * side + 128])
            faces = dot(t_op[...], istack[:, 256 * v : 256 * v + 256])
            for f in range(4):
                own[NPAD * v : NPAD * v + NPAD, 256 * f : 256 * f + 256] = faces[NPAD * f : NPAD * f + NPAD]

    def hold_traces():
        high, low = split(own[...])
        xs[0:224] = high
        xs[224:448] = low

    others = tuple(v for v in range(VARS) if v != 2)

    def pick(step):
        got = dot(xs[...], g_out[:, 0:512])
        got = got[0:224] + got[224:448]
        for k in range(4):
            sbuf[step, k] = got[:, 128 * k : 128 * k + 128]

    def project(target):
        upward = jnp.concatenate([own[2 * NPAD : 3 * NPAD], jnp.zeros((8, 1024), f32)], 0)
        high, low = split(upward)
        got = dot(jnp.concatenate([high, low], 0), g_out[:, 512:640])
        zed[0:NPAD] = got[0:NPAD] + got[32 : 32 + NPAD]
        disp_t[...] = zed[...].T

        for i in range(4):
            at_rows = pl.ds(32 * i, 32)
            values = disp_t[at_rows]
            acc = values[:, 0:1] * weights[0, at_rows, :]
            for n in range(1, NODES):
                acc = acc + values[:, n : n + 1] * weights[n, at_rows, :]
            rows[at_rows, 0:256] = acc
        count = target.shape[0]
        high, low = split(rows[:, 0 : 128 * count])
        placed = dot(place[...], high) + dot(place[...], low)
        for q in range(count):
            target[q] = placed[:, 128 * q : 128 * q + 128]

    directions = ((-1, 0), (1, 0), (0, -1), (0, 1))

    def face_copies(step):
        return [
            remote(sbuf.at[step, k], arr.at[step, k ^ 1], sem_f, 4 * step + k, at(*directions[k]))
            for k in range(4)
        ]

    def part_x(k):
        return pl.ds(pl.multiple_of(8 * k, 8), 8)

    def part_y(k):
        return pl.ds(pl.multiple_of(128 + 16 * k, 16), 16)

    def first_copies(step, payload, landing):
        copies = []
        for k in range(1, NX):
            to = lax.rem(gx + k, NX)
            copies.append(remote(payload.at[:, part_x(to), :], landing.at[:, part_x(gx), :], sem_x, 30 * step + k - 1, (to, gy)))
        for k in range(1, NY):
            to = lax.rem(gy + k, NY)
            copies.append(remote(payload.at[:, part_y(to), :], landing.at[:, part_y(gy), :], sem_y, 14 * step + k - 1, (gx, to)))
        return copies

    def second_copies(step, along_y, along_x, final_y, final_x):
        copies = []
        for k in range(1, NX):
            to = lax.rem(gx + k, NX)
            copies.append(remote(along_x.at[to], final_x.at[gx], sem_x, 30 * step + 15 + k - 1, (to, gy)))
        for k in range(1, NY):
            to = lax.rem(gy + k, NY)
            copies.append(remote(along_y.at[to], final_y.at[gy], sem_y, 14 * step + 7 + k - 1, (gx, to)))
        return copies

    def keep_own(payload, landing):
        for q in range(payload.shape[0]):
            landing[q, part_x(gx)] = payload[q, part_x(gx)]
            landing[q, part_y(gy)] = payload[q, part_y(gy)]

    def regroup(landing, along_y, along_x, final_y, final_x):
        for q in range(landing.shape[0]):
            for j in range(NY):
                along_y[j, q] = landing[q, pl.ds(j, 16, stride=8)]
            for i in range(NX):
                along_x[i, q] = landing[q, pl.ds(128 + i, 8, stride=16)]
        final_y[gy] = along_y[gy]
        final_x[gx] = along_x[gx]

    def local_partner():
        got = dot(xs[...], p_loc[...])
        part[...] = got[0:224] + got[224:448]

    def settle(step, target):
        for k in range(4):
            high, low = split(arr[step, k])
            xa[0:224, 128 * k : 128 * k + 128] = high
            xa[224:448, 128 * k : 128 * k + 128] = low
        got = dot(xa[...], p_arr[...])
        part[...] = part[...] + got[0:224] + got[224:448]

        def body(f, carry):
            for side in range(2):
                lanes = pl.ds(128 * side, 128)
                wide = pl.ds(pl.multiple_of(256 * f + 128 * side, 128), 128)
                turn = orient8[f, :, lanes]
                picks = [
                    jnp.where(turn == 0, turns[0, 8 * g : 8 * g + 8], jnp.where(turn == 1, turns[1, 8 * g : 8 * g + 8], turns[2, 8 * g : 8 * g + 8]))
                    for g in range(3)
                ]
                inner = [lax.rem(p, 8) for p in picks]
                jump = []
                for v in range(VARS):
                    source = [part[NPAD * v + 8 * g : NPAD * v + 8 * g + 8, wide] for g in range(3)]
                    jump.append([])
                    for g in range(3):
                        t = [jnp.take_along_axis(s, inner[g], axis=0, mode="promise_in_bounds") for s in source]
                        turned = jnp.where(picks[g] < 8, t[0], jnp.where(picks[g] < 16, t[1], t[2]))
                        jump[v].append(own[NPAD * v + 8 * g : NPAD * v + 8 * g + 8, wide] - turned)
                for u in range(VARS):
                    acc = None
                    for v in range(VARS):
                        w = flux8[u, v * 4 + f, :, lanes]
                        new = [w * jump[v][g] for g in range(3)]
                        acc = new if acc is None else [a + b for a, b in zip(acc, new)]
                    high, low = split(jnp.concatenate(acc + [jnp.zeros((8, 128), f32)], 0))
                    fstack[u, pl.ds(pl.multiple_of(32 * f, 32), 32), lanes] = high
                    fstack[u, pl.ds(pl.multiple_of(128 + 32 * f, 32), 32), lanes] = low
            return carry

        lax.fori_loop(0, 4, body, 0)
        for u in range(VARS):
            s = dot(l_op[...], fstack[u])
            target[u] = base[u] - (s[0:64] + s[64:128])[0:BASIS]

    def landed(final_y, final_x, q):
        return jnp.concatenate([final_y[:, q].reshape(128, 128), final_x[:, q].reshape(128, 128)], 0)

    def choose(final_y, final_x):
        labels = landed(final_y, final_x, 2).T[0:1]
        r = iota((256, 256), 0)
        block = lax.rem(r, 16) * 16 + r // 16
        sel[...] = jnp.where(block.astype(f32) + 1.0 == labels, 1.0, 0.0).astype(bf16)

    lane_group = iota((16, 128), 1) // 16

    def contribute(step, final_y, final_x):
        got = jnp.concatenate([landed(final_y, final_x, q) for q in range(2)], 1)
        high, low = split(got)
        summed = dot(sel[...], high) + dot(sel[...], low)
        for h in range(2):
            half = summed[:, 128 * h : 128 * h + 128]
            turned = [half if s == 0 else pltpu.roll(half, 16 * s, 1) for s in range(8)]
            for j in range(8):
                cx = 8 * h + j
                for hb in range(2):
                    acc = None
                    for b in range(8):
                        block = 8 * hb + b
                        piece = turned[(b - j) % 8][16 * block : 16 * block + 16]
                        acc = piece if acc is None else jnp.where(lane_group == b, piece, acc)
                    upl[16 * cx : 16 * cx + 16, 128 * hb : 128 * hb + 128] = acc
        high, low = split(upl[...])
        first = dot(wx[...], high)
        first = first[0:352] + first[352:704] + dot(wx[0:352], low)
        high, low = split(first)
        cont[step] = dot(high, wy[:, 0:640]) + dot(low, wy[:, 0:640]) + dot(high, wy[:, 640:1280])

    def halo_copies(step):
        copies = []
        x_part = {1: pl.ds(264, 40), -1: pl.ds(304, 40)}
        y_part = {1: pl.ds(384, 128), -1: pl.ds(512, 128)}
        for n, d in enumerate((1, -1)):
            copies.append(remote(cont.at[step, x_part[d], pl.ds(0, 384)], halo_x.at[step, n], sem_h, 8 * step + n, at(d, 0)))
            copies.append(remote(cont.at[step, pl.ds(0, 264), y_part[d]], halo_y.at[step, n], sem_h, 8 * step + 2 + n, at(0, d)))
            for m, e in enumerate((1, -1)):
                copies.append(remote(cont.at[step, x_part[d], y_part[e]], halo_c.at[step, 2 * n + m], sem_h, 8 * step + 4 + 2 * n + m, at(d, e)))
        return copies

    from_x = (gx > 0, gx < NX - 1)
    from_y = (gy > 0, gy < NY - 1)

    def gather_force(step):
        force[...] = cont[step, 0:EXT_X, 0:EXT_Y]

        def add_lanes(row_slice, value, m):
            low = iota(value.shape, 1) < 64
            first, second = jnp.where(low, value, 0.0), jnp.where(low, 0.0, value)
            if m == 0:
                force[row_slice, 0:128] = force[row_slice, 0:128] + first
                force[row_slice, 256:384] = force[row_slice, 256:384] + second
            else:
                force[row_slice, 256:384] = force[row_slice, 256:384] + first
                force[row_slice, 128:256] = force[row_slice, 128:256] + second

        def row_parts(n):
            return ((slice(0, 32), slice(0, 32)), (slice(256, 264), slice(32, 40))) if n == 0 else ((slice(224, 264), slice(0, 40)),)

        for n in range(2):
            value = jnp.where(from_x[n], halo_x[step, n], 0.0)
            for to, of in row_parts(n):
                force[to] = force[to] + value[of]
            add_lanes(slice(0, EXT_X), jnp.where(from_y[n], halo_y[step, n], 0.0), n)
            for m in range(2):
                value = jnp.where(from_x[n] & from_y[m], halo_c[step, 2 * n + m], 0.0)
                for to, of in row_parts(n):
                    add_lanes(to, value[of], m)

    def ghost_copies():
        copies = []
        edges_x = {1: pl.ds(248, 8), -1: pl.ds(0, 8)}
        edges_y = {1: pl.ds(128, 128), -1: pl.ds(0, 128)}
        for n, d in enumerate((1, -1)):
            copies.append(remote(sw.at[:, edges_x[d], :], gh_x.at[n], sem_g, n, at(d, 0)))
            copies.append(remote(edge_y.at[n], gh_y.at[n], sem_g, 2 + n, at(0, d)))
            for m, e in enumerate((1, -1)):
                copies.append(remote(sw.at[:, edges_x[d], edges_y[e]], gh_c.at[2 * n + m], sem_g, 4 + 2 * n + m, at(d, e)))
        return copies

    def edges():
        sw[4] = wet[...].astype(f32)
        for q in range(5):
            edge_y[0, q] = sw[q, :, 128:256].T[120:128]
            edge_y[1, q] = sw[q, :, 0:128].T[0:8]

    def extend():
        thin = iota((8, 128), 1) < 64
        upper = iota((8, 256), 0) < 4
        upper_c = iota((8, 128), 0) < 4
        for q in range(5):
            ext[q, 0:256, 0:256] = sw[q]
            minus = jnp.where(from_y[0], gh_y[0, q], 0.0)
            plus = jnp.where(from_y[1], gh_y[1, q], 0.0)
            middle = jnp.zeros((112, 256), f32)
            ext[q, 0:256, 256:384] = jnp.concatenate([plus, middle, minus], 0).T
            minus = jnp.where(from_x[0], gh_x[0, q], 0.0)
            plus = jnp.where(from_x[1], gh_x[1, q], 0.0)
            ext[q, 256:264, 0:256] = jnp.where(upper, plus, minus)
            c = [[jnp.where(from_x[n] & from_y[m], gh_c[2 * n + m, q], 0.0) for m in range(2)] for n in range(2)]
            ext[q, 256:264, 256:384] = jnp.where(
                upper_c, jnp.where(thin, c[1][1], c[1][0]), jnp.where(thin, c[0][1], c[0][0])
            )

    def water(eta, us, vs, hold):
        deep, wetf = ext[3], ext[4]
        eta = eta + wetf * force[...]
        column = deep + eta

        def px(a):
            return pltpu.roll(a, EXT_X - 1, 0)

        def mx(a):
            return pltpu.roll(a, 1, 0)

        def py(a):
            return pltpu.roll(a, EXT_Y - 1, 1)

        def my(a):
            return pltpu.roll(a, 1, 1)

        ep, em, en, es = px(eta), mx(eta), py(eta), my(eta)
        up, um, un, us_ = px(us), mx(us), py(us), my(us)
        vp, vm, vn, vs_ = px(vs), mx(vs), py(vs), my(vs)
        qx, qy = column * us, column * vs
        e2 = 0.25 * (ep + em + en + es) - 0.125 * ((px(qx) - mx(qx)) + (py(qy) - my(qy)))
        u2 = 0.25 * (up + um + un + us_) - 0.125 * (us * (up - um) + vs * (un - us_) + (ep - em))
        v2 = 0.25 * (vp + vm + vn + vs_) - 0.125 * (us * (vp - vm) + vs * (vn - vs_) + (en - es))
        hold(0, e2 * wetf)
        hold(1, u2 * wetf)
        hold(2, v2 * wetf)

    def start(copies):
        for copy in copies:
            copy.start()

    def arrive(copies):
        for copy in copies:
            copy.wait()

    need("state")
    load_field(state)
    predict(1, ORDER)
    traces(range(VARS))
    hold_traces()
    pick(0)
    pl.semaphore_wait(barrier, len(peers))
    faces = face_copies(0)
    start(faces)
    prepare_surface()
    derive(0.0, 1 / 720, True)
    local_partner()
    need("weights")
    project(pay0)
    xc = first_copies(0, pay0, bx0)
    start(xc)
    keep_own(pay0, bx0)
    need("sea", "depth", "wet")
    edges()
    arrive(faces)
    settle(0, field)

    load_field(field)
    ghosts = ghost_copies()
    start(ghosts)
    predict(1, 3)
    arrive(xc)
    regroup(bx0, my0, mx0, by0, fx0)
    yc0 = second_copies(0, my0, mx0, by0, fx0)
    start(yc0)
    predict(3, ORDER)
    traces((2,))
    project(pay1)
    xc = first_copies(1, pay1, bx1)
    start(xc)
    keep_own(pay1, bx1)
    traces(others)
    hold_traces()
    pick(1)
    need("wx", "wy")
    arrive(yc0)
    choose(by0, fx0)
    contribute(0, by0, fx0)
    hc0 = halo_copies(0)
    start(hc0)
    derive(0.0, 1 / 720, True)
    arrive(xc)
    regroup(bx1, my1, mx1, by1, fx1)
    yc1 = second_copies(1, my1, mx1, by1, fx1)
    start(yc1)
    faces = face_copies(1)
    start(faces)
    arrive(ghosts)
    extend()
    arrive(hc0)
    gather_force(0)

    def keep(n, value):
        ext[n] = value

    water(ext[0], ext[1], ext[2], keep)
    arrive(yc1)
    contribute(1, by1, fx1)
    hc1 = halo_copies(1)
    start(hc1)
    local_partner()
    arrive(faces)
    settle(1, field)
    elastic_out = pltpu.make_async_copy(field, out_el, sem_out.at[0])
    elastic_out.start()
    arrive(hc1)
    gather_force(1)

    def emit(n, value):
        water_out[n] = value[0:256, 0:256]

    water(ext[0], ext[1], ext[2], emit)
    ocean_out = pltpu.make_async_copy(water_out, out_oc, sem_out.at[1])
    ocean_out.start()
    elastic_out.wait()
    ocean_out.wait()


def hand_over(a, b, out_a, out_b, hold_a, hold_b, sems):
    loads, stores = [], []
    for source, hold, target, count in ((a, hold_a, out_a, 3), (b, hold_b, out_b, 3)):
        size = source.shape[0] // count
        for n in range(count):
            some, number = pl.ds(size * n, size), len(loads)
            loads.append(pltpu.make_async_copy(source.at[some], hold.at[some], sems.at[0, number]))
            stores.append(pltpu.make_async_copy(hold.at[some], target.at[some], sems.at[1, number]))
    for copy in loads:
        copy.start()
    for load, store in zip(loads, stores):
        load.wait()
        store.start()
    for copy in stores:
        copy.wait()


def on_device(
    state, star, deriv, trace_ops, lift, face_flux, orient, neighbours, send_faces, sea_faces,
    sea_owner, sea_blocks, sea_weights, depth, wet, sea_state,
):
    wx, wy = filter_matrices()
    once, twice = turned_nodes()
    turns = np.stack([np.arange(NPAD), once, twice]).astype(np.int32)
    turns = np.broadcast_to(turns[:, :, None], (3, NPAD, 128)).copy()
    V = lambda shape, kind=f32: pltpu.VMEM(shape, kind)
    scratch = [
        V((9, 56, 256)), V((9, 9, 3, 256)), V((3, 56, 56)), V((21, 4, 56)), V((21, 4, 56)), V((9, 9, 4, 256)),
        V((4, 256), i32), V((4, 256), i32), V((4, 128), i32), V((1, 128), i32), V((1, 128), i32), V((1, 128), i32),
        V((21, 128, 256)), V((256, 256), i32), V((704, 256), bf16), V((256, 1280), bf16), V((3, NPAD, 128), i32),
        V((9, 56, 256)), V((3, 256, 256)), pltpu.SemaphoreType.DMA((19,)), pltpu.SemaphoreType.DMA((2,)),
        V((9, 27, 8, 256)), V((9, 36, 8, 256)), V((192, 256), bf16), V((96, 256), bf16), V((128, 256), bf16),
        V((256, 1152), bf16), V((256, 1152), bf16), V((256, 2304), bf16), V((192, 1152)), V((192, 1152)), V((9, 56, 256)), V((9, 56, 256)),
        V((224, 1024)), V((448, 1024), bf16), V((1024, 640), bf16), V((1024, 1024), bf16), V((512, 1024), bf16),
        V((224, 1024)), V((2, 4, 224, 128)), V((2, 4, 224, 128)), V((448, 512), bf16), V((9, 256, 256), bf16),
        V((128, 128)), V((256, 128), bf16), V((128, 128)), V((128, 384)),
        V((3, 256, 128)), V((2, 256, 128)), V((3, 256, 128)), V((2, 256, 128)),
        V((8, 3, 16, 128)), V((8, 2, 16, 128)), V((8, 3, 16, 128)), V((8, 2, 16, 128)),
        V((16, 3, 8, 128)), V((16, 2, 8, 128)), V((16, 3, 8, 128)), V((16, 2, 8, 128)),
        V((256, 256), bf16), V((256, 256)), V((2, 352, 640)),
        V((2, 2, 40, 384)), V((2, 2, 264, 128)), V((2, 4, 40, 128)), V((EXT_X, EXT_Y)),
        V((5, 256, 256)), V((2, 5, 8, 256)), V((2, 5, 8, 256)), V((4, 5, 8, 128)), V((5, EXT_X, EXT_Y)),
        V((4, 8, 256), i32), V((2, 5, 8, 256)), V((128, 128)),
        pltpu.SemaphoreType.DMA((2, 8)), pltpu.SemaphoreType.DMA((2, 60)), pltpu.SemaphoreType.DMA((2, 28)),
        pltpu.SemaphoreType.DMA((2, 16)), pltpu.SemaphoreType.DMA((2, 8)),
    ]
    place_any = pl.BlockSpec(memory_space=pl.ANY)
    shapes = (jax.ShapeDtypeStruct((9, 56, 256), f32), jax.ShapeDtypeStruct((3, 256, 256), f32))
    results = pl.pallas_call(
        kernel,
        out_shape=shapes,
        in_specs=[place_any] * 19,
        out_specs=(place_any,) * 2,
        scratch_shapes=scratch,
        compiler_params=pltpu.CompilerParams(
            collective_id=0, has_side_effects=True, vmem_limit_bytes=60 * 2**20
        ),
    )(
        state, star.transpose(1, 2, 0, 3), deriv, trace_ops.transpose(2, 0, 1), lift.transpose(1, 0, 2),
        face_flux.transpose(1, 2, 0, 3), orient,
        neighbours, send_faces.reshape(4, 128), sea_faces.reshape(1, 128), sea_owner.reshape(1, 128),
        sea_blocks.reshape(1, 128), sea_weights, depth, wet, sea_state,
        jnp.asarray(wx), jnp.asarray(wy), jnp.asarray(turns),
    )
    return pl.pallas_call(
        hand_over, out_shape=shapes, in_specs=[place_any] * 2, out_specs=(place_any,) * 2,
        scratch_shapes=[V((9, 56, 256)), V((3, 256, 256)), pltpu.SemaphoreType.DMA((2, 6))],
    )(*results)


def solution(mesh):
    flat = ("gx", "gy")
    placed = (
        P(None, None, flat), P(None, None, None, flat), P(), P(), P(), P(None, None, None, flat), P(None, flat),
        P(None, flat), P("gx", "gy", None, None), P(flat), P(flat, None), P(flat), P(None, flat, None),
        P("gx", "gy"), P("gx", "gy"), P(None, "gx", "gy"),
    )
    return jax.shard_map(
        on_device, mesh=mesh, in_specs=placed,
        out_specs=(P(None, None, flat), P(None, "gx", "gy")), check_vma=False,
    )
```

```python
import functools
import math

import jax
import jax.numpy as jnp
import numpy as np
from jax import lax
from jax.experimental import pallas as pl
from jax.experimental.pallas import tpu as pltpu
from jax.sharding import PartitionSpec as P

VARS = 9
ORDER = 6
BASIS = 56
NODES = 21
NX, NY = 16, 8
HALF = 32
NPAD = 24
EXT_X, EXT_Y = 264, 384
bf16, f32, i32 = jnp.bfloat16, jnp.float32, jnp.int32
MESH = pl.DeviceIdType.MESH


def turned_nodes():
    upper = ORDER - 1
    nodes = [(i, j) for i in range(upper + 1) for j in range(upper + 1 - i)]
    once = [nodes.index((p[1], upper - p[0] - p[1])) for p in nodes]
    twice = [once[once[n]] for n in range(len(nodes))]
    rest = list(range(NODES, NPAD))
    return np.array(once + rest), np.array(twice + rest)


def filter_matrices():
    k = np.arange(-HALF, HALF + 1)
    raw = 1.0 / np.cosh(math.pi * k / 16.0)
    taps = raw / raw.sum()

    def tap(offset):
        inside = np.abs(offset) <= HALF
        return np.where(inside, taps[np.clip(offset + HALF, 0, 2 * HALF)], 0.0)

    far = 10**6
    cell_x = np.array([r if r < 258 else (r - EXT_X if r >= 262 else far) for r in range(EXT_X)])
    cell_y = np.array([c if c < 258 else (c - EXT_Y if c >= 382 else far) for c in range(EXT_Y)])
    rows_up = np.concatenate([np.arange(0, 32), np.arange(256, 264)])
    rows_down = np.arange(224, 264)
    xs = np.concatenate([cell_x, cell_x[rows_up] + 256, cell_x[rows_down] - 256, np.full(8, far)])
    lane = np.arange(128)
    up = np.where(lane < 64, lane, 256 + lane)
    down = np.where(lane < 64, 256 + lane, 128 + lane)
    ys = np.concatenate([cell_y, cell_y[up] + 256, cell_y[down] - 256])
    column = np.arange(256)
    x_of = (column % 16) * 16 + column // 16
    wx = tap(xs[:, None] - x_of[None, :]).astype(np.float32)
    wy = tap(ys[None, :] - np.arange(256)[:, None]).astype(np.float32)

    def parts(w):
        high = w.astype(jnp.bfloat16)
        low = (w - high.astype(np.float32)).astype(jnp.bfloat16)
        return high, low

    xh, xl = parts(wx)
    yh, yl = parts(wy)
    return np.concatenate([xh, xl], 0), np.concatenate([yh, yl], 1)


def split(x):
    high = x.astype(bf16)
    low = (x - high.astype(f32)).astype(bf16)
    return high, low


def dot(a, b):
    return jnp.dot(a, b, preferred_element_type=f32)


def iota(shape, dim):
    return lax.broadcasted_iota(i32, shape, dim)


def kernel(
    state_h, star_h, deriv_h, trace_h, lift_h, flux_h, orient_h, codes_h, sends_h, seaf_h, owner_h, blocks_h, weights_h,
    depth_h, wet_h, sea_h, wx_h, wy_h, turns_h,
    out_el, out_oc,
    state, star, deriv, trace, lift, flux9, orient, codes, sends, seaf, owner, blocks, weights,
    wet, wx, wy, turns, field, water_out, sem_in, sem_out,
    star8, flux8, a_op, t_op, l_op, stack_a, stack_b, istack, moved_a, moved_b, integ, base, own, xs, g_out, p_loc, p_arr,
    part, sbuf, arr, xa, fstack, zed, place, disp_t, rows, pay0, pay1, bx0, bx1, my0, my1, by0, by1, mx0, mx1, fx0, fx1,
    sel, upl, cont, halo_x, halo_y, halo_c, force, sw, gh_x, gh_y, gh_c, ext,
    inner, orient8, edge_y, zed_l, sem_f, sem_x, sem_y, sem_h, sem_g,
):
    gx, gy = lax.axis_index("gx"), lax.axis_index("gy")

    def at(dx, dy):
        return (lax.rem(gx + dx + NX, NX), lax.rem(gy + dy + NY, NY))

    peers = [at(k, 0) for k in range(1, NX)] + [at(0, k) for k in range(1, NY)]
    peers += [at(dx, dy) for dx in (-1, 1) for dy in (-1, 1)]
    incoming = {}
    order = (
        ("star", star_h, star), ("deriv", deriv_h, deriv), ("state", state_h, state), ("trace", trace_h, trace),
        ("sends", sends_h, sends), ("seaf", seaf_h, seaf), ("owner", owner_h, owner), ("blocks", blocks_h, blocks),
        ("weights", weights_h, weights), ("codes", codes_h, codes), ("lift", lift_h, lift), ("flux", flux_h, flux9),
        ("orient", orient_h, orient), ("turns", turns_h, turns), ("sea", sea_h, sw.at[0:3]),
        ("depth", depth_h, sw.at[3]), ("wet", wet_h, wet), ("wx", wx_h, wx), ("wy", wy_h, wy),
    )
    for number, (name, source, target) in enumerate(order):
        incoming[name] = pltpu.make_async_copy(source, target, sem_in.at[number])
        incoming[name].start()

    def need(*names):
        for name in names:
            incoming[name].wait()

    barrier = pltpu.get_barrier_semaphore()
    for peer in peers:
        pl.semaphore_signal(barrier, inc=1, device_id=peer, device_id_type=MESH)

    def remote(src, dst, sems, number, peer):
        return pltpu.make_async_remote_copy(
            src_ref=src, dst_ref=dst, send_sem=sems.at[0, number], recv_sem=sems.at[1, number],
            device_id=peer, device_id_type=MESH,
        )

    def spread(source, target, count, sign):
        def body(u, carry):
            block = source[u]
            for v in range(VARS):
                for k in range(count):
                    target[u, v * count + k] = jnp.broadcast_to(sign * block[v, k : k + 1, :], (8, 256))
            return carry
        lax.fori_loop(0, VARS, body, 0)

    def packed(x):
        high, low = split(x)
        high, low = high.astype(f32), low.astype(f32)
        both = jnp.where(iota(x.shape, 1) < 64, high, pltpu.roll(low, 64, 1))
        return jnp.concatenate([both, both], 1).astype(bf16)

    need("star", "deriv")
    spread(star, star8, 3, -1.0)
    pieces = []
    zed[...] = jnp.zeros((128, 128), f32)
    for d in range(3):
        zed[0:BASIS, 0:BASIS] = deriv[d]
        pieces.append(zed[...].T[0:64])
    a_op[...] = packed(jnp.concatenate(pieces, 0))
    need("trace")
    zed[...] = jnp.zeros((128, 128), f32)
    for n in range(NODES):
        for f in range(4):
            zed[NPAD * f + n : NPAD * f + n + 1, 0:BASIS] = trace[n, f : f + 1, :]
    t_op[...] = packed(zed[0:96])
    def hot(target, count, first, lanes, row):
        def body(i, carry):
            here = iota((64, row.shape[1]), 0) + (64 * i + first)
            target[pl.ds(pl.multiple_of(64 * i, 64), 64), lanes] = jnp.where(here == row, 1.0, 0.0).astype(bf16)
            return carry
        lax.fori_loop(0, count // 64, body, 0)

    need("sends", "seaf")
    for k in range(4):
        hot(g_out, 1024, 0, pl.ds(128 * k, 128), sends[k : k + 1, :])
    hot(g_out, 1024, 0, pl.ds(512, 128), seaf[...])
    zed[...] = jnp.zeros((128, 128), f32)
    own[216:224] = jnp.zeros((8, 1024), f32)

    def prepare_surface():
        need("lift")
        zed_l[...] = jnp.zeros((128, 128), f32)
        for n in range(NODES):
            for f in range(4):
                zed_l[32 * f + n : 32 * f + n + 1, 0:BASIS] = lift[n, f : f + 1, :]
        high, low = split(zed_l[...].T[0:64])
        l_op[0:64] = jnp.concatenate([high, high], 1)
        l_op[64:128] = jnp.concatenate([low, low], 1)
        need("flux", "orient", "owner", "blocks", "codes", "turns")
        spread(flux9, flux8, 4, 1.0)
        for f in range(4):
            orient8[f] = jnp.broadcast_to(orient[f : f + 1, :], (8, 256))

        for f in range(4):
            hot(p_loc, 1024, 0, pl.ds(256 * f, 256), codes[f : f + 1, :])
            hot(p_arr, 512, 1024, pl.ds(256 * f, 256), codes[f : f + 1, :])

        who = owner[...]
        who_t = jnp.broadcast_to(who, (128, 128)).T
        earlier = iota((128, 128), 0) < iota((128, 128), 1)
        rank = jnp.sum(jnp.where((who_t == who) & earlier, 1.0, 0.0), axis=0, keepdims=True).astype(i32)
        spot = jnp.where(rank > 0, 128 + lax.rem(who, 8) * 16 + who // 8, who)
        place[...] = jnp.where(iota((256, 128), 0) == spot, 1.0, 0.0).astype(bf16)
        rows[:, 256:384] = jnp.broadcast_to((blocks[...] + 1).astype(f32), (128, 128)).T


    halves = ((stack_a, moved_a), (stack_b, moved_b))
    blank = jnp.zeros((8, 128), f32)

    def hold_split(target, lanes, value):
        high, low = split(jnp.concatenate([value, blank], 0))
        target[0:64, lanes] = high
        target[64:128, lanes] = high
        target[128:192, lanes] = low
        target[192:256, lanes] = low

    def load_field(source):
        for v in range(VARS):
            value = source[v]
            integ[v] = value
            base[v] = value
            for side in range(2):
                hold_split(halves[side][0], pl.ds(128 * v, 128), value[:, 128 * side : 128 * side + 128])
        moved_a[...] = dot(a_op[...], stack_a[...])

    def phase(side, c_integ, c_base, last, feed):
        held, moved = halves[side]
        other_held, other_moved = halves[1 - side]
        lanes = pl.ds(128 * side, 128)

        def body(block, carry):
            if feed:
                third = pl.ds(pl.multiple_of(384 * block, 128), 384)
                other_moved[:, third] = dot(a_op[...], other_held[:, third])
            acc = None
            for v in range(VARS):
                for d in range(3):
                    m = [moved[64 * d + 8 * g : 64 * d + 8 * g + 8, 128 * v : 128 * v + 128] for g in range(7)]
                    new = []
                    for k in range(3):
                        w = star8[3 * block + k, v * 3 + d, :, lanes]
                        new += [w * x for x in m]
                    acc = new if acc is None else [p + q for p, q in zip(acc, new)]
            for k in range(3):
                u = 3 * block + k
                value = jnp.concatenate(acc[7 * k : 7 * k + 7], 0)
                base[u, :, lanes] = base[u, :, lanes] + c_base * value
                if not last:
                    integ[u, :, lanes] = integ[u, :, lanes] + c_integ * value
                    hold_split(held, pl.ds(pl.multiple_of(128 * u, 128), 128), value)
            return carry

        lax.fori_loop(0, 3, body, 0)

    def derive(c_integ, c_base, last):
        phase(0, c_integ, c_base, last, True)
        phase(1, c_integ, c_base, last, not last)

    def predict(least, most):
        def body(k, carry):
            c_base = jnp.where(k == 1, 1.0, jnp.where(k == 2, 1 / 2, jnp.where(k == 3, 1 / 6, jnp.where(k == 4, 1 / 24, 1 / 120)))).astype(f32)
            c_integ = jnp.where(k == 1, 1 / 2, jnp.where(k == 2, 1 / 6, jnp.where(k == 3, 1 / 24, jnp.where(k == 4, 1 / 120, 1 / 720)))).astype(f32)
            derive(c_integ, c_base, False)
            return carry
        lax.fori_loop(least, most, body, 0)

    def traces(variables):
        for v in variables:
            for side in range(2):
                hold_split(istack, pl.ds(256 * v + 128 * side, 128), integ[v, :, 128 * side : 128 * side + 128])
            faces = dot(t_op[...], istack[:, 256 * v : 256 * v + 256])
            for f in range(4):
                own[NPAD * v : NPAD * v + NPAD, 256 * f : 256 * f + 256] = faces[NPAD * f : NPAD * f + NPAD]

    def hold_traces():
        high, low = split(own[...])
        xs[0:224] = high
        xs[224:448] = low

    others = tuple(v for v in range(VARS) if v != 2)

    def pick(step):
        got = dot(xs[...], g_out[:, 0:512])
        got = got[0:224] + got[224:448]
        for k in range(4):
            sbuf[step, k] = got[:, 128 * k : 128 * k + 128]

    def project(target):
        upward = jnp.concatenate([own[2 * NPAD : 3 * NPAD], jnp.zeros((8, 1024), f32)], 0)
        high, low = split(upward)
        got = dot(jnp.concatenate([high, low], 0), g_out[:, 512:640])
        zed[0:NPAD] = got[0:NPAD] + got[32 : 32 + NPAD]
        disp_t[...] = zed[...].T

        for i in range(4):
            at_rows = pl.ds(32 * i, 32)
            values = disp_t[at_rows]
            acc = values[:, 0:1] * weights[0, at_rows, :]
            for n in range(1, NODES):
                acc = acc + values[:, n : n + 1] * weights[n, at_rows, :]
            rows[at_rows, 0:256] = acc
        count = target.shape[0]
        high, low = split(rows[:, 0 : 128 * count])
        placed = dot(place[...], high) + dot(place[...], low)
        for q in range(count):
            target[q] = placed[:, 128 * q : 128 * q + 128]

    directions = ((-1, 0), (1, 0), (0, -1), (0, 1))

    def face_copies(step):
        return [
            remote(sbuf.at[step, k], arr.at[step, k ^ 1], sem_f, 4 * step + k, at(*directions[k]))
            for k in range(4)
        ]

    def part_x(k):
        return pl.ds(pl.multiple_of(8 * k, 8), 8)

    def part_y(k):
        return pl.ds(pl.multiple_of(128 + 16 * k, 16), 16)

    def first_copies(step, payload, landing):
        copies = []
        for k in range(1, NX):
            to = lax.rem(gx + k, NX)
            copies.append(remote(payload.at[:, part_x(to), :], landing.at[:, part_x(gx), :], sem_x, 30 * step + k - 1, (to, gy)))
        for k in range(1, NY):
            to = lax.rem(gy + k, NY)
            copies.append(remote(payload.at[:, part_y(to), :], landing.at[:, part_y(gy), :], sem_y, 14 * step + k - 1, (gx, to)))
        return copies

    def second_copies(step, along_y, along_x, final_y, final_x):
        copies = []
        for k in range(1, NX):
            to = lax.rem(gx + k, NX)
            copies.append(remote(along_x.at[to], final_x.at[gx], sem_x, 30 * step + 15 + k - 1, (to, gy)))
        for k in range(1, NY):
            to = lax.rem(gy + k, NY)
            copies.append(remote(along_y.at[to], final_y.at[gy], sem_y, 14 * step + 7 + k - 1, (gx, to)))
        return copies

    def keep_own(payload, landing):
        for q in range(payload.shape[0]):
            landing[q, part_x(gx)] = payload[q, part_x(gx)]
            landing[q, part_y(gy)] = payload[q, part_y(gy)]

    def regroup(landing, along_y, along_x, final_y, final_x):
        for q in range(landing.shape[0]):
            for j in range(NY):
                along_y[j, q] = landing[q, pl.ds(j, 16, stride=8)]
            for i in range(NX):
                along_x[i, q] = landing[q, pl.ds(128 + i, 8, stride=16)]
        final_y[gy] = along_y[gy]
        final_x[gx] = along_x[gx]

    def local_partner():
        got = dot(xs[...], p_loc[...])
        part[...] = got[0:224] + got[224:448]

    def settle(step, target):
        for k in range(4):
            high, low = split(arr[step, k])
            xa[0:224, 128 * k : 128 * k + 128] = high
            xa[224:448, 128 * k : 128 * k + 128] = low
        got = dot(xa[...], p_arr[...])
        part[...] = part[...] + got[0:224] + got[224:448]

        def body(f, carry):
            for side in range(2):
                lanes = pl.ds(128 * side, 128)
                wide = pl.ds(pl.multiple_of(256 * f + 128 * side, 128), 128)
                turn = orient8[f, :, lanes]
                picks = [
                    jnp.where(turn == 0, turns[0, 8 * g : 8 * g + 8], jnp.where(turn == 1, turns[1, 8 * g : 8 * g + 8], turns[2, 8 * g : 8 * g + 8]))
                    for g in range(3)
                ]
                inner = [lax.rem(p, 8) for p in picks]
                jump = []
                for v in range(VARS):
                    source = [part[NPAD * v + 8 * g : NPAD * v + 8 * g + 8, wide] for g in range(3)]
                    jump.append([])
                    for g in range(3):
                        t = [jnp.take_along_axis(s, inner[g], axis=0, mode="promise_in_bounds") for s in source]
                        turned = jnp.where(picks[g] < 8, t[0], jnp.where(picks[g] < 16, t[1], t[2]))
                        jump[v].append(own[NPAD * v + 8 * g : NPAD * v + 8 * g + 8, wide] - turned)
                for u in range(VARS):
                    acc = None
                    for v in range(VARS):
                        w = flux8[u, v * 4 + f, :, lanes]
                        new = [w * jump[v][g] for g in range(3)]
                        acc = new if acc is None else [a + b for a, b in zip(acc, new)]
                    high, low = split(jnp.concatenate(acc + [jnp.zeros((8, 128), f32)], 0))
                    fstack[u, pl.ds(pl.multiple_of(32 * f, 32), 32), lanes] = high
                    fstack[u, pl.ds(pl.multiple_of(128 + 32 * f, 32), 32), lanes] = low
            return carry

        lax.fori_loop(0, 4, body, 0)
        for u in range(VARS):
            s = dot(l_op[...], fstack[u])
            target[u] = base[u] - (s[0:64] + s[64:128])[0:BASIS]

    def landed(final_y, final_x, q):
        return jnp.concatenate([final_y[:, q].reshape(128, 128), final_x[:, q].reshape(128, 128)], 0)

    def choose(final_y, final_x):
        labels = landed(final_y, final_x, 2).T[0:1]
        r = iota((256, 256), 0)
        block = lax.rem(r, 16) * 16 + r // 16
        sel[...] = jnp.where(block.astype(f32) + 1.0 == labels, 1.0, 0.0).astype(bf16)

    lane_group = iota((16, 128), 1) // 16

    def contribute(step, final_y, final_x):
        got = jnp.concatenate([landed(final_y, final_x, q) for q in range(2)], 1)
        high, low = split(got)
        summed = dot(sel[...], high) + dot(sel[...], low)
        for h in range(2):
            half = summed[:, 128 * h : 128 * h + 128]
            turned = [half if s == 0 else pltpu.roll(half, 16 * s, 1) for s in range(8)]
            for j in range(8):
                cx = 8 * h + j
                for hb in range(2):
                    acc = None
                    for b in range(8):
                        block = 8 * hb + b
                        piece = turned[(b - j) % 8][16 * block : 16 * block + 16]
                        acc = piece if acc is None else jnp.where(lane_group == b, piece, acc)
                    upl[16 * cx : 16 * cx + 16, 128 * hb : 128 * hb + 128] = acc
        high, low = split(upl[...])
        first = dot(wx[...], high)
        first = first[0:352] + first[352:704] + dot(wx[0:352], low)
        inner[...] = first[0:272]

        def along_y(value, least, most):
            high, low = split(value)
            near = wy[:, least:most]
            return dot(high, near) + dot(low, near) + dot(high, wy[:, 640 + least : 640 + most])

        cont[step, 0:264, 384:640] = along_y(first[0:272], 384, 640)[0:264]
        cont[step, 264:352] = along_y(first[256:352], 0, 640)[8:96]

    def contribute_here(step):
        high, low = split(inner[...])
        near = wy[:, 0:384]
        cont[step, 0:264, 0:384] = (dot(high, near) + dot(low, near) + dot(high, wy[:, 640:1024]))[0:264]

    def halo_copies(step):
        copies = []
        x_part = {1: pl.ds(264, 40), -1: pl.ds(304, 40)}
        y_part = {1: pl.ds(384, 128), -1: pl.ds(512, 128)}
        for n, d in enumerate((1, -1)):
            copies.append(remote(cont.at[step, x_part[d], pl.ds(0, 384)], halo_x.at[step, n], sem_h, 8 * step + n, at(d, 0)))
            copies.append(remote(cont.at[step, pl.ds(0, 264), y_part[d]], halo_y.at[step, n], sem_h, 8 * step + 2 + n, at(0, d)))
            for m, e in enumerate((1, -1)):
                copies.append(remote(cont.at[step, x_part[d], y_part[e]], halo_c.at[step, 2 * n + m], sem_h, 8 * step + 4 + 2 * n + m, at(d, e)))
        return copies

    from_x = (gx > 0, gx < NX - 1)
    from_y = (gy > 0, gy < NY - 1)

    def gather_force(step):
        force[...] = cont[step, 0:EXT_X, 0:EXT_Y]

        def add_lanes(row_slice, value, m):
            low = iota(value.shape, 1) < 64
            first, second = jnp.where(low, value, 0.0), jnp.where(low, 0.0, value)
            if m == 0:
                force[row_slice, 0:128] = force[row_slice, 0:128] + first
                force[row_slice, 256:384] = force[row_slice, 256:384] + second
            else:
                force[row_slice, 256:384] = force[row_slice, 256:384] + first
                force[row_slice, 128:256] = force[row_slice, 128:256] + second

        def row_parts(n):
            return ((slice(0, 32), slice(0, 32)), (slice(256, 264), slice(32, 40))) if n == 0 else ((slice(224, 264), slice(0, 40)),)

        for n in range(2):
            value = jnp.where(from_x[n], halo_x[step, n], 0.0)
            for to, of in row_parts(n):
                force[to] = force[to] + value[of]
            add_lanes(slice(0, EXT_X), jnp.where(from_y[n], halo_y[step, n], 0.0), n)
            for m in range(2):
                value = jnp.where(from_x[n] & from_y[m], halo_c[step, 2 * n + m], 0.0)
                for to, of in row_parts(n):
                    add_lanes(to, value[of], m)

    def ghost_copies():
        copies = []
        edges_x = {1: pl.ds(248, 8), -1: pl.ds(0, 8)}
        edges_y = {1: pl.ds(128, 128), -1: pl.ds(0, 128)}
        for n, d in enumerate((1, -1)):
            copies.append(remote(sw.at[:, edges_x[d], :], gh_x.at[n], sem_g, n, at(d, 0)))
            copies.append(remote(edge_y.at[n], gh_y.at[n], sem_g, 2 + n, at(0, d)))
            for m, e in enumerate((1, -1)):
                copies.append(remote(sw.at[:, edges_x[d], edges_y[e]], gh_c.at[2 * n + m], sem_g, 4 + 2 * n + m, at(d, e)))
        return copies

    def edges():
        sw[4] = wet[...].astype(f32)
        for q in range(5):
            edge_y[0, q] = sw[q, :, 128:256].T[120:128]
            edge_y[1, q] = sw[q, :, 0:128].T[0:8]

    def extend():
        thin = iota((8, 128), 1) < 64
        upper = iota((8, 256), 0) < 4
        upper_c = iota((8, 128), 0) < 4
        for q in range(5):
            ext[q, 0:256, 0:256] = sw[q]
            minus = jnp.where(from_y[0], gh_y[0, q], 0.0)
            plus = jnp.where(from_y[1], gh_y[1, q], 0.0)
            middle = jnp.zeros((112, 256), f32)
            ext[q, 0:256, 256:384] = jnp.concatenate([plus, middle, minus], 0).T
            minus = jnp.where(from_x[0], gh_x[0, q], 0.0)
            plus = jnp.where(from_x[1], gh_x[1, q], 0.0)
            ext[q, 256:264, 0:256] = jnp.where(upper, plus, minus)
            c = [[jnp.where(from_x[n] & from_y[m], gh_c[2 * n + m, q], 0.0) for m in range(2)] for n in range(2)]
            ext[q, 256:264, 256:384] = jnp.where(
                upper_c, jnp.where(thin, c[1][1], c[1][0]), jnp.where(thin, c[0][1], c[0][0])
            )

    def water(eta, us, vs, hold):
        deep, wetf = ext[3], ext[4]
        eta = eta + wetf * force[...]
        column = deep + eta

        def px(a):
            return pltpu.roll(a, EXT_X - 1, 0)

        def mx(a):
            return pltpu.roll(a, 1, 0)

        def py(a):
            return pltpu.roll(a, EXT_Y - 1, 1)

        def my(a):
            return pltpu.roll(a, 1, 1)

        ep, em, en, es = px(eta), mx(eta), py(eta), my(eta)
        up, um, un, us_ = px(us), mx(us), py(us), my(us)
        vp, vm, vn, vs_ = px(vs), mx(vs), py(vs), my(vs)
        qx, qy = column * us, column * vs
        e2 = 0.25 * (ep + em + en + es) - 0.125 * ((px(qx) - mx(qx)) + (py(qy) - my(qy)))
        u2 = 0.25 * (up + um + un + us_) - 0.125 * (us * (up - um) + vs * (un - us_) + (ep - em))
        v2 = 0.25 * (vp + vm + vn + vs_) - 0.125 * (us * (vp - vm) + vs * (vn - vs_) + (en - es))
        hold(0, e2 * wetf)
        hold(1, u2 * wetf)
        hold(2, v2 * wetf)

    def start(copies):
        for copy in copies:
            copy.start()

    def arrive(copies):
        for copy in copies:
            copy.wait()

    need("state")
    load_field(state)
    predict(1, ORDER)
    traces(range(VARS))
    hold_traces()
    pick(0)
    pl.semaphore_wait(barrier, len(peers))
    faces = face_copies(0)
    start(faces)
    prepare_surface()
    derive(0.0, 1 / 720, True)
    local_partner()
    need("weights")
    project(pay0)
    xc = first_copies(0, pay0, bx0)
    start(xc)
    keep_own(pay0, bx0)
    need("sea", "depth", "wet")
    edges()
    arrive(faces)
    settle(0, field)

    load_field(field)
    ghosts = ghost_copies()
    start(ghosts)
    predict(1, 3)
    arrive(xc)
    regroup(bx0, my0, mx0, by0, fx0)
    yc0 = second_copies(0, my0, mx0, by0, fx0)
    start(yc0)
    predict(3, ORDER)
    traces((2,))
    project(pay1)
    xc = first_copies(1, pay1, bx1)
    start(xc)
    keep_own(pay1, bx1)
    traces(others)
    hold_traces()
    pick(1)
    need("wx", "wy")
    arrive(yc0)
    choose(by0, fx0)
    contribute(0, by0, fx0)
    hc0 = halo_copies(0)
    start(hc0)
    contribute_here(0)
    derive(0.0, 1 / 720, True)
    arrive(xc)
    regroup(bx1, my1, mx1, by1, fx1)
    yc1 = second_copies(1, my1, mx1, by1, fx1)
    start(yc1)
    faces = face_copies(1)
    start(faces)
    arrive(ghosts)
    extend()
    arrive(hc0)
    gather_force(0)

    def keep(n, value):
        ext[n] = value

    water(ext[0], ext[1], ext[2], keep)
    arrive(yc1)
    contribute(1, by1, fx1)
    hc1 = halo_copies(1)
    start(hc1)
    contribute_here(1)
    local_partner()
    arrive(faces)
    settle(1, field)
    elastic_out = pltpu.make_async_copy(field, out_el, sem_out.at[0])
    elastic_out.start()
    arrive(hc1)
    gather_force(1)

    def emit(n, value):
        water_out[n] = value[0:256, 0:256]

    water(ext[0], ext[1], ext[2], emit)
    ocean_out = pltpu.make_async_copy(water_out, out_oc, sem_out.at[1])
    ocean_out.start()
    elastic_out.wait()
    ocean_out.wait()


def hand_over(a, b, out_a, out_b, hold_a, hold_b, sems):
    loads, stores = [], []
    for source, hold, target, count in ((a, hold_a, out_a, 3), (b, hold_b, out_b, 3)):
        size = source.shape[0] // count
        for n in range(count):
            some, number = pl.ds(size * n, size), len(loads)
            loads.append(pltpu.make_async_copy(source.at[some], hold.at[some], sems.at[0, number]))
            stores.append(pltpu.make_async_copy(hold.at[some], target.at[some], sems.at[1, number]))
    for copy in loads:
        copy.start()
    for load, store in zip(loads, stores):
        load.wait()
        store.start()
    for copy in stores:
        copy.wait()


def on_device(
    state, star, deriv, trace_ops, lift, face_flux, orient, neighbours, send_faces, sea_faces,
    sea_owner, sea_blocks, sea_weights, depth, wet, sea_state,
):
    wx, wy = filter_matrices()
    once, twice = turned_nodes()
    turns = np.stack([np.arange(NPAD), once, twice]).astype(np.int32)
    turns = np.broadcast_to(turns[:, :, None], (3, NPAD, 128)).copy()
    V = lambda shape, kind=f32: pltpu.VMEM(shape, kind)
    scratch = [
        V((9, 56, 256)), V((9, 9, 3, 256)), V((3, 56, 56)), V((21, 4, 56)), V((21, 4, 56)), V((9, 9, 4, 256)),
        V((4, 256), i32), V((4, 256), i32), V((4, 128), i32), V((1, 128), i32), V((1, 128), i32), V((1, 128), i32),
        V((21, 128, 256)), V((256, 256), i32), V((704, 256), bf16), V((256, 1280), bf16), V((3, NPAD, 128), i32),
        V((9, 56, 256)), V((3, 256, 256)), pltpu.SemaphoreType.DMA((19,)), pltpu.SemaphoreType.DMA((2,)),
        V((9, 27, 8, 256)), V((9, 36, 8, 256)), V((192, 256), bf16), V((96, 256), bf16), V((128, 256), bf16),
        V((256, 1152), bf16), V((256, 1152), bf16), V((256, 2304), bf16), V((192, 1152)), V((192, 1152)), V((9, 56, 256)), V((9, 56, 256)),
        V((224, 1024)), V((448, 1024), bf16), V((1024, 640), bf16), V((1024, 1024), bf16), V((512, 1024), bf16),
        V((224, 1024)), V((2, 4, 224, 128)), V((2, 4, 224, 128)), V((448, 512), bf16), V((9, 256, 256), bf16),
        V((128, 128)), V((256, 128), bf16), V((128, 128)), V((128, 384)),
        V((3, 256, 128)), V((2, 256, 128)), V((3, 256, 128)), V((2, 256, 128)),
        V((8, 3, 16, 128)), V((8, 2, 16, 128)), V((8, 3, 16, 128)), V((8, 2, 16, 128)),
        V((16, 3, 8, 128)), V((16, 2, 8, 128)), V((16, 3, 8, 128)), V((16, 2, 8, 128)),
        V((256, 256), bf16), V((256, 256)), V((2, 352, 640)),
        V((2, 2, 40, 384)), V((2, 2, 264, 128)), V((2, 4, 40, 128)), V((EXT_X, EXT_Y)),
        V((5, 256, 256)), V((2, 5, 8, 256)), V((2, 5, 8, 256)), V((4, 5, 8, 128)), V((5, EXT_X, EXT_Y)),
        V((272, 256)), V((4, 8, 256), i32), V((2, 5, 8, 256)), V((128, 128)),
        pltpu.SemaphoreType.DMA((2, 8)), pltpu.SemaphoreType.DMA((2, 60)), pltpu.SemaphoreType.DMA((2, 28)),
        pltpu.SemaphoreType.DMA((2, 16)), pltpu.SemaphoreType.DMA((2, 8)),
    ]
    place_any = pl.BlockSpec(memory_space=pl.ANY)
    shapes = (jax.ShapeDtypeStruct((9, 56, 256), f32), jax.ShapeDtypeStruct((3, 256, 256), f32))
    results = pl.pallas_call(
        kernel,
        out_shape=shapes,
        in_specs=[place_any] * 19,
        out_specs=(place_any,) * 2,
        scratch_shapes=scratch,
        compiler_params=pltpu.CompilerParams(
            collective_id=0, has_side_effects=True, vmem_limit_bytes=60 * 2**20
        ),
    )(
        state, star.transpose(1, 2, 0, 3), deriv, trace_ops.transpose(2, 0, 1), lift.transpose(1, 0, 2),
        face_flux.transpose(1, 2, 0, 3), orient,
        neighbours, send_faces.reshape(4, 128), sea_faces.reshape(1, 128), sea_owner.reshape(1, 128),
        sea_blocks.reshape(1, 128), sea_weights, depth, wet, sea_state,
        jnp.asarray(wx), jnp.asarray(wy), jnp.asarray(turns),
    )
    return pl.pallas_call(
        hand_over, out_shape=shapes, in_specs=[place_any] * 2, out_specs=(place_any,) * 2,
        scratch_shapes=[V((9, 56, 256)), V((3, 256, 256)), pltpu.SemaphoreType.DMA((2, 6))],
    )(*results)


def solution(mesh):
    flat = ("gx", "gy")
    placed = (
        P(None, None, flat), P(None, None, None, flat), P(), P(), P(), P(None, None, None, flat), P(None, flat),
        P(None, flat), P("gx", "gy", None, None), P(flat), P(flat, None), P(flat), P(None, flat, None),
        P("gx", "gy"), P("gx", "gy"), P(None, "gx", "gy"),
    )
    return jax.shard_map(
        on_device, mesh=mesh, in_specs=placed,
        out_specs=(P(None, None, flat), P(None, "gx", "gy")), check_vma=False,
    )
```
